512 devices in a mesh: phase: 2 (over y_lo), lat: 8 (over x, core), lon: 32 (over y_hi, z).
Axes of the slice: x: 4, y: 8 (y_hi: 4, y_lo: 2; y = y_hi * 2 + y_lo), z: 8, core: 2. Of those that a mesh axis runs over, the one named last changes fastest.
Arguments:
- x_in: bfloat16 [2, 2, 48, 384, 512], P('phase', None, 'lat', 'lon'), may hold values from -430 to 430
- out_grad: bfloat16 [2, 2, 48, 384, 512], P('phase', None, 'lat', 'lon'), may hold values from -6 to 6
- w_qkv: bfloat16 [2, 1536, 512], P('phase'), may hold values from -0.25 to 0.25
- w_proj: bfloat16 [2, 512, 512], P('phase'), may hold values from -0.25 to 0.25
- norm_gain: float32 [2, 512], P('phase'), may hold values from 0.25 to 1.75
- bias_table: float32 [2, 8, 759], P('phase'), may hold values from -80 to 165
- lat_labels: int32 [48], P('lat'), may hold values from 0 to 11, never falling along the last dimension, each value on 1 to 8 neighbouring positions
Outputs:
- grad_input: bfloat16 [2, 2, 48, 384, 512], P('phase', None, 'lat', 'lon')
- grad_qkv: float32 [2, 1536, 512], P('phase', 'lat', 'lon')
The draws below stay inside these ranges and needn't reach their ends.
Inputs may be any that keep to these rules, and one draw needn't show every extreme that they name: `lat_labels`: labels never fall from one latitude row to the next; each label holds 1 to 8 consecutive rows, and one holds 8.
All inputs are finite; a program needn't handle non-finite values.
Results may differ from the reference program's by a relative error of at most 0.028.
Values may be sent and summed in bfloat16 or wider, within the bound.
No kernel may reach another device: no remote copies, remote signals or barrier semaphores. Data moves between devices by JAX's collectives and lax.ppermute only.
A program may use at most 64 MiB of HBM per device.

```python
import math
import jax
import jax.numpy as jnp
import numpy as np
from jax import lax

D = 512
HEADS = 8
LEVELS = 2
WIN_LEV = 2
WIN_LAT = 6
WIN_LON = 12
NLAT = 48
NLON = 384
REL = 759


def draw_x_in(key, part):
    key = jax.random.fold_in(key, 11)
    subkeys = jax.random.split(key, 1)
    full_shape = (2, LEVELS, NLAT, NLON, D)
    base = jnp.clip(jax.random.normal(subkeys[0], full_shape, jnp.float32), -4.0, 4.0)
    return base.astype(jnp.bfloat16)


def draw_bias_table(key, part):
    key = jax.random.fold_in(key, 23)
    subkeys = jax.random.split(key, 1)
    full_shape = (2, HEADS, REL)
    return jnp.clip(jax.random.normal(subkeys[0], full_shape, jnp.float32), -4.0, 4.0)


def strengthened(result, stream_key, source, target, blocks, factor):
    owner, partner = [(jnp.arange(result.shape[dim]) // (result.shape[dim] // blocks)).reshape([-1 if axis == dim else 1 for axis in range(result.ndim)]) for dim in (source, target)]
    chosen = jax.random.permutation(stream_key, blocks)[partner]
    strong = (owner == chosen) | (owner == (partner + blocks // 2) % blocks)
    return jnp.where(strong, factor * result, result)


def shard_levels(rng, dims, shards, low, top_value):
    gain = 1.0
    for dim, blocks in shards:
        steps = jax.random.uniform(jax.random.fold_in(jax.random.fold_in(rng, 6), dim), (blocks,), jnp.float32, low / len(shards), top_value / len(shards))
        gain = gain * jnp.repeat(jnp.exp(steps), dims[dim] // blocks).reshape((-1,) + (1,) * (len(dims) - 1 - dim))
    return gain


def split_up(count, total, bound, lean):
    weights = [(1 << 20) // math.isqrt(grade ** lean) + 1 for grade in range(2, count + 1)]
    surplus, holding = total - bound - (count - 1), [1] * (count - 1)
    while surplus > 0:
        free = [i for i in range(count - 1) if holding[i] < bound]
        whole, left = sum([weights[i] for i in free]), surplus
        for i in free:
            addition = min(bound - holding[i], max(1, left * weights[i] // whole), surplus)
            holding[i] = holding[i] + addition
            surplus = surplus - addition
    return np.array([bound] + holding)


def uneven_parts(rng, count, total, limit, skew):
    if count == 2:
        one = jax.random.randint(rng, (), max(1, total - limit), min(limit, total - 1) + 1)
        return jnp.stack([one, total - one])
    lengths = jnp.asarray(split_up(count, total, limit, skew), jnp.int32)
    couples = (count - 1) // 2
    donor, taker = lengths[1:1 + 2 * couples:2], lengths[2:2 + 2 * couples:2]
    margin = jnp.minimum(donor - 1, limit - taker)
    passed = jax.random.randint(jax.random.fold_in(rng, 1), (couples,), 0, 1 << 20) % (margin + 1)
    lengths = lengths.at[1:1 + 2 * couples:2].set(donor - passed).at[2:2 + 2 * couples:2].set(taker + passed)
    return lengths[jax.random.permutation(jax.random.fold_in(rng, 2), count)]


def gaussian(rng, shape, deviation, bound, cuts=(), kind=jnp.bfloat16):
    array = jax.random.normal(rng, shape, jnp.float32) * deviation
    if len(cuts) > 0:
        array = shard_levels(rng, shape, cuts, -0.22, 0.18) * array
    return jnp.clip(array, min=-bound, max=bound).astype(kind)


def noise_with(own_key, dims, width, most, cuts, heavy, held_as=jnp.bfloat16):
    array = width * jax.random.normal(own_key, dims, jnp.float32)
    if cuts:
        array = array * shard_levels(own_key, dims, cuts, -0.22, 0.18)
    return jnp.clip(strengthened(array, jax.random.fold_in(own_key, 3), *heavy), -most, most).astype(held_as)


def setup_inputs(seed: int = 0) -> dict:
    splits = jax.random.split(jax.random.key(seed), 8)
    x_in = draw_x_in(jax.random.fold_in(splits[7], 71), 0)
    out_grad = noise_with(splits[1], (2, LEVELS, NLAT, NLON, D), 1.0, 6.0, ((0, 2), (2, 8), (3, 32)), (3, 4, 32, 2.75))
    w_qkv = gaussian(splits[2], (2, 3 * D, D), D ** -0.5, 0.25, ((0, 2),))
    w_proj = gaussian(splits[3], (2, D, D), D ** -0.5, 0.25, ((0, 2),))
    norm_gain = jnp.clip(1.0 + 0.15 * jax.random.normal(splits[4], (2, D), jnp.float32), 0.25, 1.75)
    bias_table = draw_bias_table(jax.random.fold_in(splits[7], 71), 0)
    lat_labels = jnp.searchsorted(jnp.cumsum(uneven_parts(splits[6], NLAT // 4, NLAT, 8, 0)), jnp.arange(NLAT), side="right").astype(jnp.int32)
    return dict(x_in=x_in, out_grad=out_grad, w_qkv=w_qkv, w_proj=w_proj, norm_gain=norm_gain, bias_table=bias_table, lat_labels=lat_labels)


EPSILON = 1e-05
MASKED = -1e+30

def mixing(formula, left_side, right_side):
    return jnp.einsum(formula, left_side.astype(jnp.float32), right_side.astype(jnp.float32))

def window_split(grid_field):
    levels, lat_rows, lon_cols, features = grid_field.shape
    grid_field = grid_field.reshape(levels // WIN_LEV, WIN_LEV, lat_rows // WIN_LAT, WIN_LAT, lon_cols // WIN_LON, WIN_LON, features)
    grid_field = grid_field.transpose(0, 2, 4, 1, 3, 5, 6)
    return grid_field.reshape(-1, WIN_LEV * WIN_LAT * WIN_LON, features)

def window_merge(blocks, levels, lat_rows, lon_cols):
    features = blocks.shape[-1]
    grid_field = blocks.reshape(levels // WIN_LEV, lat_rows // WIN_LAT, lon_cols // WIN_LON, WIN_LEV, WIN_LAT, WIN_LON, features)
    grid_field = grid_field.transpose(0, 3, 1, 4, 2, 5, 6)
    return grid_field.reshape(levels, lat_rows, lon_cols, features)

def make_tags(labels_shifted, levels, lon_cols):
    position = jnp.arange(levels, dtype=jnp.int32)
    region = jnp.where(position < levels - 2, 0, jnp.where(position == levels - 2, 1, 2)).astype(jnp.int32)
    tag_grid = 3 * labels_shifted[None, :, None] + region[:, None, None]
    tag_grid = jnp.broadcast_to(tag_grid, (levels, labels_shifted.shape[0], lon_cols))
    return window_split(tag_grid[..., None])[..., 0]

def selector(extent):
    offsets = jnp.arange(extent, dtype=jnp.int32)
    target = offsets[:, None] - offsets[None, :] + extent - 1
    return (target[:, :, None] == jnp.arange(2 * extent - 1, dtype=jnp.int32)[None, None, :]).astype(jnp.float32)

def window_bias(rel_table):
    head_count = rel_table.shape[0]
    table_grid = rel_table.reshape(head_count, 2 * WIN_LEV - 1, 2 * WIN_LAT - 1, 2 * WIN_LON - 1)
    highest = lax.Precision.HIGHEST
    step_one = jnp.einsum('habc,pqa->hpqbc', table_grid, selector(WIN_LEV), precision=highest)
    step_two = jnp.einsum('hpqbc,rsb->hpqrsc', step_one, selector(WIN_LAT), precision=highest)
    step_three = jnp.einsum('hpqrsc,tuc->hpqrstu', step_two, selector(WIN_LON), precision=highest)
    cell_count = WIN_LEV * WIN_LAT * WIN_LON
    return step_three.transpose(0, 1, 3, 5, 2, 4, 6).reshape(head_count, cell_count, cell_count)

def recompute(blocks, tag_blocks, qkv_weight, gain_vector, attn_bias):
    window_count, cell_count, features = blocks.shape
    head_dim = features // HEADS
    values_wide = blocks.astype(jnp.float32)
    center = lax.optimization_barrier(jnp.mean(values_wide, axis=-1, keepdims=True))
    spread = lax.optimization_barrier(jnp.mean(jnp.square(values_wide - center), axis=-1, keepdims=True))
    inv_std = lax.rsqrt(spread + EPSILON)
    normed = (values_wide - center) * inv_std
    scaled_input = (normed * gain_vector).astype(jnp.bfloat16)
    projected = mixing('wnd,ed->wne', scaled_input, qkv_weight).astype(jnp.bfloat16)
    split_heads = projected.reshape(window_count, cell_count, 3, HEADS, head_dim)
    query_heads = split_heads[:, :, 0]
    key_heads = split_heads[:, :, 1]
    value_heads = split_heads[:, :, 2]
    score_scale = head_dim ** (-0.5)
    scores = mixing('wihc,wjhc->whij', query_heads, key_heads) * score_scale + attn_bias[None]
    allowed = tag_blocks[:, None, :, None] == tag_blocks[:, None, None, :]
    scores = jnp.where(allowed, scores, MASKED)
    row_max = lax.optimization_barrier(jnp.max(scores, axis=-1, keepdims=True))
    weights = jnp.exp(scores - row_max)
    attention = weights / lax.optimization_barrier(jnp.sum(weights, axis=-1, keepdims=True))
    return (scaled_input, normed, inv_std, query_heads, key_heads, value_heads, attention, attention.astype(jnp.bfloat16))

def backprop(stored, grad_blocks, qkv_weight, proj_weight, gain_vector):
    scaled_input, normed, inv_std, query_heads, key_heads, value_heads, attention, attention_low = stored
    window_count, cell_count, features = grad_blocks.shape
    head_dim = features // HEADS
    score_scale = head_dim ** (-0.5)
    d_attended = mixing('wne,ed->wnd', grad_blocks, proj_weight).astype(jnp.bfloat16)
    d_heads = d_attended.reshape(window_count, cell_count, HEADS, head_dim)
    d_probs = mixing('wihc,wjhc->whij', d_heads, value_heads)
    d_value = mixing('whij,wihc->wjhc', attention_low, d_heads)
    inner_sum = lax.optimization_barrier(jnp.sum(attention * d_probs, axis=-1, keepdims=True))
    d_scores = (attention * (d_probs - inner_sum)).astype(jnp.bfloat16)
    d_query = mixing('whij,wjhc->wihc', d_scores, key_heads) * score_scale
    d_key = mixing('whij,wihc->wjhc', d_scores, query_heads) * score_scale
    d_qkv = jnp.stack([d_query, d_key, d_value], axis=2).reshape(window_count, cell_count, 3 * features)
    d_normed = mixing('wne,ed->wnd', d_qkv.astype(jnp.bfloat16), qkv_weight) * gain_vector
    d_shifted = inv_std * (d_normed - lax.optimization_barrier(jnp.mean(d_normed, axis=-1, keepdims=True)) - normed * lax.optimization_barrier(jnp.mean(d_normed * normed, axis=-1, keepdims=True)))
    return (d_shifted, d_qkv)

def phase_pass(blocks, tag_blocks, cotangents, qkv_weight, proj_weight, gain_vector, attn_bias, group_size):
    group_count = blocks.shape[0] // group_size
    features = blocks.shape[-1]

    def regroup(array_in):
        return array_in.reshape((group_count, group_size) + array_in.shape[1:])

    def one_group(running, pieces):
        stored = recompute(pieces[0], pieces[1], qkv_weight, gain_vector, attn_bias)
        results = [backprop(stored, member, qkv_weight, proj_weight, gain_vector) for member in pieces[2:]]
        summed = results[0][1]
        for further in results[1:]:
            summed = summed + further[1]
        grad_low = summed.astype(jnp.bfloat16).reshape(-1, 3 * features)
        flat_input = stored[0].reshape(-1, features)
        running = running + jnp.dot(grad_low.T, flat_input, preferred_element_type=jnp.float32)
        return (running, tuple((further[0] for further in results)))
    start_sum = jnp.zeros((3 * features, features), jnp.float32)
    pieces = (regroup(blocks), regroup(tag_blocks)) + tuple((regroup(member) for member in cotangents))
    running, outputs = lax.scan(one_group, start_sum, pieces)
    return (running, tuple((member.reshape(blocks.shape) for member in outputs)))

def reference(x_in, out_grad, w_qkv, w_proj, norm_gain, bias_table, lat_labels):
    lat_half = WIN_LAT // 2
    lon_half = WIN_LON // 2
    lev_half = WIN_LEV // 2

    def forward_roll(grid_field):
        return jnp.roll(grid_field, (-lev_half, -lat_half, -lon_half), axis=(0, 1, 2))

    def backward_roll(grid_field):
        return jnp.roll(grid_field, (lev_half, lat_half, lon_half), axis=(0, 1, 2))
    labels_shifted = jnp.roll(lat_labels, -lat_half)
    tag_blocks = make_tags(labels_shifted, LEVELS, NLON)
    group_size = NLON // WIN_LON

    def run_phase(phase_index, cotangents):
        blocks = window_split(forward_roll(x_in[phase_index]))
        cot_blocks = tuple((window_split(forward_roll(member)) for member in cotangents))
        attn_bias = window_bias(bias_table[phase_index])
        return phase_pass(blocks, tag_blocks, cot_blocks, w_qkv[phase_index], w_proj[phase_index], norm_gain[phase_index], attn_bias, group_size)
    total_dec, dec_parts = run_phase(1, (out_grad[1],))
    dec_grad = out_grad[1].astype(jnp.float32) + backward_roll(window_merge(dec_parts[0], LEVELS, NLAT, NLON))
    skip_grad = dec_grad.astype(jnp.bfloat16)
    total_enc, enc_parts = run_phase(0, (out_grad[0], skip_grad))
    first_part = out_grad[0].astype(jnp.float32) + backward_roll(window_merge(enc_parts[0], LEVELS, NLAT, NLON))
    second_part = skip_grad.astype(jnp.float32) + backward_roll(window_merge(enc_parts[1], LEVELS, NLAT, NLON))
    enc_grad = first_part + second_part
    grad_input = jnp.stack([enc_grad.astype(jnp.bfloat16), skip_grad])
    grad_qkv = jnp.stack([total_enc, total_dec])
    return (grad_input, grad_qkv)
```

```python
import functools

import jax
import jax.numpy as jnp
from jax import lax
from jax.experimental import pallas as pl
from jax.experimental.pallas import tpu as pltpu
from jax.sharding import PartitionSpec as P

F32 = jnp.float32
BF16 = jnp.bfloat16
HEADS = 8
FEATURES = 512
EPSILON = 1e-05
MASKED = -1e30
SCORE_SCALE = 0.125
VMEM_LIMIT = 40 * 1024 * 1024

LEVEL_ROWS = 96
ROWS = 192
PACKED_ROWS = 144


def call(kernel, out_shape, scratch=(), smem_first=0):
    def run(*args):
        specs = [
            pl.BlockSpec(memory_space=pltpu.SMEM if i < smem_first else pltpu.VMEM)
            for i in range(len(args))
        ]
        outs = jax.tree.map(lambda _: pl.BlockSpec(memory_space=pltpu.VMEM), out_shape)
        return pl.pallas_call(
            kernel,
            out_shape=out_shape,
            in_specs=specs,
            out_specs=outs,
            scratch_shapes=list(scratch),
            compiler_params=pltpu.CompilerParams(vmem_limit_bytes=VMEM_LIMIT),
        )(*args)

    return run


def struct(shape, dtype):
    return jax.ShapeDtypeStruct(shape, dtype)


def dot(left, right, dims=((1,), (0,))):
    return lax.dot_general(left, right, (dims, ((), ())), preferred_element_type=F32)


def row_index(shape, dim):
    return lax.broadcasted_iota(jnp.int32, shape, dim)


def cut_kernel(labels, x_ref, g_ref, own, lon, lat, cor):
    row = row_index((8, FEATURES), 0)

    def halves(ref, level, i, fill):
        low = ref[0, level, i, 0:8, :].astype(F32)
        high = ref[0, level, i, 4:12, :].astype(F32)
        return (
            jnp.where(row < 6, low, fill),
            jnp.where(row < 6, pltpu.roll(high, 6, 0), fill),
        )

    for level in range(2):
        for i in range(6):
            label = labels[i].astype(F32)
            x_low, x_high = halves(x_ref, level, i, label)
            g_low, g_high = halves(g_ref, level, i, 0.0)
            low = jnp.concatenate([x_low, g_low], axis=0).astype(BF16)
            high = jnp.concatenate([x_high, g_high], axis=0).astype(BF16)
            if i < 3:
                cor[level, i] = low
                lat[level, i] = high
            else:
                lon[level, i - 3] = low
                own[level, i - 3] = high


def bias_kernel(table, out):
    parts = []
    for h in range(HEADS):
        line = jnp.broadcast_to(table[h : h + 1, :], (8, 256))
        parts.append(pltpu.roll(line, 0, 1, stride=1, stride_axis=0))
        parts.append(pltpu.roll(line, 6, 1, stride=1, stride_axis=0))
    shifted = jnp.concatenate(parts, axis=0)
    source = row_index((256, 256), 0)
    lane = row_index((256, 256), 1)
    column = lane & 7
    target = (lane >> 4) * 23 + ((lane >> 3) & 1) * 6 + column + 11
    picked = jnp.where((source == target) & (column < 6), 1.0, 0.0).astype(BF16)
    first = shifted.astype(BF16)
    rest = shifted - first.astype(F32)
    second = rest.astype(BF16)
    third = (rest - second.astype(F32)).astype(BF16)
    spread = dot(first, picked) + dot(second, picked) + dot(third, picked)
    empty = (row_index((128, 128), 0) & 7) >= 6
    for b in range(6):
        shift = (256 - (5 - b) * 16) % 256
        moved = spread if shift == 0 else pltpu.roll(spread, shift, 1)
        moved = jnp.where(empty, MASKED, moved[:, :128])
        for h in range(HEADS):
            out[h * 96 + b * 16 : h * 96 + b * 16 + 16, :] = moved[h * 16 : h * 16 + 16, :]


def pack_rows(array):
    columns = array.shape[1]
    groups = array.reshape(6, 4, 8, columns)
    row = row_index((8, columns), 0)
    out = []
    for q in range(6):
        last = groups[q, 3]
        for g in range(3):
            out.append(jnp.where(row < 6, groups[q, g], pltpu.roll(last, 6 - 2 * g, 0)))
    return jnp.concatenate(out, axis=0)


def attention_backward(att, d_low, q_ref, k_ref, v_ref, dqkv):
    lane = row_index((LEVEL_ROWS, 128), 1)
    for level in range(2):
        rows = slice(level * LEVEL_ROWS, (level + 1) * LEVEL_ROWS)
        for pair in range(4):
            cols = slice(pair * 128, (pair + 1) * 128)
            probs = att(level, pair)
            probs_low = probs.astype(BF16).reshape(2 * LEVEL_ROWS, LEVEL_ROWS)
            d_out = d_low[rows, cols]
            query = q_ref[rows, cols]
            keys = k_ref[:, rows, cols].reshape(2 * LEVEL_ROWS, 128)
            values = v_ref[:, rows, cols].reshape(2 * LEVEL_ROWS, 128)
            d_probs = dot(values, d_out, ((1,), (1,))).reshape(2, LEVEL_ROWS, LEVEL_ROWS)
            inner = jnp.sum(probs * d_probs, axis=1, keepdims=True)
            d_scores = (probs * (d_probs - inner)).astype(BF16).reshape(2 * LEVEL_ROWS, LEVEL_ROWS)
            d_value = dot(probs_low, d_out)
            d_key = dot(d_scores, query)
            d_query = dot(d_scores, keys, ((0,), (0,)))
            dqkv[rows, pair * 128 : (pair + 1) * 128] = d_query * SCORE_SCALE
            dqkv[rows, 512 + pair * 128 : 512 + (pair + 1) * 128] = (
                jnp.where(lane < 64, d_key[:LEVEL_ROWS], d_key[LEVEL_ROWS:]) * SCORE_SCALE
            )
            dqkv[rows, 1024 + pair * 128 : 1024 + (pair + 1) * 128] = jnp.where(
                lane < 64, d_value[:LEVEL_ROWS], d_value[LEVEL_ROWS:]
            )


def input_gradient(dqkv, w_qkv, gain, normed, inv_std):
    d_normed = dot(dqkv[...].astype(BF16), w_qkv[...]) * gain[...]
    mean_plain = jnp.mean(d_normed, axis=-1, keepdims=True)
    mean_normed = jnp.mean(d_normed * normed, axis=-1, keepdims=True)
    return inv_std * (d_normed - mean_plain - normed * mean_normed)


def first_kernel(
    own, lon, lat, cor, w_qkv, w_proj, gain, bias,
    skip, packed_input, cot, d_first, normed_out, inv_out, q_out, k_out, v_out, att_out,
    dqkv,
):
    tiles_x, tiles_g = [], []
    labels = []
    row = row_index((8, FEATURES), 0)
    for level in range(2):
        for i in range(6):
            left, right = (own, lon) if i < 3 else (lat, cor)
            left, right = left[level, i % 3].astype(F32), right[level, i % 3].astype(F32)
            if level == 0:
                labels.append(left[6:7, :128])
            for tile in (left, right):
                tiles_x.append(jnp.where(row < 6, tile[:8], 0.0))
                tiles_g.append(tile[8:])
    x = jnp.concatenate(tiles_x, axis=0)
    c = jnp.concatenate(tiles_g, axis=0)
    center = jnp.mean(x, axis=-1, keepdims=True)
    moved = x - center
    spread = jnp.mean(jnp.square(moved), axis=-1, keepdims=True)
    inv_std = lax.rsqrt(spread + EPSILON)
    normed = moved * inv_std
    scaled = normed * gain[...]
    packed_input[...] = pack_rows(scaled).astype(BF16)
    projected = dot(scaled.astype(BF16), w_qkv[...], ((1,), (1,)))
    c_low = c.astype(BF16)
    d_first_value = dot(c_low, w_proj[...])
    cot[...] = c_low
    d_first[...] = d_first_value
    normed_out[...] = normed
    inv_out[...] = jnp.broadcast_to(inv_std, (ROWS, 128))
    q_out[...] = projected[:, :512].astype(BF16)
    even = (row_index((ROWS, 512), 1) & 64) == 0
    k = projected[:, 512:1024]
    v = projected[:, 1024:]
    k_out[0] = jnp.where(even, k, 0.0).astype(BF16)
    k_out[1] = jnp.where(even, 0.0, k).astype(BF16)
    v_out[0] = jnp.where(even, v, 0.0).astype(BF16)
    v_out[1] = jnp.where(even, 0.0, v).astype(BF16)

    lane_row = row_index((1, 128), 1) >> 4
    along = labels[0]
    for b in range(1, 6):
        along = jnp.where(lane_row == b, labels[b], along)
    allowed = jnp.concatenate(
        [
            jnp.broadcast_to(jnp.where(labels[b] == along, 0.0, MASKED), (16, 128))
            for b in range(6)
        ],
        axis=0,
    )

    def probabilities(level, pair):
        rows = slice(level * LEVEL_ROWS, (level + 1) * LEVEL_ROWS)
        cols = slice(pair * 128, (pair + 1) * 128)
        added = bias[pair * 192 : (pair + 1) * 192, :].reshape(2, LEVEL_ROWS, 128) + allowed[None]
        keys = k_out[:, rows, cols].reshape(2 * LEVEL_ROWS, 128)
        scores = dot(keys, q_out[rows, cols], ((1,), (1,))).reshape(2, LEVEL_ROWS, LEVEL_ROWS)
        scores = scores * SCORE_SCALE + added[:, :, :LEVEL_ROWS]
        weights = jnp.exp(scores - jnp.max(scores, axis=1, keepdims=True))
        probs = weights * (1.0 / jnp.sum(weights, axis=1, keepdims=True))
        att_out[level, pair] = probs
        return probs

    attention_backward(probabilities, d_first_value.astype(BF16), q_out, k_out, v_out, dqkv)
    skip[...] = (c + input_gradient(dqkv, w_qkv, gain, normed, inv_std)).astype(BF16)


def second_kernel(
    arrived, cot, d_first, normed, inv, q_ref, k_ref, v_ref, att, w_qkv, w_proj, gain,
    blocks, own, lon, lat, cor, dqkv,
):
    c2 = arrived[...]
    d_low = (d_first[...] + dot(c2, w_proj[...])).astype(BF16)
    attention_backward(lambda level, pair: att[level, pair], d_low, q_ref, k_ref, v_ref, dqkv)
    lane = row_index((80, 128), 1)
    for t in range(4):
        whole = [pack_rows(dqkv[:, 384 * t + 128 * j : 384 * t + 128 * (j + 1)]) for j in range(3)]
        blocks[2 * t, :144, :] = whole[0].astype(BF16)
        blocks[2 * t + 1, :144, :] = whole[2].astype(BF16)
        top = whole[1][:80]
        bottom = jnp.concatenate([whole[1][80:], jnp.zeros((16, 128), F32)], axis=0)
        blocks[2 * t, 144:, :] = jnp.where(lane < 64, top, pltpu.roll(bottom, 64, 1)).astype(BF16)
        blocks[2 * t + 1, 144:, :] = jnp.where(lane < 64, pltpu.roll(top, 64, 1), bottom).astype(BF16)
    shifted = input_gradient(dqkv, w_qkv, gain, normed[...], inv[:, 0:1])
    total = cot[...].astype(F32) + (c2.astype(F32) + shifted)
    for i in range(6):
        for half in range(2):
            start = 16 * i + 8 * half
            both = jnp.concatenate(
                [total[start : start + 8], total[96 + start : 96 + start + 8]], axis=0
            )
            target = ((own, lon), (lat, cor))[i // 3][half]
            target[i % 3] = both.astype(BF16)


def product_kernel(blocks, inputs, out):
    whole = jnp.zeros((128, FEATURES), F32)
    upper = jnp.zeros((128, FEATURES), F32)
    lower = jnp.zeros((128, FEATURES), F32)
    for p in range(blocks.shape[0]):
        cells = inputs[p]
        whole += dot(blocks[p, :144], cells, ((0,), (0,)))
        folded = blocks[p, 144:]
        upper += dot(folded, cells[:80], ((0,), (0,)))
        lower += dot(folded[:64], cells[80:], ((0,), (0,)))
    half = upper[:64] + lower[64:]
    whole_t = whole.T
    half_t = jnp.concatenate([half, jnp.zeros((64, FEATURES), F32)], axis=0).T
    bands = out.shape[0]
    width = FEATURES // bands
    lane = row_index((width // 2, 128), 1)
    for band in range(bands):
        out[band, :width, :] = whole_t[band * width : (band + 1) * width].astype(BF16)
        part = half_t[band * width : (band + 1) * width]
        out[band, width:, :] = jnp.where(
            lane < 64, part[: width // 2], pltpu.roll(part[width // 2 :], 64, 1)
        ).astype(BF16)


def sum_kernel(odd, parts, out):
    bands, rows, _ = parts.shape
    width = rows * 2 // 3
    total = parts[0].astype(F32)
    for band in range(1, bands):
        total = total + parts[band].astype(F32)
    whole = total[:width]
    folded = total[width:]
    half = jnp.concatenate([folded, pltpu.roll(folded, 64, 1)], axis=0)
    pad = jnp.zeros((128 - width, 128), F32)
    whole_t = jnp.concatenate([whole, pad], axis=0).T[:, :width]
    half_t = jnp.concatenate([half, pad], axis=0).T[:64, :width]

    @pl.when(odd[0] == 0)
    def _():
        out[0, :128, :] = whole_t
        out[0, 128:, :] = half_t

    @pl.when(odd[0] == 1)
    def _():
        out[0, :64, :] = half_t
        out[0, 64:, :] = whole_t


def join_kernel(own, lon, lat, cor, out):
    row = row_index((8, FEATURES), 0)
    for level in range(2):
        part = slice(level * 8, level * 8 + 8)
        for i in range(6):
            left, right = (cor, lat) if i < 3 else (lon, own)
            left = left[i % 3].astype(F32)[part]
            right = pltpu.roll(right[i % 3].astype(F32)[part], 6, 0)
            out[0, level, i, 0:8, :] = jnp.where(row < 6, left, right).astype(BF16)
            out[0, level, i, 8:12, :] = right[:4].astype(BF16)


def passed(array, lat_by, lon_by):
    lats, lons = lax.axis_size("lat"), lax.axis_size("lon")
    pairs = [
        (a * lons + o, ((a + lat_by) % lats) * lons + (o + lon_by) % lons)
        for a in range(lats)
        for o in range(lons)
    ]
    return lax.ppermute(array, ("lat", "lon"), pairs)


def per_device(x_in, out_grad, w_qkv, w_proj, norm_gain, bias_table, lat_labels):
    lats, lons = lax.axis_size("lat"), lax.axis_size("lon")
    w_qkv, w_proj = w_qkv[0], w_proj[0]
    piece = struct((2, 3, 16, FEATURES), BF16)
    own, lon, lat, cor = call(cut_kernel, (piece,) * 4, smem_first=1)(lat_labels, x_in, out_grad)
    lon = passed(lon, 0, -1)
    lat = passed(lat, -1, 0)
    cor = passed(cor, -1, -1)
    table = jnp.pad(bias_table[0, :, 253:506], ((0, 0), (0, 3)))
    bias = call(bias_kernel, struct((HEADS * LEVEL_ROWS, 128), F32))(table)

    window = struct((ROWS, FEATURES), BF16)
    wide = struct((ROWS, FEATURES), F32)
    scratch = [pltpu.VMEM((ROWS, 3 * FEATURES), F32)]
    skip, packed_input, cot, d_first, normed, inv, q, k, v, att = call(
        first_kernel,
        (
            window,
            struct((PACKED_ROWS, FEATURES), BF16),
            window,
            wide,
            wide,
            struct((ROWS, 128), F32),
            window,
            struct((2, ROWS, FEATURES), BF16),
            struct((2, ROWS, FEATURES), BF16),
            struct((2, 4, 2, LEVEL_ROWS, LEVEL_ROWS), F32),
        ),
        scratch,
    )(own, lon, lat, cor, w_qkv, w_proj, norm_gain, bias)

    inputs = lax.all_gather(packed_input, "lat", axis=0, tiled=False)
    arrived = lax.ppermute(skip, "phase", [(1, 0)])
    back = struct((3, 16, FEATURES), BF16)
    blocks, own, lon, lat, cor = call(
        second_kernel,
        (struct((8, 224, 128), BF16), back, back, back, back),
        scratch,
    )(arrived, cot, d_first, normed, inv, q, k, v, att, w_qkv, w_proj, norm_gain)
    lon = passed(lon, 0, 1)
    lat = passed(lat, 1, 0)
    cor = passed(cor, 1, 1)
    blocks = lax.all_to_all(blocks, "lat", 0, 0, tiled=True)
    slices = call(product_kernel, struct((lons, FEATURES * 3 // 2 // lons, 128), BF16))(
        blocks, inputs
    )
    slices = lax.all_to_all(slices, "lon", 0, 0, tiled=True)
    odd = (lax.axis_index("lat") % 2).astype(jnp.int32).reshape(1)
    grad_qkv = call(sum_kernel, struct((1, 192, FEATURES // lons), F32), smem_first=1)(odd, slices)
    grad_input = call(join_kernel, struct((1, 2, 6, 12, FEATURES), BF16))(own, lon, lat, cor)
    return grad_input, grad_qkv


def solution(mesh):
    in_specs = (
        P("phase", None, "lat", "lon", None),
        P("phase", None, "lat", "lon", None),
        P("phase", None, None),
        P("phase", None, None),
        P("phase", None),
        P("phase", None, None),
        P("lat"),
    )
    out_specs = (P("phase", None, "lat", "lon", None), P("phase", "lat", "lon"))
    return jax.shard_map(
        per_device, mesh=mesh, in_specs=in_specs, out_specs=out_specs, check_vma=False
    )
```

```python
import functools

import jax
import jax.numpy as jnp
from jax import lax
from jax.experimental import pallas as pl
from jax.experimental.pallas import tpu as pltpu
from jax.sharding import PartitionSpec as P

F32 = jnp.float32
BF16 = jnp.bfloat16
HEADS = 8
FEATURES = 512
EPSILON = 1e-05
MASKED = -1e30
SCORE_SCALE = 0.125
VMEM_LIMIT = 16 * 1024 * 1024

LEVEL_ROWS = 96
ROWS = 192
PACKED_ROWS = 144


def call(kernel, out_shape, scratch=(), places=(), out_places=()):
    def run(*args):
        places_of = dict(places)
        specs = [
            pl.BlockSpec(memory_space=places_of.get(i, pltpu.VMEM)) for i in range(len(args))
        ]
        outs_of = dict(out_places)
        outs = [
            pl.BlockSpec(memory_space=outs_of.get(i, pltpu.VMEM))
            for i in range(len(jax.tree.leaves(out_shape)))
        ]
        outs = tuple(outs) if isinstance(out_shape, tuple) else outs[0]
        return pl.pallas_call(
            kernel,
            out_shape=out_shape,
            in_specs=specs,
            out_specs=outs,
            scratch_shapes=list(scratch),
            compiler_params=pltpu.CompilerParams(vmem_limit_bytes=VMEM_LIMIT),
        )(*args)

    return run


def struct(shape, dtype):
    return jax.ShapeDtypeStruct(shape, dtype)


def dot(left, right, dims=((1,), (0,))):
    return lax.dot_general(left, right, (dims, ((), ())), preferred_element_type=F32)


def row_index(shape, dim):
    return lax.broadcasted_iota(jnp.int32, shape, dim)


def cut_kernel(labels_ref, x_ref, g_ref, own, lon, lat, cor, labels, sem):
    fetch = pltpu.make_async_copy(labels_ref, labels, sem)
    fetch.start()
    fetch.wait()
    row = row_index((8, FEATURES), 0)

    def halves(ref, level, i, fill):
        low = ref[0, level, i, 0:8, :].astype(F32)
        high = ref[0, level, i, 4:12, :].astype(F32)
        return (
            jnp.where(row < 6, low, fill),
            jnp.where(row < 6, pltpu.roll(high, 6, 0), fill),
        )

    for level in range(2):
        for i in range(6):
            label = labels[i].astype(F32)
            x_low, x_high = halves(x_ref, level, i, label)
            g_low, g_high = halves(g_ref, level, i, 0.0)
            low = jnp.concatenate([x_low, g_low], axis=0).astype(BF16)
            high = jnp.concatenate([x_high, g_high], axis=0).astype(BF16)
            if i < 3:
                cor[level, i] = low
                lat[level, i] = high
            else:
                lon[level, i - 3] = low
                own[level, i - 3] = high


def bias_kernel(table, out):
    parts = []
    for h in range(HEADS):
        line = jnp.broadcast_to(table[h : h + 1, :], (8, 256))
        parts.append(pltpu.roll(line, 0, 1, stride=1, stride_axis=0))
        parts.append(pltpu.roll(line, 6, 1, stride=1, stride_axis=0))
    shifted = jnp.concatenate(parts, axis=0)
    source = row_index((256, 256), 0)
    lane = row_index((256, 256), 1)
    column = lane & 7
    target = (lane >> 4) * 23 + ((lane >> 3) & 1) * 6 + column + 11
    picked = jnp.where((source == target) & (column < 6), 1.0, 0.0).astype(BF16)
    first = shifted.astype(BF16)
    rest = shifted - first.astype(F32)
    second = rest.astype(BF16)
    third = (rest - second.astype(F32)).astype(BF16)
    spread = dot(first, picked) + dot(second, picked) + dot(third, picked)
    empty = (row_index((128, 128), 0) & 7) >= 6
    for b in range(6):
        shift = (256 - (5 - b) * 16) % 256
        moved = spread if shift == 0 else pltpu.roll(spread, shift, 1)
        moved = jnp.where(empty, MASKED, moved[:, :128])
        for h in range(HEADS):
            out[h * 96 + b * 16 : h * 96 + b * 16 + 16, :] = moved[h * 16 : h * 16 + 16, :]


def pack_rows(array):
    columns = array.shape[1]
    groups = array.reshape(6, 4, 8, columns)
    row = row_index((8, columns), 0)
    out = []
    for q in range(6):
        last = groups[q, 3]
        for g in range(3):
            out.append(jnp.where(row < 6, groups[q, g], pltpu.roll(last, 6 - 2 * g, 0)))
    return jnp.concatenate(out, axis=0)


def per_head(pair):
    even = row_index(pair.shape, 1) < 64
    wide = pair.astype(F32)
    return jnp.concatenate(
        [jnp.where(even, wide, 0.0).astype(BF16), jnp.where(even, 0.0, wide).astype(BF16)], axis=0
    )


def attention_backward(att, d_low, projected, dqkv):
    lane = row_index((LEVEL_ROWS, 128), 1)
    for level in range(2):
        rows = slice(level * LEVEL_ROWS, (level + 1) * LEVEL_ROWS)
        for pair in range(4):
            cols = slice(pair * 128, (pair + 1) * 128)
            probs = att(level, pair)
            probs_low = probs.astype(BF16).reshape(2 * LEVEL_ROWS, LEVEL_ROWS)
            d_out = d_low[rows, cols]
            query = projected[rows, cols]
            keys = per_head(projected[rows, 512 + pair * 128 : 512 + (pair + 1) * 128])
            values = per_head(projected[rows, 1024 + pair * 128 : 1024 + (pair + 1) * 128])
            d_probs = dot(values, d_out, ((1,), (1,))).reshape(2, LEVEL_ROWS, LEVEL_ROWS)
            inner = jnp.sum(probs * d_probs, axis=1, keepdims=True)
            d_scores = (probs * (d_probs - inner)).astype(BF16).reshape(2 * LEVEL_ROWS, LEVEL_ROWS)
            d_value = dot(probs_low, d_out)
            d_key = dot(d_scores, query)
            d_query = dot(d_scores, keys, ((0,), (0,)))
            dqkv[rows, pair * 128 : (pair + 1) * 128] = d_query * SCORE_SCALE
            dqkv[rows, 512 + pair * 128 : 512 + (pair + 1) * 128] = (
                jnp.where(lane < 64, d_key[:LEVEL_ROWS], d_key[LEVEL_ROWS:]) * SCORE_SCALE
            )
            dqkv[rows, 1024 + pair * 128 : 1024 + (pair + 1) * 128] = jnp.where(
                lane < 64, d_value[:LEVEL_ROWS], d_value[LEVEL_ROWS:]
            )


def input_gradient(dqkv, w_qkv, gain, normed, inv_std):
    d_normed = dot(dqkv[...].astype(BF16), w_qkv[...]) * gain[...]
    mean_plain = jnp.mean(d_normed, axis=-1, keepdims=True)
    mean_normed = jnp.mean(d_normed * normed, axis=-1, keepdims=True)
    return inv_std * (d_normed - mean_plain - normed * mean_normed)


def first_kernel(
    own, lon, lat, cor, w_qkv, w_proj, gain, bias,
    skip, inputs_out, cot, normed_out, inv_out, projected_out, att_out,
    dqkv, packed, sems,
):
    tiles_x, tiles_g = [], []
    labels = []
    row = row_index((8, FEATURES), 0)
    for level in range(2):
        for i in range(6):
            left, right = (own, lon) if i < 3 else (lat, cor)
            left, right = left[level, i % 3].astype(F32), right[level, i % 3].astype(F32)
            if level == 0:
                labels.append(left[6:7, :128])
            for tile in (left, right):
                tiles_x.append(jnp.where(row < 6, tile[:8], 0.0))
                tiles_g.append(tile[8:])
    x = jnp.concatenate(tiles_x, axis=0)
    c = jnp.concatenate(tiles_g, axis=0)
    center = jnp.mean(x, axis=-1, keepdims=True)
    moved = x - center
    spread = jnp.mean(jnp.square(moved), axis=-1, keepdims=True)
    inv_std = lax.rsqrt(spread + EPSILON)
    normed = moved * inv_std
    scaled = normed * gain[...]
    packed[...] = pack_rows(scaled).astype(BF16)
    copies = [
        pltpu.make_async_copy(packed, inputs_out.at[p], sems.at[p])
        for p in range(inputs_out.shape[0])
    ]
    for copy in copies:
        copy.start()
    projected = dot(scaled.astype(BF16), w_qkv[...], ((1,), (1,)))
    c_low = c.astype(BF16)
    d_first_value = dot(c_low, w_proj[...])
    cot[...] = c_low
    normed_out[...] = normed
    inv_out[...] = jnp.broadcast_to(inv_std, (ROWS, 128))
    projected_out[...] = projected.astype(BF16)

    lane_row = row_index((1, 128), 1) >> 4
    along = labels[0]
    for b in range(1, 6):
        along = jnp.where(lane_row == b, labels[b], along)
    allowed = jnp.concatenate(
        [
            jnp.broadcast_to(jnp.where(labels[b] == along, 0.0, MASKED), (16, 128))
            for b in range(6)
        ],
        axis=0,
    )

    def probabilities(level, pair):
        rows = slice(level * LEVEL_ROWS, (level + 1) * LEVEL_ROWS)
        cols = slice(pair * 128, (pair + 1) * 128)
        added = bias[pair * 192 : (pair + 1) * 192, :].reshape(2, LEVEL_ROWS, 128) + allowed[None]
        keys = per_head(projected_out[rows, 512 + pair * 128 : 512 + (pair + 1) * 128])
        scores = dot(keys, projected_out[rows, cols], ((1,), (1,))).reshape(2, LEVEL_ROWS, LEVEL_ROWS)
        scores = scores * SCORE_SCALE + added[:, :, :LEVEL_ROWS]
        weights = jnp.exp(scores - jnp.max(scores, axis=1, keepdims=True))
        probs = weights * (1.0 / jnp.sum(weights, axis=1, keepdims=True))
        att_out[level, pair] = probs
        return probs

    attention_backward(probabilities, d_first_value.astype(BF16), projected_out, dqkv)
    skip[...] = (c + input_gradient(dqkv, w_qkv, gain, normed, inv_std)).astype(BF16)
    for copy in copies:
        copy.wait()


def second_kernel(
    arrived, cot, projected, att, w_proj,
    blocks, low, dqkv,
):
    d_low = (dot(cot[...], w_proj[...]) + dot(arrived[...], w_proj[...])).astype(BF16)
    attention_backward(lambda level, pair: att[level, pair], d_low, projected, dqkv)
    low[...] = dqkv[...].astype(BF16)
    lane = row_index((80, 128), 1)
    for t in range(4):
        whole = [pack_rows(dqkv[:, 384 * t + 128 * j : 384 * t + 128 * (j + 1)]) for j in range(3)]
        blocks[2 * t, :144, :] = whole[0].astype(BF16)
        blocks[2 * t + 1, :144, :] = whole[2].astype(BF16)
        top = whole[1][:80]
        bottom = jnp.concatenate([whole[1][80:], jnp.zeros((16, 128), F32)], axis=0)
        blocks[2 * t, 144:, :] = jnp.where(lane < 64, top, pltpu.roll(bottom, 64, 1)).astype(BF16)
        blocks[2 * t + 1, 144:, :] = jnp.where(lane < 64, pltpu.roll(top, 64, 1), bottom).astype(BF16)


def third_kernel(arrived, cot, low, normed, inv, w_qkv, gain, own, lon, lat, cor):
    shifted = input_gradient(low, w_qkv, gain, normed[...], inv[:, 0:1])
    total = cot[...].astype(F32) + (arrived[...].astype(F32) + shifted)
    for i in range(6):
        for half in range(2):
            start = 16 * i + 8 * half
            both = jnp.concatenate(
                [total[start : start + 8], total[96 + start : 96 + start + 8]], axis=0
            )
            target = ((own, lon), (lat, cor))[i // 3][half]
            target[i % 3] = both.astype(BF16)


def product_kernel(blocks, inputs, out):
    whole = jnp.zeros((128, FEATURES), F32)
    upper = jnp.zeros((128, FEATURES), F32)
    lower = jnp.zeros((128, FEATURES), F32)
    for p in range(blocks.shape[0]):
        cells = inputs[p]
        whole += dot(blocks[p, :144], cells, ((0,), (0,)))
        folded = blocks[p, 144:]
        upper += dot(folded, cells[:80], ((0,), (0,)))
        lower += dot(folded[:64], cells[80:], ((0,), (0,)))
    half = upper[:64] + lower[64:]
    whole_t = whole.T
    half_t = jnp.concatenate([half, jnp.zeros((64, FEATURES), F32)], axis=0).T
    bands = out.shape[0]
    width = FEATURES // bands
    lane = row_index((width // 2, 128), 1)
    for band in range(bands):
        out[band, :width, :] = whole_t[band * width : (band + 1) * width].astype(BF16)
        part = half_t[band * width : (band + 1) * width]
        out[band, width:, :] = jnp.where(
            lane < 64, part[: width // 2], pltpu.roll(part[width // 2 :], 64, 1)
        ).astype(BF16)


def sum_kernel(odd, parts, out):
    bands, rows, _ = parts.shape
    width = rows * 2 // 3
    total = parts[0].astype(F32)
    for band in range(1, bands):
        total = total + parts[band].astype(F32)
    whole = total[:width]
    folded = total[width:]
    half = jnp.concatenate([folded, pltpu.roll(folded, 64, 1)], axis=0)
    half = half[:, :64]

    @pl.when(odd[0] == 0)
    def _():
        out[0, :, :128] = whole
        out[0, :, 128:] = half

    @pl.when(odd[0] == 1)
    def _():
        out[0, :, :64] = half
        out[0, :, 64:] = whole


def join_kernel(own, lon, lat, cor, out):
    row = row_index((8, FEATURES), 0)
    for level in range(2):
        part = slice(level * 8, level * 8 + 8)
        for i in range(6):
            left, right = (cor, lat) if i < 3 else (lon, own)
            left = left[i % 3].astype(F32)[part]
            right = pltpu.roll(right[i % 3].astype(F32)[part], 6, 0)
            out[0, level, i, 0:8, :] = jnp.where(row < 6, left, right).astype(BF16)
            out[0, level, i, 8:12, :] = right[:4].astype(BF16)


def passed(array, lat_by, lon_by):
    lats, lons = lax.axis_size("lat"), lax.axis_size("lon")
    pairs = [
        (a * lons + o, ((a + lat_by) % lats) * lons + (o + lon_by) % lons)
        for a in range(lats)
        for o in range(lons)
    ]
    return lax.ppermute(array, ("lat", "lon"), pairs)


def per_device(x_in, out_grad, w_qkv, w_proj, norm_gain, bias_table, lat_labels):
    lats, lons = lax.axis_size("lat"), lax.axis_size("lon")
    w_qkv, w_proj = w_qkv[0], w_proj[0]
    piece = struct((2, 3, 16, FEATURES), BF16)
    own, lon, lat, cor = call(
        cut_kernel,
        (piece,) * 4,
        [pltpu.SMEM(lat_labels.shape, jnp.int32), pltpu.SemaphoreType.DMA],
        places={0: pl.ANY},
    )(lat_labels, x_in, out_grad)
    lon = passed(lon, 0, -1)
    lat = passed(lat, -1, 0)
    cor = passed(cor, -1, -1)
    table = jnp.pad(bias_table[0, :, 253:506], ((0, 0), (0, 3)))
    bias = call(bias_kernel, struct((HEADS * LEVEL_ROWS, 128), F32))(table)

    window = struct((ROWS, FEATURES), BF16)
    scratch = [pltpu.VMEM((ROWS, 3 * FEATURES), F32)]
    skip, inputs, cot, normed, inv, projected, att = call(
        first_kernel,
        (
            window,
            struct((lats, PACKED_ROWS, FEATURES), BF16),
            window,
            struct((ROWS, FEATURES), F32),
            struct((ROWS, 128), F32),
            struct((ROWS, 3 * FEATURES), BF16),
            struct((2, 4, 2, LEVEL_ROWS, LEVEL_ROWS), F32),
        ),
        scratch
        + [pltpu.VMEM((PACKED_ROWS, FEATURES), BF16), pltpu.SemaphoreType.DMA((lats,))],
        out_places={1: pl.ANY},
    )(own, lon, lat, cor, w_qkv, w_proj, norm_gain, bias)

    arrived = lax.ppermute(skip, "phase", [(1, 0)])
    inputs = lax.all_to_all(inputs, "lat", 0, 0, tiled=True)
    back = struct((3, 16, FEATURES), BF16)
    blocks, low = call(
        second_kernel,
        (struct((8, 224, 128), BF16), struct((ROWS, 3 * FEATURES), BF16)),
        scratch,
    )(arrived, cot, projected, att, w_proj)
    blocks = lax.all_to_all(blocks, "lat", 0, 0, tiled=True)
    own, lon, lat, cor = call(third_kernel, (back,) * 4)(
        arrived, cot, low, normed, inv, w_qkv, norm_gain
    )
    lon = passed(lon, 0, 1)
    lat = passed(lat, 1, 0)
    cor = passed(cor, 1, 1)
    slices = call(product_kernel, struct((lons, FEATURES * 3 // 2 // lons, 128), BF16))(
        blocks, inputs
    )
    slices = lax.all_to_all(slices, "lon", 0, 0, tiled=True)
    odd = (lax.axis_index("lat") % 2).astype(jnp.int32).reshape(1)
    grad_qkv = call(
        sum_kernel, struct((1, FEATURES // lons, 192), F32), places={0: pltpu.SMEM}
    )(odd, slices)
    grad_input = call(join_kernel, struct((1, 2, 6, 12, FEATURES), BF16))(own, lon, lat, cor)
    return grad_input, grad_qkv.transpose(0, 2, 1)


def solution(mesh):
    in_specs = (
        P("phase", None, "lat", "lon", None),
        P("phase", None, "lat", "lon", None),
        P("phase", None, None),
        P("phase", None, None),
        P("phase", None),
        P("phase", None, None),
        P("lat"),
    )
    out_specs = (P("phase", None, "lat", "lon", None), P("phase", "lat", "lon"))
    return jax.shard_map(
        per_device, mesh=mesh, in_specs=in_specs, out_specs=out_specs, check_vma=False
    )
```

```python
import functools

import jax
import jax.numpy as jnp
from jax import lax
from jax.experimental import pallas as pl
from jax.experimental.pallas import tpu as pltpu
from jax.sharding import PartitionSpec as P

F32 = jnp.float32
BF16 = jnp.bfloat16
HEADS = 8
FEATURES = 512
EPSILON = 1e-05
MASKED = -1e30
SCORE_SCALE = 0.125
VMEM_LIMIT = 8 * 1024 * 1024

LEVEL_ROWS = 96
ROWS = 192
PACKED_ROWS = 144


def call(kernel, out_shape, scratch=(), places=(), out_places=(), cost=None):
    def run(*args):
        places_of = dict(places)
        specs = [
            pl.BlockSpec(memory_space=places_of.get(i, pltpu.VMEM)) for i in range(len(args))
        ]
        outs_of = dict(out_places)
        outs = [
            pl.BlockSpec(memory_space=outs_of.get(i, pltpu.VMEM))
            for i in range(len(jax.tree.leaves(out_shape)))
        ]
        outs = tuple(outs) if isinstance(out_shape, tuple) else outs[0]
        return pl.pallas_call(
            kernel,
            out_shape=out_shape,
            in_specs=specs,
            out_specs=outs,
            scratch_shapes=list(scratch),
            cost_estimate=cost,
            compiler_params=pltpu.CompilerParams(vmem_limit_bytes=VMEM_LIMIT),
        )(*args)

    return run


def struct(shape, dtype):
    return jax.ShapeDtypeStruct(shape, dtype)


def dot(left, right, dims=((1,), (0,))):
    return lax.dot_general(left, right, (dims, ((), ())), preferred_element_type=F32)


def row_index(shape, dim):
    return lax.broadcasted_iota(jnp.int32, shape, dim)


def cut_kernel(labels_ref, x_ref, g_ref, own, lon, lat, cor, labels, sem):
    fetch = pltpu.make_async_copy(labels_ref, labels, sem)
    fetch.start()
    fetch.wait()
    row = row_index((8, FEATURES), 0)

    def halves(ref, level, i, fill):
        low = ref[0, level, i, 0:8, :].astype(F32)
        high = ref[0, level, i, 4:12, :].astype(F32)
        return (
            jnp.where(row < 6, low, fill),
            jnp.where(row < 6, pltpu.roll(high, 6, 0), fill),
        )

    for level in range(2):
        for i in range(6):
            label = labels[i].astype(F32)
            x_low, x_high = halves(x_ref, level, i, label)
            g_low, g_high = halves(g_ref, level, i, 0.0)
            low = jnp.concatenate([x_low, g_low], axis=0).astype(BF16)
            high = jnp.concatenate([x_high, g_high], axis=0).astype(BF16)
            if i < 3:
                cor[level, i] = low
                lat[level, i] = high
            else:
                lon[level, i - 3] = low
                own[level, i - 3] = high


def bias_kernel(table, out):
    parts = []
    for h in range(HEADS):
        line = jnp.broadcast_to(table[h : h + 1, :], (8, 256))
        parts.append(pltpu.roll(line, 0, 1, stride=1, stride_axis=0))
        parts.append(pltpu.roll(line, 6, 1, stride=1, stride_axis=0))
    shifted = jnp.concatenate(parts, axis=0)
    source = row_index((256, 256), 0)
    lane = row_index((256, 256), 1)
    column = lane & 7
    target = (lane >> 4) * 23 + ((lane >> 3) & 1) * 6 + column + 11
    picked = jnp.where((source == target) & (column < 6), 1.0, 0.0).astype(BF16)
    first = shifted.astype(BF16)
    rest = shifted - first.astype(F32)
    second = rest.astype(BF16)
    third = (rest - second.astype(F32)).astype(BF16)
    spread = dot(first, picked) + dot(second, picked) + dot(third, picked)
    empty = (row_index((128, 128), 0) & 7) >= 6
    for b in range(6):
        shift = (256 - (5 - b) * 16) % 256
        moved = spread if shift == 0 else pltpu.roll(spread, shift, 1)
        moved = jnp.where(empty, MASKED, moved[:, :128])
        for h in range(HEADS):
            out[h * 96 + b * 16 : h * 96 + b * 16 + 16, :] = moved[h * 16 : h * 16 + 16, :]


def pack_rows(array):
    columns = array.shape[1]
    groups = array.reshape(6, 4, 8, columns)
    row = row_index((8, columns), 0)
    out = []
    for q in range(6):
        last = groups[q, 3]
        for g in range(3):
            out.append(jnp.where(row < 6, groups[q, g], pltpu.roll(last, 6 - 2 * g, 0)))
    return jnp.concatenate(out, axis=0)


def per_head(pair):
    even = row_index(pair.shape, 1) < 64
    wide = pair.astype(F32)
    return jnp.concatenate(
        [jnp.where(even, wide, 0.0).astype(BF16), jnp.where(even, 0.0, wide).astype(BF16)], axis=0
    )


def attention_backward(att, d_low, projected, dqkv):
    lane = row_index((LEVEL_ROWS, 128), 1)
    for level in range(2):
        rows = slice(level * LEVEL_ROWS, (level + 1) * LEVEL_ROWS)
        for pair in range(4):
            cols = slice(pair * 128, (pair + 1) * 128)
            probs = att(level, pair)
            probs_low = probs.astype(BF16).reshape(2 * LEVEL_ROWS, LEVEL_ROWS)
            d_out = d_low[rows, cols]
            query = projected[rows, cols]
            keys = per_head(projected[rows, 512 + pair * 128 : 512 + (pair + 1) * 128])
            values = per_head(projected[rows, 1024 + pair * 128 : 1024 + (pair + 1) * 128])
            d_probs = dot(values, d_out, ((1,), (1,))).reshape(2, LEVEL_ROWS, LEVEL_ROWS)
            inner = jnp.sum(probs * d_probs, axis=1, keepdims=True)
            d_scores = (probs * (d_probs - inner)).astype(BF16).reshape(2 * LEVEL_ROWS, LEVEL_ROWS)
            d_value = dot(probs_low, d_out)
            d_key = dot(d_scores, query)
            d_query = dot(d_scores, keys, ((0,), (0,)))
            dqkv[rows, pair * 128 : (pair + 1) * 128] = d_query * SCORE_SCALE
            dqkv[rows, 512 + pair * 128 : 512 + (pair + 1) * 128] = (
                jnp.where(lane < 64, d_key[:LEVEL_ROWS], d_key[LEVEL_ROWS:]) * SCORE_SCALE
            )
            dqkv[rows, 1024 + pair * 128 : 1024 + (pair + 1) * 128] = jnp.where(
                lane < 64, d_value[:LEVEL_ROWS], d_value[LEVEL_ROWS:]
            )


def input_gradient(dqkv, w_qkv, gain, normed, inv_std):
    d_normed = dot(dqkv[...].astype(BF16), w_qkv[...]) * gain[...]
    mean_plain = jnp.mean(d_normed, axis=-1, keepdims=True)
    mean_normed = jnp.mean(d_normed * normed, axis=-1, keepdims=True)
    return inv_std * (d_normed - mean_plain - normed * mean_normed)


def normalised(x):
    center = jnp.mean(x, axis=-1, keepdims=True)
    moved = x - center
    spread = jnp.mean(jnp.square(moved), axis=-1, keepdims=True)
    inv_std = lax.rsqrt(spread + EPSILON)
    return moved * inv_std, inv_std


def first_kernel(
    own, lon, lat, cor, w_qkv, w_proj, gain, bias,
    skip, packed, fields, projected_out, att_out,
    dqkv,
):
    tiles_x, tiles_g = [], []
    labels = []
    row = row_index((8, FEATURES), 0)
    for level in range(2):
        for i in range(6):
            left, right = (own, lon) if i < 3 else (lat, cor)
            left, right = left[level, i % 3].astype(F32), right[level, i % 3].astype(F32)
            if level == 0:
                labels.append(left[6:7, :128])
            for tile in (left, right):
                tiles_x.append(jnp.where(row < 6, tile[:8], 0.0))
                tiles_g.append(tile[8:])
    x = jnp.concatenate(tiles_x, axis=0)
    c = jnp.concatenate(tiles_g, axis=0)
    normed, inv_std = normalised(x)
    scaled = normed * gain[...]
    packed[...] = pack_rows(scaled).astype(BF16)
    projected = dot(scaled.astype(BF16), w_qkv[...], ((1,), (1,)))
    c_low = c.astype(BF16)
    d_first_value = dot(c_low, w_proj[...])
    fields[0] = x.astype(BF16)
    fields[1] = c_low
    projected_out[...] = projected.astype(BF16)

    lane_row = row_index((1, 128), 1) >> 4
    along = labels[0]
    for b in range(1, 6):
        along = jnp.where(lane_row == b, labels[b], along)
    allowed = jnp.concatenate(
        [
            jnp.broadcast_to(jnp.where(labels[b] == along, 0.0, MASKED), (16, 128))
            for b in range(6)
        ],
        axis=0,
    )

    def probabilities(level, pair):
        rows = slice(level * LEVEL_ROWS, (level + 1) * LEVEL_ROWS)
        cols = slice(pair * 128, (pair + 1) * 128)
        added = bias[pair * 192 : (pair + 1) * 192, :].reshape(2, LEVEL_ROWS, 128) + allowed[None]
        keys = per_head(projected_out[rows, 512 + pair * 128 : 512 + (pair + 1) * 128])
        scores = dot(keys, projected_out[rows, cols], ((1,), (1,))).reshape(2, LEVEL_ROWS, LEVEL_ROWS)
        scores = scores * SCORE_SCALE + added[:, :, :LEVEL_ROWS]
        weights = jnp.exp(scores - jnp.max(scores, axis=1, keepdims=True))
        probs = weights * (1.0 / jnp.sum(weights, axis=1, keepdims=True))
        att_out[level, pair] = probs.astype(BF16)
        return probs

    attention_backward(probabilities, d_first_value.astype(BF16), projected_out, dqkv)
    skip[...] = (c + input_gradient(dqkv, w_qkv, gain, normed, inv_std)).astype(BF16)


def second_kernel(
    core, arrived, fields, projected, att, w_proj, w_qkv, gain,
    kept, sent, own, lon, lat, cor, dqkv,
):
    d_low = (dot(fields[1], w_proj[...]) + dot(arrived[...], w_proj[...])).astype(BF16)
    attention_backward(lambda level, pair: att[level, pair].astype(F32), d_low, projected, dqkv)
    lane = row_index((PACKED_ROWS, 128), 1)
    halves = []
    for t in range(4):
        first, middle, last = (
            pack_rows(dqkv[:, 384 * t + 128 * j : 384 * t + 128 * (j + 1)]) for j in range(3)
        )
        halves.append(middle)
        cols = slice(128 * t, 128 * (t + 1))

        @pl.when(core[0] == 0)
        def _():
            kept[:, cols] = first.astype(BF16)
            sent[:, cols] = last.astype(BF16)

        @pl.when(core[0] == 1)
        def _():
            kept[:, cols] = last.astype(BF16)
            sent[:, cols] = first.astype(BF16)

    for t in range(2):
        left, right = halves[2 * t], halves[2 * t + 1]
        first = jnp.where(lane < 64, left, pltpu.roll(right, 64, 1)).astype(BF16)
        last = jnp.where(lane < 64, pltpu.roll(left, 64, 1), right).astype(BF16)
        cols = slice(512 + 128 * t, 512 + 128 * (t + 1))

        @pl.when(core[0] == 0)
        def _():
            kept[:, cols] = first
            sent[:, cols] = last

        @pl.when(core[0] == 1)
        def _():
            kept[:, cols] = last
            sent[:, cols] = first

    normed, inv_std = normalised(fields[0].astype(F32))
    shifted = input_gradient(dqkv, w_qkv, gain, normed, inv_std)
    total = fields[1].astype(F32) + (arrived[...].astype(F32) + shifted)
    for i in range(6):
        for half in range(2):
            start = 16 * i + 8 * half
            both = jnp.concatenate(
                [total[start : start + 8], total[96 + start : 96 + start + 8]], axis=0
            )
            target = ((own, lon), (lat, cor))[i // 3][half]
            target[i % 3] = both.astype(BF16)


def product_kernel(kept, got, inputs, other_inputs, out):
    product = dot(inputs[...], kept[...], ((0,), (0,)))
    product = product + dot(other_inputs[...], got[...], ((0,), (0,)))
    bands = out.shape[1]
    width = FEATURES // bands
    lane = row_index((bands, width // 2, 128), 2)
    for t in range(4):
        whole = product[:, 128 * t : 128 * (t + 1)].reshape(bands, width, 128)
        out[t, :, :width, :] = whole.astype(BF16)
        start = 512 + 128 * (t // 2)
        half = product[:, start : start + 128].reshape(bands, width, 128)
        top, bottom = half[:, : width // 2], half[:, width // 2 :]
        if t % 2 == 0:
            folded = jnp.where(lane < 64, top, pltpu.roll(bottom, 64, 2))
        else:
            folded = jnp.where(lane < 64, pltpu.roll(top, 64, 2), bottom)
        out[t, :, width:, :] = folded.astype(BF16)


def chips_kernel(products, own, lon, lat, cor, out, joined):
    total = products[0].astype(F32)
    for t in range(1, products.shape[0]):
        total = total + products[t].astype(F32)
    out[...] = total.astype(BF16)
    join(own, lon, lat, cor, joined)


def sum_kernel(odd, parts, out):
    bands, rows, _ = parts.shape
    width = rows * 2 // 3
    total = parts[0].astype(F32)
    for band in range(1, bands):
        total = total + parts[band].astype(F32)
    whole = total[:width]
    folded = total[width:]
    half = jnp.concatenate([folded, pltpu.roll(folded, 64, 1)], axis=0)
    half = half[:, :64]

    @pl.when(odd[0] == 0)
    def _():
        out[0, :, :128] = whole
        out[0, :, 128:] = half

    @pl.when(odd[0] == 1)
    def _():
        out[0, :, :64] = half
        out[0, :, 64:] = whole


def join(own, lon, lat, cor, out):
    row = row_index((8, FEATURES), 0)
    for level in range(2):
        part = slice(level * 8, level * 8 + 8)
        for i in range(6):
            left, right = (cor, lat) if i < 3 else (lon, own)
            left = left[i % 3].astype(F32)[part]
            right = pltpu.roll(right[i % 3].astype(F32)[part], 6, 0)
            out[0, level, i, 0:8, :] = jnp.where(row < 6, left, right).astype(BF16)
            out[0, level, i, 8:12, :] = right[:4].astype(BF16)


def passed(array, lat_by, lon_by):
    lats, lons = lax.axis_size("lat"), lax.axis_size("lon")
    pairs = [
        (a * lons + o, ((a + lat_by) % lats) * lons + (o + lon_by) % lons)
        for a in range(lats)
        for o in range(lons)
    ]
    return lax.ppermute(array, ("lat", "lon"), pairs)


def other_core(array):
    return lax.ppermute(array, "lat", [(a, a ^ 1) for a in range(lax.axis_size("lat"))])


def per_device(x_in, out_grad, w_qkv, w_proj, norm_gain, bias_table, lat_labels):
    lats, lons = lax.axis_size("lat"), lax.axis_size("lon")
    w_qkv, w_proj = w_qkv[0], w_proj[0]
    piece = struct((2, 3, 16, FEATURES), BF16)
    own, lon, lat, cor = call(
        cut_kernel,
        (piece,) * 4,
        [pltpu.SMEM(lat_labels.shape, jnp.int32), pltpu.SemaphoreType.DMA],
        places={0: pl.ANY},
    )(lat_labels, x_in, out_grad)
    lon = passed(lon, 0, -1)
    lat = passed(lat, -1, 0)
    cor = passed(cor, -1, -1)
    table = jnp.pad(bias_table[0, :, 253:506], ((0, 0), (0, 3)))
    bias = call(
        bias_kernel,
        struct((HEADS * LEVEL_ROWS, 128), F32),
        cost=pl.CostEstimate(flops=4_000_000_000, bytes_accessed=20_000_000, transcendentals=0),
    )(table)

    window = struct((ROWS, FEATURES), BF16)
    scratch = [pltpu.VMEM((ROWS, 3 * FEATURES), F32)]
    skip, packed, fields, projected, att = call(
        first_kernel,
        (
            window,
            struct((PACKED_ROWS, FEATURES), BF16),
            struct((2, ROWS, FEATURES), BF16),
            struct((ROWS, 3 * FEATURES), BF16),
            struct((2, 4, 2, LEVEL_ROWS, LEVEL_ROWS), BF16),
        ),
        scratch,
    )(own, lon, lat, cor, w_qkv, w_proj, norm_gain, bias)

    core = (lax.axis_index("lat") % 2).astype(jnp.int32).reshape(1)
    arrived = lax.ppermute(skip, "phase", [(1, 0)])
    other_packed = other_core(packed)
    back = struct((3, 16, FEATURES), BF16)
    half = struct((PACKED_ROWS, 768), BF16)
    kept, sent, own, lon, lat, cor = call(
        second_kernel,
        (half, half, back, back, back, back),
        scratch,
        places={0: pltpu.SMEM},
    )(core, arrived, fields, projected, att, w_proj, w_qkv, norm_gain)
    got = other_core(sent)
    lon = passed(lon, 0, 1)
    lat = passed(lat, 1, 0)
    cor = passed(cor, 1, 1)
    rows = FEATURES * 3 // 2 // lons
    products = call(product_kernel, struct((lats // 2, lons, rows, 128), BF16))(
        kept, got, packed, other_packed
    )
    chips = [[2 * x + c for x in range(lats // 2)] for c in range(2)]
    products = lax.all_to_all(products, "lat", 0, 0, tiled=True, axis_index_groups=chips)
    slices, grad_input = call(
        chips_kernel,
        (struct((lons, rows, 128), BF16), struct((1, 2, 6, 12, FEATURES), BF16)),
    )(products, own, lon, lat, cor)
    slices = lax.all_to_all(slices, "lon", 0, 0, tiled=True)
    grad_qkv = call(
        sum_kernel, struct((1, FEATURES // lons, 192), F32), places={0: pltpu.SMEM}
    )(core, slices)
    return grad_input, grad_qkv.transpose(0, 2, 1)


def solution(mesh):
    in_specs = (
        P("phase", None, "lat", "lon", None),
        P("phase", None, "lat", "lon", None),
        P("phase", None, None),
        P("phase", None, None),
        P("phase", None),
        P("phase", None, None),
        P("lat"),
    )
    out_specs = (P("phase", None, "lat", "lon", None), P("phase", "lat", "lon"))
    return jax.shard_map(
        per_device, mesh=mesh, in_specs=in_specs, out_specs=out_specs, check_vma=False
    )
```

```python
import functools

import jax
import jax.numpy as jnp
from jax import lax
from jax.experimental import pallas as pl
from jax.experimental.pallas import tpu as pltpu
from jax.sharding import PartitionSpec as P

F32 = jnp.float32
BF16 = jnp.bfloat16
HEADS = 8
FEATURES = 512
EPSILON = 1e-05
MASKED = -1e30
SCORE_SCALE = 0.125
VMEM_LIMIT = 8 * 1024 * 1024

LEVEL_ROWS = 96
ROWS = 192
PACKED_ROWS = 144


def call(kernel, out_shape, scratch=(), places=(), out_places=(), cost=None):
    def run(*args):
        places_of = dict(places)
        specs = [
            pl.BlockSpec(memory_space=places_of.get(i, pltpu.VMEM)) for i in range(len(args))
        ]
        outs_of = dict(out_places)
        outs = [
            pl.BlockSpec(memory_space=outs_of.get(i, pltpu.VMEM))
            for i in range(len(jax.tree.leaves(out_shape)))
        ]
        outs = tuple(outs) if isinstance(out_shape, tuple) else outs[0]
        return pl.pallas_call(
            kernel,
            out_shape=out_shape,
            in_specs=specs,
            out_specs=outs,
            scratch_shapes=list(scratch),
            cost_estimate=cost,
            compiler_params=pltpu.CompilerParams(vmem_limit_bytes=VMEM_LIMIT),
        )(*args)

    return run


def struct(shape, dtype):
    return jax.ShapeDtypeStruct(shape, dtype)


def dot(left, right, dims=((1,), (0,))):
    return lax.dot_general(left, right, (dims, ((), ())), preferred_element_type=F32)


def row_index(shape, dim):
    return lax.broadcasted_iota(jnp.int32, shape, dim)


def cut_kernel(labels_ref, x_ref, g_ref, own, lon, lat, cor, labels, sem):
    fetch = pltpu.make_async_copy(labels_ref, labels, sem)
    fetch.start()
    fetch.wait()
    row = row_index((8, FEATURES), 0)

    def halves(ref, level, i, fill):
        low = ref[0, level, i, 0:8, :].astype(F32)
        high = ref[0, level, i, 4:12, :].astype(F32)
        return (
            jnp.where(row < 6, low, fill),
            jnp.where(row < 6, pltpu.roll(high, 6, 0), fill),
        )

    for level in range(2):
        for i in range(6):
            label = labels[i].astype(F32)
            x_low, x_high = halves(x_ref, level, i, label)
            g_low, g_high = halves(g_ref, level, i, 0.0)
            low = jnp.concatenate([x_low, g_low], axis=0).astype(BF16)
            high = jnp.concatenate([x_high, g_high], axis=0).astype(BF16)
            if i < 3:
                cor[level, i] = low
                lat[level, i] = high
            else:
                lon[level, i - 3] = low
                own[level, i - 3] = high


def bias_kernel(table, out):
    parts = []
    for h in range(HEADS):
        line = jnp.broadcast_to(table[h : h + 1, :], (8, 256))
        parts.append(pltpu.roll(line, 0, 1, stride=1, stride_axis=0))
        parts.append(pltpu.roll(line, 6, 1, stride=1, stride_axis=0))
    shifted = jnp.concatenate(parts, axis=0)
    source = row_index((256, 256), 0)
    lane = row_index((256, 256), 1)
    column = lane & 7
    target = (lane >> 4) * 23 + ((lane >> 3) & 1) * 6 + column + 11
    picked = jnp.where((source == target) & (column < 6), 1.0, 0.0).astype(BF16)
    first = shifted.astype(BF16)
    rest = shifted - first.astype(F32)
    second = rest.astype(BF16)
    third = (rest - second.astype(F32)).astype(BF16)
    spread = dot(first, picked) + dot(second, picked) + dot(third, picked)
    empty = (row_index((128, 128), 0) & 7) >= 6
    for b in range(6):
        shift = (256 - (5 - b) * 16) % 256
        moved = spread if shift == 0 else pltpu.roll(spread, shift, 1)
        moved = jnp.where(empty, MASKED, moved[:, :128])
        for h in range(HEADS):
            out[h * 96 + b * 16 : h * 96 + b * 16 + 16, :] = moved[h * 16 : h * 16 + 16, :]


def pack_rows(array):
    columns = array.shape[1]
    groups = array.reshape(6, 4, 8, columns)
    row = row_index((8, columns), 0)
    out = []
    for q in range(6):
        last = groups[q, 3]
        for g in range(3):
            out.append(jnp.where(row < 6, groups[q, g], pltpu.roll(last, 6 - 2 * g, 0)))
    return jnp.concatenate(out, axis=0)


def unpack_rows(array):
    columns = array.shape[1]
    groups = array.reshape(6, 3, 8, columns)
    row = row_index((8, columns), 0)
    out = []
    for q in range(6):
        for g in range(3):
            out.append(jnp.where(row < 6, groups[q, g], 0.0))
        last = jnp.where(row < 2, pltpu.roll(groups[q, 0], 2, 0), 0.0)
        last = jnp.where((row >= 2) & (row < 4), pltpu.roll(groups[q, 1], 4, 0), last)
        last = jnp.where((row >= 4) & (row < 6), pltpu.roll(groups[q, 2], 6, 0), last)
        out.append(last)
    return jnp.concatenate(out, axis=0)


def per_head(pair):
    even = row_index(pair.shape, 1) < 64
    wide = pair.astype(F32)
    return jnp.concatenate(
        [jnp.where(even, wide, 0.0).astype(BF16), jnp.where(even, 0.0, wide).astype(BF16)], axis=0
    )


def attention_backward(att, d_low, projected, dqkv):
    lane = row_index((LEVEL_ROWS, 128), 1)
    for level in range(2):
        rows = slice(level * LEVEL_ROWS, (level + 1) * LEVEL_ROWS)
        for pair in range(4):
            cols = slice(pair * 128, (pair + 1) * 128)
            probs = att(level, pair)
            probs_low = probs.astype(BF16).reshape(2 * LEVEL_ROWS, LEVEL_ROWS)
            d_out = d_low[rows, cols]
            query = projected[rows, cols]
            keys = per_head(projected[rows, 512 + pair * 128 : 512 + (pair + 1) * 128])
            values = per_head(projected[rows, 1024 + pair * 128 : 1024 + (pair + 1) * 128])
            d_probs = dot(values, d_out, ((1,), (1,))).reshape(2, LEVEL_ROWS, LEVEL_ROWS)
            inner = jnp.sum(probs * d_probs, axis=1, keepdims=True)
            d_scores = (probs * (d_probs - inner)).astype(BF16).reshape(2 * LEVEL_ROWS, LEVEL_ROWS)
            d_value = dot(probs_low, d_out)
            d_key = dot(d_scores, query)
            d_query = dot(d_scores, keys, ((0,), (0,)))
            dqkv[rows, pair * 128 : (pair + 1) * 128] = d_query * SCORE_SCALE
            dqkv[rows, 512 + pair * 128 : 512 + (pair + 1) * 128] = (
                jnp.where(lane < 64, d_key[:LEVEL_ROWS], d_key[LEVEL_ROWS:]) * SCORE_SCALE
            )
            dqkv[rows, 1024 + pair * 128 : 1024 + (pair + 1) * 128] = jnp.where(
                lane < 64, d_value[:LEVEL_ROWS], d_value[LEVEL_ROWS:]
            )


def input_gradient(dqkv, w_qkv, gain, normed, inv_std):
    d_normed = dot(dqkv[...].astype(BF16), w_qkv[...]) * gain[...]
    mean_plain = jnp.mean(d_normed, axis=-1, keepdims=True)
    mean_normed = jnp.mean(d_normed * normed, axis=-1, keepdims=True)
    return inv_std * (d_normed - mean_plain - normed * mean_normed)


def normalised(x):
    center = jnp.mean(x, axis=-1, keepdims=True)
    moved = x - center
    spread = jnp.mean(jnp.square(moved), axis=-1, keepdims=True)
    inv_std = lax.rsqrt(spread + EPSILON)
    return moved * inv_std, inv_std


def first_kernel(
    own, lon, lat, cor, w_qkv, w_proj, gain, bias,
    skip, packed, fields, projected_out, att_out,
    dqkv,
):
    tiles_x, tiles_g = [], []
    labels = []
    row = row_index((8, FEATURES), 0)
    for level in range(2):
        for i in range(6):
            left, right = (own, lon) if i < 3 else (lat, cor)
            left, right = left[level, i % 3].astype(F32), right[level, i % 3].astype(F32)
            if level == 0:
                labels.append(left[6:7, :128])
            for tile in (left, right):
                tiles_x.append(jnp.where(row < 6, tile[:8], 0.0))
                tiles_g.append(tile[8:])
    x = jnp.concatenate(tiles_x, axis=0)
    c = jnp.concatenate(tiles_g, axis=0)
    normed, inv_std = normalised(x)
    scaled = normed * gain[...]
    packed[...] = pack_rows(scaled).astype(BF16)
    projected = dot(scaled.astype(BF16), w_qkv[...], ((1,), (1,)))
    c_low = c.astype(BF16)
    d_first_value = dot(c_low, w_proj[...])
    fields[0] = x.astype(BF16)
    fields[1] = c_low
    projected_out[...] = projected.astype(BF16)

    lane_row = row_index((1, 128), 1) >> 4
    along = labels[0]
    for b in range(1, 6):
        along = jnp.where(lane_row == b, labels[b], along)
    allowed = jnp.concatenate(
        [
            jnp.broadcast_to(jnp.where(labels[b] == along, 0.0, MASKED), (16, 128))
            for b in range(6)
        ],
        axis=0,
    )

    def probabilities(level, pair):
        rows = slice(level * LEVEL_ROWS, (level + 1) * LEVEL_ROWS)
        cols = slice(pair * 128, (pair + 1) * 128)
        added = bias[pair * 192 : (pair + 1) * 192, :].reshape(2, LEVEL_ROWS, 128) + allowed[None]
        keys = per_head(projected_out[rows, 512 + pair * 128 : 512 + (pair + 1) * 128])
        scores = dot(keys, projected_out[rows, cols], ((1,), (1,))).reshape(2, LEVEL_ROWS, LEVEL_ROWS)
        scores = scores * SCORE_SCALE + added[:, :, :LEVEL_ROWS]
        weights = jnp.exp(scores - jnp.max(scores, axis=1, keepdims=True))
        probs = weights * (1.0 / jnp.sum(weights, axis=1, keepdims=True))
        att_out[level, pair] = probs.astype(BF16)
        return probs

    attention_backward(probabilities, d_first_value.astype(BF16), projected_out, dqkv)
    skip[...] = pack_rows(c + input_gradient(dqkv, w_qkv, gain, normed, inv_std)).astype(BF16)


def second_kernel(
    core, arrived, fields, projected, att, w_proj, w_qkv, gain,
    kept, sent, near, far, dqkv,
):
    c2 = unpack_rows(arrived[...].astype(F32))
    d_low = (dot(fields[1], w_proj[...]) + dot(c2.astype(BF16), w_proj[...])).astype(BF16)
    attention_backward(lambda level, pair: att[level, pair].astype(F32), d_low, projected, dqkv)
    lane = row_index((PACKED_ROWS, 128), 1)
    is_first = core[0] == 0
    halves = []

    def share(cols, first, last):
        kept[:, cols] = jnp.where(is_first, first, last).astype(BF16)
        sent[:, cols] = jnp.where(is_first, last, first).astype(BF16)

    for t in range(4):
        first, middle, last = (
            pack_rows(dqkv[:, 384 * t + 128 * j : 384 * t + 128 * (j + 1)]) for j in range(3)
        )
        halves.append(middle)
        share(slice(128 * t, 128 * (t + 1)), first, last)
    for t in range(2):
        left, right = halves[2 * t], halves[2 * t + 1]
        first = jnp.where(lane < 64, left, pltpu.roll(right, 64, 1))
        last = jnp.where(lane < 64, pltpu.roll(left, 64, 1), right)
        share(slice(512 + 128 * t, 512 + 128 * (t + 1)), first, last)

    normed, inv_std = normalised(fields[0].astype(F32))
    shifted = input_gradient(dqkv, w_qkv, gain, normed, inv_std)
    total = fields[1].astype(F32) + (c2 + shifted)
    for i in range(6):
        for half, target in ((0, near), (1, far)):
            start = 16 * i + 8 * half
            both = jnp.concatenate(
                [total[start : start + 8], total[96 + start : 96 + start + 8]], axis=0
            )
            target[i] = both.astype(BF16)


def turn_kernel(inputs, other_inputs, out):
    out[0] = inputs[...].astype(F32).T.astype(BF16)
    out[1] = other_inputs[...].astype(F32).T.astype(BF16)


def product_kernel(kept, got, inputs, out):
    product = dot(inputs[0], kept[...]) + dot(inputs[1], got[...])
    bands = out.shape[1]
    width = FEATURES // bands
    lane = row_index((bands, width // 2, 128), 2)
    for t in range(4):
        whole = product[:, 128 * t : 128 * (t + 1)].reshape(bands, width, 128)
        out[t, :, :width, :] = whole.astype(BF16)
        start = 512 + 128 * (t // 2)
        half = product[:, start : start + 128].reshape(bands, width, 128)
        top, bottom = half[:, : width // 2], half[:, width // 2 :]
        if t % 2 == 0:
            folded = jnp.where(lane < 64, top, pltpu.roll(bottom, 64, 2))
        else:
            folded = jnp.where(lane < 64, pltpu.roll(top, 64, 2), bottom)
        out[t, :, width:, :] = folded.astype(BF16)


def upward_kernel(near, left, out):
    for i in range(3):
        out[0, i] = left[3 + i]
        out[1, i] = near[3 + i]


def sum_kernel(odd, parts, out):
    bands, rows, _ = parts.shape
    width = rows * 2 // 3
    total = parts[0].astype(F32)
    for band in range(1, bands):
        total = total + parts[band].astype(F32)
    whole = total[:width]
    folded = total[width:]
    half = jnp.concatenate([folded, pltpu.roll(folded, 64, 1)], axis=0)
    half = half[:, :64]

    @pl.when(odd[0] == 0)
    def _():
        out[0, :, :128] = whole
        out[0, :, 128:] = half

    @pl.when(odd[0] == 1)
    def _():
        out[0, :, :64] = half
        out[0, :, 64:] = whole


def join_kernel(near, left, arrived, out):
    row = row_index((8, FEATURES), 0)
    for level in range(2):
        part = slice(level * 8, level * 8 + 8)
        for i in range(6):
            low, high = (arrived[0, i], arrived[1, i]) if i < 3 else (left[i - 3], near[i - 3])
            low = low.astype(F32)[part]
            high = pltpu.roll(high.astype(F32)[part], 6, 0)
            out[0, level, i, 0:8, :] = jnp.where(row < 6, low, high).astype(BF16)
            out[0, level, i, 8:12, :] = high[:4].astype(BF16)


def passed(array, lat_by, lon_by):
    lats, lons = lax.axis_size("lat"), lax.axis_size("lon")
    pairs = [
        (a * lons + o, ((a + lat_by) % lats) * lons + (o + lon_by) % lons)
        for a in range(lats)
        for o in range(lons)
    ]
    return lax.ppermute(array, ("lat", "lon"), pairs)


def other_core(array):
    return lax.ppermute(array, "lat", [(a, a ^ 1) for a in range(lax.axis_size("lat"))])


def per_device(x_in, out_grad, w_qkv, w_proj, norm_gain, bias_table, lat_labels):
    lats, lons = lax.axis_size("lat"), lax.axis_size("lon")
    w_qkv, w_proj = w_qkv[0], w_proj[0]
    piece = struct((2, 3, 16, FEATURES), BF16)
    own, lon, lat, cor = call(
        cut_kernel,
        (piece,) * 4,
        [pltpu.SMEM(lat_labels.shape, jnp.int32), pltpu.SemaphoreType.DMA],
        places={0: pl.ANY},
    )(lat_labels, x_in, out_grad)
    lon = passed(lon, 0, -1)
    lat = passed(lat, -1, 0)
    cor = passed(cor, -1, -1)
    table = jnp.pad(bias_table[0, :, 253:506], ((0, 0), (0, 3)))
    bias = call(
        bias_kernel,
        struct((HEADS * LEVEL_ROWS, 128), F32),
        cost=pl.CostEstimate(flops=4_000_000_000, bytes_accessed=20_000_000, transcendentals=0),
    )(table)

    scratch = [pltpu.VMEM((ROWS, 3 * FEATURES), F32)]
    skip, packed, fields, projected, att = call(
        first_kernel,
        (
            struct((PACKED_ROWS, FEATURES), BF16),
            struct((PACKED_ROWS, FEATURES), BF16),
            struct((2, ROWS, FEATURES), BF16),
            struct((ROWS, 3 * FEATURES), BF16),
            struct((2, 4, 2, LEVEL_ROWS, LEVEL_ROWS), BF16),
        ),
        scratch,
    )(own, lon, lat, cor, w_qkv, w_proj, norm_gain, bias)

    core = (lax.axis_index("lat") % 2).astype(jnp.int32).reshape(1)
    arrived = lax.ppermute(skip, "phase", [(1, 0)])
    turned = call(turn_kernel, struct((2, FEATURES, PACKED_ROWS), BF16))(
        packed, other_core(packed)
    )
    arrived, turned = lax.optimization_barrier((arrived, turned))
    back = struct((6, 16, FEATURES), BF16)
    half = struct((PACKED_ROWS, 768), BF16)
    kept, sent, near, far = call(
        second_kernel,
        (half, half, back, back),
        scratch,
        places={0: pltpu.SMEM},
    )(core, arrived, fields, projected, att, w_proj, w_qkv, norm_gain)
    got = other_core(sent)
    left = passed(far, 0, 1)
    rows = FEATURES * 3 // 2 // lons
    products = call(product_kernel, struct((lats // 2, lons, rows, 128), BF16))(
        kept, got, turned
    )
    upward = call(upward_kernel, struct((2, 3, 16, FEATURES), BF16))(near, left)
    above = passed(upward, 1, 0)
    grad_input = call(join_kernel, struct((1, 2, 6, 12, FEATURES), BF16))(near, left, above)
    same_core = [
        [(2 * x + c) * lons + o for x in range(lats // 2) for o in range(lons)] for c in range(2)
    ]
    slices = lax.all_to_all(
        products.reshape(lats // 2 * lons, rows, 128),
        ("lat", "lon"),
        0,
        0,
        tiled=True,
        axis_index_groups=same_core,
    )
    grad_qkv = call(
        sum_kernel, struct((1, FEATURES // lons, 192), F32), places={0: pltpu.SMEM}
    )(core, slices)
    return grad_input, grad_qkv.transpose(0, 2, 1)


def solution(mesh):
    in_specs = (
        P("phase", None, "lat", "lon", None),
        P("phase", None, "lat", "lon", None),
        P("phase", None, None),
        P("phase", None, None),
        P("phase", None),
        P("phase", None, None),
        P("lat"),
    )
    out_specs = (P("phase", None, "lat", "lon", None), P("phase", "lat", "lon"))
    return jax.shard_map(
        per_device, mesh=mesh, in_specs=in_specs, out_specs=out_specs, check_vma=False
    )
```

```python
import functools

import jax
import jax.numpy as jnp
from jax import lax
from jax.experimental import pallas as pl
from jax.experimental.pallas import tpu as pltpu
from jax.sharding import PartitionSpec as P

F32 = jnp.float32
BF16 = jnp.bfloat16
HEADS = 8
FEATURES = 512
EPSILON = 1e-05
MASKED = -1e30
SCORE_SCALE = 0.125
VMEM_LIMIT = 8 * 1024 * 1024

LEVEL_ROWS = 96
ROWS = 192
PACKED_ROWS = 144


def call(kernel, out_shape, scratch=(), places=(), out_places=(), cost=None):
    def run(*args):
        places_of = dict(places)
        specs = [
            pl.BlockSpec(memory_space=places_of.get(i, pltpu.VMEM)) for i in range(len(args))
        ]
        outs_of = dict(out_places)
        outs = [
            pl.BlockSpec(memory_space=outs_of.get(i, pltpu.VMEM))
            for i in range(len(jax.tree.leaves(out_shape)))
        ]
        outs = tuple(outs) if isinstance(out_shape, tuple) else outs[0]
        return pl.pallas_call(
            kernel,
            out_shape=out_shape,
            in_specs=specs,
            out_specs=outs,
            scratch_shapes=list(scratch),
            cost_estimate=cost,
            compiler_params=pltpu.CompilerParams(vmem_limit_bytes=VMEM_LIMIT),
        )(*args)

    return run


def struct(shape, dtype):
    return jax.ShapeDtypeStruct(shape, dtype)


def dot(left, right, dims=((1,), (0,))):
    return lax.dot_general(left, right, (dims, ((), ())), preferred_element_type=F32)


def row_index(shape, dim):
    return lax.broadcasted_iota(jnp.int32, shape, dim)


def cut_kernel(labels_ref, x_ref, g_ref, own, lon, lat, cor, labels, sem):
    fetch = pltpu.make_async_copy(labels_ref, labels, sem)
    fetch.start()
    fetch.wait()
    row = row_index((8, FEATURES), 0)

    def halves(ref, level, i, fill):
        low = ref[0, level, i, 0:8, :].astype(F32)
        high = ref[0, level, i, 4:12, :].astype(F32)
        return (
            jnp.where(row < 6, low, fill),
            jnp.where(row < 6, pltpu.roll(high, 6, 0), fill),
        )

    for level in range(2):
        for i in range(6):
            label = labels[i].astype(F32)
            x_low, x_high = halves(x_ref, level, i, label)
            g_low, g_high = halves(g_ref, level, i, 0.0)
            low = jnp.concatenate([x_low, g_low], axis=0).astype(BF16)
            high = jnp.concatenate([x_high, g_high], axis=0).astype(BF16)
            if i < 3:
                cor[level, i] = low
                lat[level, i] = high
            else:
                lon[level, i - 3] = low
                own[level, i - 3] = high


def bias_kernel(table, out):
    parts = []
    for h in range(HEADS):
        line = jnp.broadcast_to(table[h : h + 1, :], (8, 256))
        parts.append(pltpu.roll(line, 0, 1, stride=1, stride_axis=0))
        parts.append(pltpu.roll(line, 6, 1, stride=1, stride_axis=0))
    shifted = jnp.concatenate(parts, axis=0)
    source = row_index((256, 256), 0)
    lane = row_index((256, 256), 1)
    column = lane & 7
    target = (lane >> 4) * 23 + ((lane >> 3) & 1) * 6 + column + 11
    picked = jnp.where((source == target) & (column < 6), 1.0, 0.0).astype(BF16)
    first = shifted.astype(BF16)
    rest = shifted - first.astype(F32)
    second = rest.astype(BF16)
    third = (rest - second.astype(F32)).astype(BF16)
    spread = dot(first, picked) + dot(second, picked) + dot(third, picked)
    empty = (row_index((128, 128), 0) & 7) >= 6
    for b in range(6):
        shift = (256 - (5 - b) * 16) % 256
        moved = spread if shift == 0 else pltpu.roll(spread, shift, 1)
        moved = jnp.where(empty, MASKED, moved[:, :128])
        for h in range(HEADS):
            out[h * 96 + b * 16 : h * 96 + b * 16 + 16, :] = moved[h * 16 : h * 16 + 16, :]


def pack_rows(array):
    columns = array.shape[1]
    groups = array.reshape(6, 4, 8, columns)
    row = row_index((8, columns), 0)
    out = []
    for q in range(6):
        last = groups[q, 3]
        for g in range(3):
            out.append(jnp.where(row < 6, groups[q, g], pltpu.roll(last, 6 - 2 * g, 0)))
    return jnp.concatenate(out, axis=0)


def unpack_rows(array):
    columns = array.shape[1]
    groups = array.reshape(6, 3, 8, columns)
    row = row_index((8, columns), 0)
    out = []
    for q in range(6):
        for g in range(3):
            out.append(jnp.where(row < 6, groups[q, g], 0.0))
        last = jnp.where(row < 2, pltpu.roll(groups[q, 0], 2, 0), 0.0)
        last = jnp.where((row >= 2) & (row < 4), pltpu.roll(groups[q, 1], 4, 0), last)
        last = jnp.where((row >= 4) & (row < 6), pltpu.roll(groups[q, 2], 6, 0), last)
        out.append(last)
    return jnp.concatenate(out, axis=0)


def per_head(pair):
    even = row_index(pair.shape, 1) < 64
    wide = pair.astype(F32)
    return jnp.concatenate(
        [jnp.where(even, wide, 0.0).astype(BF16), jnp.where(even, 0.0, wide).astype(BF16)], axis=0
    )


def attention_backward(att, d_low, projected, dqkv):
    lane = row_index((LEVEL_ROWS, 128), 1)
    for level in range(2):
        rows = slice(level * LEVEL_ROWS, (level + 1) * LEVEL_ROWS)
        for pair in range(4):
            cols = slice(pair * 128, (pair + 1) * 128)
            probs = att(level, pair)
            probs_low = probs.astype(BF16).reshape(2 * LEVEL_ROWS, LEVEL_ROWS)
            d_out = d_low[rows, cols]
            query = projected[rows, cols]
            keys = per_head(projected[rows, 512 + pair * 128 : 512 + (pair + 1) * 128])
            values = per_head(projected[rows, 1024 + pair * 128 : 1024 + (pair + 1) * 128])
            d_probs = dot(values, d_out, ((1,), (1,))).reshape(2, LEVEL_ROWS, LEVEL_ROWS)
            inner = jnp.sum(probs * d_probs, axis=1, keepdims=True)
            d_scores = (probs * (d_probs - inner)).astype(BF16).reshape(2 * LEVEL_ROWS, LEVEL_ROWS)
            d_value = dot(probs_low, d_out)
            d_key = dot(d_scores, query)
            d_query = dot(d_scores, keys, ((0,), (0,)))
            dqkv[rows, pair * 128 : (pair + 1) * 128] = d_query * SCORE_SCALE
            dqkv[rows, 512 + pair * 128 : 512 + (pair + 1) * 128] = (
                jnp.where(lane < 64, d_key[:LEVEL_ROWS], d_key[LEVEL_ROWS:]) * SCORE_SCALE
            )
            dqkv[rows, 1024 + pair * 128 : 1024 + (pair + 1) * 128] = jnp.where(
                lane < 64, d_value[:LEVEL_ROWS], d_value[LEVEL_ROWS:]
            )


def input_gradient(dqkv, w_qkv, gain, normed, inv_std):
    d_normed = dot(dqkv[...].astype(BF16), w_qkv[...]) * gain[...]
    mean_plain = jnp.mean(d_normed, axis=-1, keepdims=True)
    mean_normed = jnp.mean(d_normed * normed, axis=-1, keepdims=True)
    return inv_std * (d_normed - mean_plain - normed * mean_normed)


def normalised(x):
    center = jnp.mean(x, axis=-1, keepdims=True)
    moved = x - center
    spread = jnp.mean(jnp.square(moved), axis=-1, keepdims=True)
    inv_std = lax.rsqrt(spread + EPSILON)
    return moved * inv_std, inv_std


def first_kernel(
    own, lon, lat, cor, w_qkv, w_proj, gain, bias,
    skip, packed, fields, projected_out, att_out,
    dqkv,
):
    tiles_x, tiles_g = [], []
    labels = []
    row = row_index((8, FEATURES), 0)
    for level in range(2):
        for i in range(6):
            left, right = (own, lon) if i < 3 else (lat, cor)
            left, right = left[level, i % 3].astype(F32), right[level, i % 3].astype(F32)
            if level == 0:
                labels.append(left[6:7, :128])
            for tile in (left, right):
                tiles_x.append(jnp.where(row < 6, tile[:8], 0.0))
                tiles_g.append(tile[8:])
    x = jnp.concatenate(tiles_x, axis=0)
    c = jnp.concatenate(tiles_g, axis=0)
    normed, inv_std = normalised(x)
    scaled = normed * gain[...]
    packed[...] = pack_rows(scaled).astype(BF16)
    projected = dot(scaled.astype(BF16), w_qkv[...], ((1,), (1,)))
    c_low = c.astype(BF16)
    d_first_value = dot(c_low, w_proj[...])
    fields[0] = x.astype(BF16)
    fields[1] = c_low
    projected_out[...] = projected.astype(BF16)

    lane_row = row_index((1, 128), 1) >> 4
    along = labels[0]
    for b in range(1, 6):
        along = jnp.where(lane_row == b, labels[b], along)
    allowed = jnp.concatenate(
        [
            jnp.broadcast_to(jnp.where(labels[b] == along, 0.0, MASKED), (16, 128))
            for b in range(6)
        ],
        axis=0,
    )

    def probabilities(level, pair):
        rows = slice(level * LEVEL_ROWS, (level + 1) * LEVEL_ROWS)
        cols = slice(pair * 128, (pair + 1) * 128)
        added = bias[pair * 192 : (pair + 1) * 192, :].reshape(2, LEVEL_ROWS, 128) + allowed[None]
        keys = per_head(projected_out[rows, 512 + pair * 128 : 512 + (pair + 1) * 128])
        scores = dot(keys, projected_out[rows, cols], ((1,), (1,))).reshape(2, LEVEL_ROWS, LEVEL_ROWS)
        scores = scores * SCORE_SCALE + added[:, :, :LEVEL_ROWS]
        weights = jnp.exp(scores - jnp.max(scores, axis=1, keepdims=True))
        probs = weights * (1.0 / jnp.sum(weights, axis=1, keepdims=True))
        att_out[level, pair] = probs.astype(BF16)
        return probs

    attention_backward(probabilities, d_first_value.astype(BF16), projected_out, dqkv)
    skip[...] = pack_rows(c + input_gradient(dqkv, w_qkv, gain, normed, inv_std)).astype(BF16)


def second_kernel(
    core, arrived, fields, projected, att, w_proj, w_qkv, gain,
    kept, sent, near, far, dqkv,
):
    c2 = unpack_rows(arrived[...].astype(F32))
    d_low = (dot(fields[1], w_proj[...]) + dot(c2.astype(BF16), w_proj[...])).astype(BF16)
    attention_backward(lambda level, pair: att[level, pair].astype(F32), d_low, projected, dqkv)
    lane = row_index((PACKED_ROWS, 128), 1)
    is_first = core[0] == 0
    halves = []

    def share(cols, first, last):
        kept[:, cols] = jnp.where(is_first, first, last).astype(BF16)
        sent[:, cols] = jnp.where(is_first, last, first).astype(BF16)

    for t in range(4):
        first, middle, last = (
            pack_rows(dqkv[:, 384 * t + 128 * j : 384 * t + 128 * (j + 1)]) for j in range(3)
        )
        halves.append(middle)
        share(slice(128 * t, 128 * (t + 1)), first, last)
    for t in range(2):
        left, right = halves[2 * t], halves[2 * t + 1]
        first = jnp.where(lane < 64, left, pltpu.roll(right, 64, 1))
        last = jnp.where(lane < 64, pltpu.roll(left, 64, 1), right)
        share(slice(512 + 128 * t, 512 + 128 * (t + 1)), first, last)

    normed, inv_std = normalised(fields[0].astype(F32))
    shifted = input_gradient(dqkv, w_qkv, gain, normed, inv_std)
    total = fields[1].astype(F32) + (c2 + shifted)
    for i in range(6):
        for half, target in ((0, near), (1, far)):
            start = 16 * i + 8 * half
            both = jnp.concatenate(
                [total[start : start + 8], total[96 + start : 96 + start + 8]], axis=0
            )
            target[i] = both.astype(BF16)


def turn_kernel(inputs, other_inputs, out):
    out[0] = inputs[...].astype(F32).T.astype(BF16)
    out[1] = other_inputs[...].astype(F32).T.astype(BF16)


def product_kernel(kept, got, inputs, out):
    product = dot(inputs[0], kept[...]) + dot(inputs[1], got[...])
    bands = out.shape[1]
    width = FEATURES // bands
    lane = row_index((bands, width // 2, 128), 2)
    for t in range(4):
        whole = product[:, 128 * t : 128 * (t + 1)].reshape(bands, width, 128)
        out[t, :, :width, :] = whole.astype(BF16)
        start = 512 + 128 * (t // 2)
        half = product[:, start : start + 128].reshape(bands, width, 128)
        top, bottom = half[:, : width // 2], half[:, width // 2 :]
        if t % 2 == 0:
            folded = jnp.where(lane < 64, top, pltpu.roll(bottom, 64, 2))
        else:
            folded = jnp.where(lane < 64, pltpu.roll(top, 64, 2), bottom)
        out[t, :, width:, :] = folded.astype(BF16)


def chips_kernel(products, near, left, out, upward):
    total = products[0].astype(F32)
    for t in range(1, products.shape[0]):
        total = total + products[t].astype(F32)
    out[...] = total.astype(BF16)
    for i in range(3):
        upward[0, i] = left[3 + i]
        upward[1, i] = near[3 + i]


def sum_kernel(odd, parts, out):
    bands, rows, _ = parts.shape
    width = rows * 2 // 3
    total = parts[0].astype(F32)
    for band in range(1, bands):
        total = total + parts[band].astype(F32)
    whole = total[:width]
    folded = total[width:]
    half = jnp.concatenate([folded, pltpu.roll(folded, 64, 1)], axis=0)
    half = half[:, :64]

    @pl.when(odd[0] == 0)
    def _():
        out[0, :, :128] = whole
        out[0, :, 128:] = half

    @pl.when(odd[0] == 1)
    def _():
        out[0, :, :64] = half
        out[0, :, 64:] = whole


def join_kernel(near, left, arrived, out):
    row = row_index((8, FEATURES), 0)
    for level in range(2):
        part = slice(level * 8, level * 8 + 8)
        for i in range(6):
            low, high = (arrived[0, i], arrived[1, i]) if i < 3 else (left[i - 3], near[i - 3])
            low = low.astype(F32)[part]
            high = pltpu.roll(high.astype(F32)[part], 6, 0)
            out[0, level, i, 0:8, :] = jnp.where(row < 6, low, high).astype(BF16)
            out[0, level, i, 8:12, :] = high[:4].astype(BF16)


def passed(array, lat_by, lon_by):
    lats, lons = lax.axis_size("lat"), lax.axis_size("lon")
    pairs = [
        (a * lons + o, ((a + lat_by) % lats) * lons + (o + lon_by) % lons)
        for a in range(lats)
        for o in range(lons)
    ]
    return lax.ppermute(array, ("lat", "lon"), pairs)


def other_core(array):
    return lax.ppermute(array, "lat", [(a, a ^ 1) for a in range(lax.axis_size("lat"))])


def per_device(x_in, out_grad, w_qkv, w_proj, norm_gain, bias_table, lat_labels):
    lats, lons = lax.axis_size("lat"), lax.axis_size("lon")
    w_qkv, w_proj = w_qkv[0], w_proj[0]
    piece = struct((2, 3, 16, FEATURES), BF16)
    own, lon, lat, cor = call(
        cut_kernel,
        (piece,) * 4,
        [pltpu.SMEM(lat_labels.shape, jnp.int32), pltpu.SemaphoreType.DMA],
        places={0: pl.ANY},
    )(lat_labels, x_in, out_grad)
    lon = passed(lon, 0, -1)
    lat = passed(lat, -1, 0)
    cor = passed(cor, -1, -1)
    table = jnp.pad(bias_table[0, :, 253:506], ((0, 0), (0, 3)))
    bias = call(
        bias_kernel,
        struct((HEADS * LEVEL_ROWS, 128), F32),
        cost=pl.CostEstimate(flops=4_000_000_000, bytes_accessed=20_000_000, transcendentals=0),
    )(table)

    scratch = [pltpu.VMEM((ROWS, 3 * FEATURES), F32)]
    skip, packed, fields, projected, att = call(
        first_kernel,
        (
            struct((PACKED_ROWS, FEATURES), BF16),
            struct((PACKED_ROWS, FEATURES), BF16),
            struct((2, ROWS, FEATURES), BF16),
            struct((ROWS, 3 * FEATURES), BF16),
            struct((2, 4, 2, LEVEL_ROWS, LEVEL_ROWS), BF16),
        ),
        scratch,
    )(own, lon, lat, cor, w_qkv, w_proj, norm_gain, bias)

    core = (lax.axis_index("lat") % 2).astype(jnp.int32).reshape(1)
    arrived = lax.ppermute(skip, "phase", [(1, 0)])
    turned = call(turn_kernel, struct((2, FEATURES, PACKED_ROWS), BF16))(
        packed, other_core(packed)
    )
    arrived, turned = lax.optimization_barrier((arrived, turned))
    back = struct((6, 16, FEATURES), BF16)
    half = struct((PACKED_ROWS, 768), BF16)
    kept, sent, near, far = call(
        second_kernel,
        (half, half, back, back),
        scratch,
        places={0: pltpu.SMEM},
    )(core, arrived, fields, projected, att, w_proj, w_qkv, norm_gain)
    got = other_core(sent)
    left = passed(far, 0, 1)
    rows = FEATURES * 3 // 2 // lons
    products = call(product_kernel, struct((lats // 2, lons, rows, 128), BF16))(
        kept, got, turned
    )
    chips = [[2 * x + c for x in range(lats // 2)] for c in range(2)]
    products = lax.all_to_all(products, "lat", 0, 0, tiled=True, axis_index_groups=chips)
    slices, upward = call(
        chips_kernel,
        (struct((lons, rows, 128), BF16), struct((2, 3, 16, FEATURES), BF16)),
    )(products, near, left)
    above = passed(upward, 1, 0)
    grad_input = call(join_kernel, struct((1, 2, 6, 12, FEATURES), BF16))(near, left, above)
    slices = lax.all_to_all(slices, "lon", 0, 0, tiled=True)
    grad_qkv = call(
        sum_kernel, struct((1, FEATURES // lons, 192), F32), places={0: pltpu.SMEM}
    )(core, slices)
    return grad_input, grad_qkv.transpose(0, 2, 1)


def solution(mesh):
    in_specs = (
        P("phase", None, "lat", "lon", None),
        P("phase", None, "lat", "lon", None),
        P("phase", None, None),
        P("phase", None, None),
        P("phase", None),
        P("phase", None, None),
        P("lat"),
    )
    out_specs = (P("phase", None, "lat", "lon", None), P("phase", "lat", "lon"))
    return jax.shard_map(
        per_device, mesh=mesh, in_specs=in_specs, out_specs=out_specs, check_vma=False
    )
```

```python
import functools

import jax
import jax.numpy as jnp
from jax import lax
from jax.experimental import pallas as pl
from jax.experimental.pallas import tpu as pltpu
from jax.sharding import PartitionSpec as P

F32 = jnp.float32
BF16 = jnp.bfloat16
HEADS = 8
FEATURES = 512
EPSILON = 1e-05
MASKED = -1e30
SCORE_SCALE = 0.125
MIB = 1024 * 1024

LEVEL_ROWS = 96
ROWS = 192


def call(kernel, out_shape, scratch=(), places=(), out_places=(), cost=None, limit=50 * MIB):
    def run(*args):
        places_of = dict(places)
        specs = [
            pl.BlockSpec(memory_space=places_of.get(i, pltpu.VMEM)) for i in range(len(args))
        ]
        outs_of = dict(out_places)
        outs = [
            pl.BlockSpec(memory_space=outs_of.get(i, pltpu.VMEM))
            for i in range(len(jax.tree.leaves(out_shape)))
        ]
        outs = tuple(outs) if isinstance(out_shape, tuple) else outs[0]
        return pl.pallas_call(
            kernel,
            out_shape=out_shape,
            in_specs=specs,
            out_specs=outs,
            scratch_shapes=list(scratch),
            cost_estimate=cost,
            compiler_params=pltpu.CompilerParams(vmem_limit_bytes=limit),
        )(*args)

    return run


def struct(shape, dtype):
    return jax.ShapeDtypeStruct(shape, dtype)


def dot(left, right, dims=((1,), (0,))):
    return lax.dot_general(left, right, (dims, ((), ())), preferred_element_type=F32)


def row_index(shape, dim):
    return lax.broadcasted_iota(jnp.int32, shape, dim)


def cut_kernel(labels_ref, x_ref, g_ref, own, lon, lat, cor, labels, x_rows, g_rows, sem, sems):
    fetch = pltpu.make_async_copy(labels_ref, labels, sem)
    fetch.start()
    fetches = []
    for i in range(6):
        fetches.append(pltpu.make_async_copy(x_ref.at[i], x_rows.at[i], sems.at[0, i]))
        fetches.append(pltpu.make_async_copy(g_ref.at[i], g_rows.at[i], sems.at[1, i]))
    for copy in fetches:
        copy.start()
    row = row_index((8, FEATURES), 0)

    def halves(field, level, fill):
        low, high = field[0:8, level, :], field[4:12, level, :]
        return (
            jnp.where(row < 6, low, fill),
            jnp.where(row < 6, pltpu.roll(high, 6, 0), fill),
        )

    fetch.wait()
    for i in range(6):
        label = labels[i].astype(F32)
        fetches[2 * i].wait()
        fetches[2 * i + 1].wait()
        x, g = x_rows[i].astype(F32), g_rows[i].astype(F32)
        for level in range(2):
            x_low, x_high = halves(x, level, label)
            g_low, g_high = halves(g, level, 0.0)
            low = jnp.concatenate([x_low, g_low], axis=0).astype(BF16)
            high = jnp.concatenate([x_high, g_high], axis=0).astype(BF16)
            if i < 3:
                cor[level, i] = low
                lat[level, i] = high
            else:
                lon[level, i - 3] = low
                own[level, i - 3] = high


def bias_kernel(table, out):
    parts = []
    for h in range(HEADS):
        line = jnp.broadcast_to(table[h : h + 1, :], (8, 256))
        parts.append(pltpu.roll(line, 0, 1, stride=1, stride_axis=0))
        parts.append(pltpu.roll(line, 6, 1, stride=1, stride_axis=0))
    shifted = jnp.concatenate(parts, axis=0)
    source = row_index((256, 256), 0)
    lane = row_index((256, 256), 1)
    column = lane & 7
    target = (lane >> 4) * 23 + ((lane >> 3) & 1) * 6 + column + 11
    picked = jnp.where((source == target) & (column < 6), 1.0, 0.0).astype(BF16)
    first = shifted.astype(BF16)
    rest = shifted - first.astype(F32)
    second = rest.astype(BF16)
    third = (rest - second.astype(F32)).astype(BF16)
    spread = dot(first, picked) + dot(second, picked) + dot(third, picked)
    empty = (row_index((128, 128), 0) & 7) >= 6
    for b in range(6):
        shift = (256 - (5 - b) * 16) % 256
        moved = spread if shift == 0 else pltpu.roll(spread, shift, 1)
        moved = jnp.where(empty, MASKED, moved[:, :128])
        for h in range(HEADS):
            out[h * 96 + b * 16 : h * 96 + b * 16 + 16, :] = moved[h * 16 : h * 16 + 16, :]


def per_head(pair):
    even = row_index(pair.shape, 1) < 64
    wide = pair.astype(F32)
    return jnp.concatenate(
        [jnp.where(even, wide, 0.0).astype(BF16), jnp.where(even, 0.0, wide).astype(BF16)], axis=0
    )


def attention_backward(att, d_low, projected, dqkv):
    lane = row_index((LEVEL_ROWS, 128), 1)
    for level in range(2):
        rows = slice(level * LEVEL_ROWS, (level + 1) * LEVEL_ROWS)
        for pair in range(4):
            cols = slice(pair * 128, (pair + 1) * 128)
            probs = att(level, pair)
            probs_low = probs.astype(BF16).reshape(2 * LEVEL_ROWS, LEVEL_ROWS)
            d_out = d_low[rows, cols]
            query = projected[rows, cols]
            keys = per_head(projected[rows, 512 + pair * 128 : 512 + (pair + 1) * 128])
            values = per_head(projected[rows, 1024 + pair * 128 : 1024 + (pair + 1) * 128])
            d_probs = dot(values, d_out, ((1,), (1,))).reshape(2, LEVEL_ROWS, LEVEL_ROWS)
            inner = jnp.sum(probs * d_probs, axis=1, keepdims=True)
            d_scores = (probs * (d_probs - inner)).astype(BF16).reshape(2 * LEVEL_ROWS, LEVEL_ROWS)
            d_value = dot(probs_low, d_out)
            d_key = dot(d_scores, query)
            d_query = dot(d_scores, keys, ((0,), (0,)))
            dqkv[rows, pair * 128 : (pair + 1) * 128] = (d_query * SCORE_SCALE).astype(BF16)
            dqkv[rows, 512 + pair * 128 : 512 + (pair + 1) * 128] = (
                jnp.where(lane < 64, d_key[:LEVEL_ROWS], d_key[LEVEL_ROWS:]) * SCORE_SCALE
            ).astype(BF16)
            dqkv[rows, 1024 + pair * 128 : 1024 + (pair + 1) * 128] = jnp.where(
                lane < 64, d_value[:LEVEL_ROWS], d_value[LEVEL_ROWS:]
            ).astype(BF16)


def input_gradient(dqkv, w_qkv, gain, normed, inv_std):
    d_normed = dot(dqkv[...], w_qkv[...]) * gain[...]
    mean_plain = jnp.mean(d_normed, axis=-1, keepdims=True)
    mean_normed = jnp.mean(d_normed * normed, axis=-1, keepdims=True)
    return inv_std * (d_normed - mean_plain - normed * mean_normed)


def normalised(x):
    center = jnp.mean(x, axis=-1, keepdims=True)
    moved = x - center
    spread = jnp.mean(jnp.square(moved), axis=-1, keepdims=True)
    inv_std = lax.rsqrt(spread + EPSILON)
    return moved * inv_std, inv_std


def first_kernel(
    own, lon, lat, cor, w_qkv_ref, w_proj, gain, bias,
    skip, inputs, fields, projected_out, att_out,
    dqkv, w_qkv, sem,
):
    fetch = pltpu.make_async_copy(w_qkv_ref, w_qkv, sem)
    fetch.start()
    tiles_x, tiles_g = [], []
    labels = []
    row = row_index((8, FEATURES), 0)
    for level in range(2):
        for i in range(6):
            left, right = (own, lon) if i < 3 else (lat, cor)
            left, right = left[level, i % 3].astype(F32), right[level, i % 3].astype(F32)
            if level == 0:
                labels.append(left[6:7, :128])
            for tile in (left, right):
                tiles_x.append(jnp.where(row < 6, tile[:8], 0.0))
                tiles_g.append(tile[8:])
    x = jnp.concatenate(tiles_x, axis=0)
    c = jnp.concatenate(tiles_g, axis=0)
    normed, inv_std = normalised(x)
    scaled = normed * gain[...]
    inputs[...] = scaled.astype(BF16)
    fetch.wait()
    projected = dot(inputs[...], w_qkv[...], ((1,), (1,)))
    c_low = c.astype(BF16)
    d_first_value = dot(c_low, w_proj[...])
    fields[0] = x.astype(BF16)
    fields[1] = c_low
    projected_out[...] = projected.astype(BF16)

    lane_row = row_index((1, 128), 1) >> 4
    along = labels[0]
    for b in range(1, 6):
        along = jnp.where(lane_row == b, labels[b], along)
    allowed = jnp.concatenate(
        [
            jnp.broadcast_to(jnp.where(labels[b] == along, 0.0, MASKED), (16, 128))
            for b in range(6)
        ],
        axis=0,
    )

    def probabilities(level, pair):
        rows = slice(level * LEVEL_ROWS, (level + 1) * LEVEL_ROWS)
        cols = slice(pair * 128, (pair + 1) * 128)
        added = bias[pair * 192 : (pair + 1) * 192, :].reshape(2, LEVEL_ROWS, 128) + allowed[None]
        keys = per_head(projected_out[rows, 512 + pair * 128 : 512 + (pair + 1) * 128])
        scores = dot(keys, projected_out[rows, cols], ((1,), (1,))).reshape(2, LEVEL_ROWS, LEVEL_ROWS)
        scores = scores * SCORE_SCALE + added[:, :, :LEVEL_ROWS]
        weights = jnp.exp(scores - jnp.max(scores, axis=1, keepdims=True))
        probs = weights * (1.0 / jnp.sum(weights, axis=1, keepdims=True))
        att_out[level, pair] = probs.astype(BF16)
        return probs

    attention_backward(probabilities, d_first_value.astype(BF16), projected_out, dqkv)
    skip[...] = (c + input_gradient(dqkv, w_qkv, gain, normed, inv_std)).astype(BF16)


def second_kernel(
    core, arrived, inputs, fields, projected, att, w_proj, w_qkv_ref, gain,
    kept, sent, near, far, dqkv, w_qkv, sem,
):
    fetch = pltpu.make_async_copy(w_qkv_ref, w_qkv, sem)
    fetch.start()
    d_low = (dot(fields[1], w_proj[...]) + dot(arrived[...], w_proj[...])).astype(BF16)
    attention_backward(lambda level, pair: att[level, pair].astype(F32), d_low, projected, dqkv)
    lane = row_index((ROWS, 128), 1)
    is_first = core[0] == 0
    halves = []

    def share(cols, first, last):
        kept[:, cols] = jnp.where(is_first, first, last).astype(BF16)
        sent[:, cols] = jnp.where(is_first, last, first).astype(BF16)

    for t in range(4):
        first, middle, last = (
            dqkv[:, 384 * t + 128 * j : 384 * t + 128 * (j + 1)].astype(F32) for j in range(3)
        )
        halves.append(middle)
        share(slice(128 * t, 128 * (t + 1)), first, last)
    for t in range(2):
        left, right = halves[2 * t], halves[2 * t + 1]
        first = jnp.where(lane < 64, left, pltpu.roll(right, 64, 1))
        last = jnp.where(lane < 64, pltpu.roll(left, 64, 1), right)
        share(slice(512 + 128 * t, 512 + 128 * (t + 1)), first, last)
    sent[:, 768:] = inputs[...]

    normed, inv_std = normalised(fields[0].astype(F32))
    fetch.wait()
    shifted = input_gradient(dqkv, w_qkv, gain, normed, inv_std)
    total = fields[1].astype(F32) + (arrived[...].astype(F32) + shifted)
    for i in range(6):
        for half, target in ((0, near), (1, far)):
            start = 16 * i + 8 * half
            both = jnp.concatenate(
                [total[start : start + 8], total[96 + start : 96 + start + 8]], axis=0
            )
            target[i] = both.astype(BF16)


def product_kernel(kept, inputs, got, out):
    product = dot(inputs[...], kept[...], ((0,), (0,)))
    product = product + dot(got[:, 768:], got[:, :768], ((0,), (0,)))
    bands = out.shape[1]
    width = FEATURES // bands
    lane = row_index((bands, width // 2, 128), 2)
    for t in range(4):
        whole = product[:, 128 * t : 128 * (t + 1)].reshape(bands, width, 128)
        out[t, :, :width, :] = whole.astype(BF16)
        start = 512 + 128 * (t // 2)
        half = product[:, start : start + 128].reshape(bands, width, 128)
        top, bottom = half[:, : width // 2], half[:, width // 2 :]
        if t % 2 == 0:
            folded = jnp.where(lane < 64, top, pltpu.roll(bottom, 64, 2))
        else:
            folded = jnp.where(lane < 64, pltpu.roll(top, 64, 2), bottom)
        out[t, :, width:, :] = folded.astype(BF16)


def chips_kernel(products, near, left, out, upward):
    total = products[0].astype(F32)
    for t in range(1, products.shape[0]):
        total = total + products[t].astype(F32)
    out[...] = total.astype(BF16)
    for i in range(3):
        upward[0, i] = left[3 + i]
        upward[1, i] = near[3 + i]


def sum_kernel(odd, parts, out):
    bands, rows, _ = parts.shape
    width = rows * 2 // 3
    total = parts[0].astype(F32)
    for band in range(1, bands):
        total = total + parts[band].astype(F32)
    whole = total[:width]
    folded = total[width:]
    half = jnp.concatenate([folded, pltpu.roll(folded, 64, 1)], axis=0)
    half = half[:, :64]

    @pl.when(odd[0] == 0)
    def _():
        out[0, :, :128] = whole
        out[0, :, 128:] = half

    @pl.when(odd[0] == 1)
    def _():
        out[0, :, :64] = half
        out[0, :, 64:] = whole


def join_kernel(near, left, arrived, out):
    row = row_index((8, FEATURES), 0)
    for level in range(2):
        part = slice(level * 8, level * 8 + 8)
        for i in range(6):
            low, high = (arrived[0, i], arrived[1, i]) if i < 3 else (left[i - 3], near[i - 3])
            low = low.astype(F32)[part]
            high = pltpu.roll(high.astype(F32)[part], 6, 0)
            out[0, level, i, 0:8, :] = jnp.where(row < 6, low, high).astype(BF16)
            out[0, level, i, 8:12, :] = high[:4].astype(BF16)


def passed(array, lat_by, lon_by):
    lats, lons = lax.axis_size("lat"), lax.axis_size("lon")
    pairs = [
        (a * lons + o, ((a + lat_by) % lats) * lons + (o + lon_by) % lons)
        for a in range(lats)
        for o in range(lons)
    ]
    return lax.ppermute(array, ("lat", "lon"), pairs)


def other_core(array):
    return lax.ppermute(array, "lat", [(a, a ^ 1) for a in range(lax.axis_size("lat"))])


def per_device(x_in, out_grad, w_qkv, w_proj, norm_gain, bias_table, lat_labels):
    lats, lons = lax.axis_size("lat"), lax.axis_size("lon")
    w_qkv, w_proj = w_qkv[0], w_proj[0]
    piece = struct((2, 3, 16, FEATURES), BF16)
    own, lon, lat, cor = call(
        cut_kernel,
        (piece,) * 4,
        [
            pltpu.SMEM(lat_labels.shape, jnp.int32),
            pltpu.VMEM((6, 12, 2, FEATURES), BF16),
            pltpu.VMEM((6, 12, 2, FEATURES), BF16),
            pltpu.SemaphoreType.DMA,
            pltpu.SemaphoreType.DMA((2, 6)),
        ],
        places={0: pl.ANY, 1: pl.ANY, 2: pl.ANY},
        limit=58 * MIB,
    )(lat_labels, x_in[0].transpose(1, 2, 0, 3), out_grad[0].transpose(1, 2, 0, 3))
    lon = passed(lon, 0, -1)
    lat = passed(lat, -1, 0)
    cor = passed(cor, -1, -1)
    table = jnp.pad(bias_table[0, :, 253:506], ((0, 0), (0, 3)))
    bias = call(
        bias_kernel,
        struct((HEADS * LEVEL_ROWS, 128), F32),
        cost=pl.CostEstimate(flops=4_000_000_000, bytes_accessed=20_000_000, transcendentals=0),
    )(table)

    scratch = [
        pltpu.VMEM((ROWS, 3 * FEATURES), BF16),
        pltpu.VMEM(w_qkv.shape, BF16),
        pltpu.SemaphoreType.DMA,
    ]
    skip, inputs, fields, projected, att = call(
        first_kernel,
        (
            struct((ROWS, FEATURES), BF16),
            struct((ROWS, FEATURES), BF16),
            struct((2, ROWS, FEATURES), BF16),
            struct((ROWS, 3 * FEATURES), BF16),
            struct((2, 4, 2, LEVEL_ROWS, LEVEL_ROWS), BF16),
        ),
        scratch,
        places={4: pl.ANY},
    )(own, lon, lat, cor, w_qkv, w_proj, norm_gain, bias)

    core = (lax.axis_index("lat") % 2).astype(jnp.int32).reshape(1)
    arrived = lax.ppermute(skip, "phase", [(1, 0)])
    back = struct((6, 16, FEATURES), BF16)
    half = struct((ROWS, 768), BF16)
    half_and_inputs = struct((ROWS, 768 + FEATURES), BF16)
    kept, sent, near, far = call(
        second_kernel,
        (half, half_and_inputs, back, back),
        scratch,
        places={0: pltpu.SMEM, 7: pl.ANY},
    )(core, arrived, inputs, fields, projected, att, w_proj, w_qkv, norm_gain)
    got = other_core(sent)
    left = passed(far, 0, 1)
    rows = FEATURES * 3 // 2 // lons
    products = call(product_kernel, struct((lats // 2, lons, rows, 128), BF16))(
        kept, inputs, got
    )
    chips = [[2 * x + c for x in range(lats // 2)] for c in range(2)]
    products = lax.all_to_all(products, "lat", 0, 0, tiled=True, axis_index_groups=chips)
    slices, upward = call(
        chips_kernel,
        (struct((lons, rows, 128), BF16), struct((2, 3, 16, FEATURES), BF16)),
    )(products, near, left)
    above = passed(upward, 1, 0)
    grad_input = call(join_kernel, struct((1, 2, 6, 12, FEATURES), BF16))(near, left, above)
    slices = lax.all_to_all(slices, "lon", 0, 0, tiled=True)
    grad_qkv = call(
        sum_kernel, struct((1, FEATURES // lons, 192), F32), places={0: pltpu.SMEM}
    )(core, slices)
    return grad_input, grad_qkv.transpose(0, 2, 1)


def solution(mesh):
    in_specs = (
        P("phase", None, "lat", "lon", None),
        P("phase", None, "lat", "lon", None),
        P("phase", None, None),
        P("phase", None, None),
        P("phase", None),
        P("phase", None, None),
        P("lat"),
    )
    out_specs = (P("phase", None, "lat", "lon", None), P("phase", "lat", "lon"))
    return jax.shard_map(
        per_device, mesh=mesh, in_specs=in_specs, out_specs=out_specs, check_vma=False
    )
```

```python
import functools

import jax
import jax.numpy as jnp
from jax import lax
from jax.experimental import pallas as pl
from jax.experimental.pallas import tpu as pltpu
from jax.sharding import PartitionSpec as P

F32 = jnp.float32
BF16 = jnp.bfloat16
HEADS = 8
FEATURES = 512
EPSILON = 1e-05
MASKED = -1e30
SCORE_SCALE = 0.125
MIB = 1024 * 1024

LEVEL_ROWS = 96
ROWS = 192
PACKED_ROWS = 144


def call(kernel, out_shape, scratch=(), places=(), out_places=(), cost=None, limit=50 * MIB):
    def run(*args):
        places_of = dict(places)
        specs = [
            pl.BlockSpec(memory_space=places_of.get(i, pltpu.VMEM)) for i in range(len(args))
        ]
        outs_of = dict(out_places)
        outs = [
            pl.BlockSpec(memory_space=outs_of.get(i, pltpu.VMEM))
            for i in range(len(jax.tree.leaves(out_shape)))
        ]
        outs = tuple(outs) if isinstance(out_shape, tuple) else outs[0]
        return pl.pallas_call(
            kernel,
            out_shape=out_shape,
            in_specs=specs,
            out_specs=outs,
            scratch_shapes=list(scratch),
            cost_estimate=cost,
            compiler_params=pltpu.CompilerParams(vmem_limit_bytes=limit),
        )(*args)

    return run


def struct(shape, dtype):
    return jax.ShapeDtypeStruct(shape, dtype)


def dot(left, right, dims=((1,), (0,))):
    return lax.dot_general(left, right, (dims, ((), ())), preferred_element_type=F32)


def row_index(shape, dim):
    return lax.broadcasted_iota(jnp.int32, shape, dim)


def cut_kernel(labels_ref, x_ref, g_ref, own, lon, lat, cor, labels, x_rows, g_rows, sem, sems):
    fetch = pltpu.make_async_copy(labels_ref, labels, sem)
    fetch.start()
    fetches = []
    for i in range(6):
        fetches.append(pltpu.make_async_copy(x_ref.at[i], x_rows.at[i], sems.at[0, i]))
        fetches.append(pltpu.make_async_copy(g_ref.at[i], g_rows.at[i], sems.at[1, i]))
    for copy in fetches:
        copy.start()
    row = row_index((8, FEATURES), 0)

    def halves(field, level, fill):
        low, high = field[0:8, level, :], field[4:12, level, :]
        return (
            jnp.where(row < 6, low, fill),
            jnp.where(row < 6, pltpu.roll(high, 6, 0), fill),
        )

    fetch.wait()
    for i in range(6):
        label = labels[i].astype(F32)
        fetches[2 * i].wait()
        fetches[2 * i + 1].wait()
        x, g = x_rows[i].astype(F32), g_rows[i].astype(F32)
        for level in range(2):
            x_low, x_high = halves(x, level, label)
            g_low, g_high = halves(g, level, 0.0)
            low = jnp.concatenate([x_low, g_low], axis=0).astype(BF16)
            high = jnp.concatenate([x_high, g_high], axis=0).astype(BF16)
            if i < 3:
                cor[level, i] = low
                lat[level, i] = high
            else:
                lon[level, i - 3] = low
                own[level, i - 3] = high


def bias_kernel(table, out):
    parts = []
    for h in range(HEADS):
        line = jnp.broadcast_to(table[h : h + 1, :], (8, 256))
        parts.append(pltpu.roll(line, 0, 1, stride=1, stride_axis=0))
        parts.append(pltpu.roll(line, 6, 1, stride=1, stride_axis=0))
    shifted = jnp.concatenate(parts, axis=0)
    source = row_index((256, 256), 0)
    lane = row_index((256, 256), 1)
    column = lane & 7
    target = (lane >> 4) * 23 + ((lane >> 3) & 1) * 6 + column + 11
    picked = jnp.where((source == target) & (column < 6), 1.0, 0.0).astype(BF16)
    first = shifted.astype(BF16)
    rest = shifted - first.astype(F32)
    second = rest.astype(BF16)
    third = (rest - second.astype(F32)).astype(BF16)
    spread = dot(first, picked) + dot(second, picked) + dot(third, picked)
    empty = (row_index((128, 128), 0) & 7) >= 6
    for b in range(6):
        shift = (256 - (5 - b) * 16) % 256
        moved = spread if shift == 0 else pltpu.roll(spread, shift, 1)
        moved = jnp.where(empty, MASKED, moved[:, :128])
        for h in range(HEADS):
            out[h * 96 + b * 16 : h * 96 + b * 16 + 16, :] = moved[h * 16 : h * 16 + 16, :]


def pack_rows(array):
    columns = array.shape[1]
    groups = array.reshape(6, 4, 8, columns)
    row = row_index((8, columns), 0)
    out = []
    for q in range(6):
        last = groups[q, 3]
        for g in range(3):
            out.append(jnp.where(row < 6, groups[q, g], pltpu.roll(last, 6 - 2 * g, 0)))
    return jnp.concatenate(out, axis=0)


def per_head(pair):
    even = row_index(pair.shape, 1) < 64
    wide = pair.astype(F32)
    return jnp.concatenate(
        [jnp.where(even, wide, 0.0).astype(BF16), jnp.where(even, 0.0, wide).astype(BF16)], axis=0
    )


def attention_backward(att, d_low, projected, dqkv):
    lane = row_index((LEVEL_ROWS, 128), 1)
    for level in range(2):
        rows = slice(level * LEVEL_ROWS, (level + 1) * LEVEL_ROWS)
        for pair in range(4):
            cols = slice(pair * 128, (pair + 1) * 128)
            probs = att(level, pair)
            probs_low = probs.astype(BF16).reshape(2 * LEVEL_ROWS, LEVEL_ROWS)
            d_out = d_low[rows, cols]
            query = projected[rows, cols]
            keys = per_head(projected[rows, 512 + pair * 128 : 512 + (pair + 1) * 128])
            values = per_head(projected[rows, 1024 + pair * 128 : 1024 + (pair + 1) * 128])
            d_probs = dot(values, d_out, ((1,), (1,))).reshape(2, LEVEL_ROWS, LEVEL_ROWS)
            inner = jnp.sum(probs * d_probs, axis=1, keepdims=True)
            d_scores = (probs * (d_probs - inner)).astype(BF16).reshape(2 * LEVEL_ROWS, LEVEL_ROWS)
            d_value = dot(probs_low, d_out)
            d_key = dot(d_scores, query)
            d_query = dot(d_scores, keys, ((0,), (0,)))
            dqkv[rows, pair * 128 : (pair + 1) * 128] = (d_query * SCORE_SCALE).astype(BF16)
            dqkv[rows, 512 + pair * 128 : 512 + (pair + 1) * 128] = (
                jnp.where(lane < 64, d_key[:LEVEL_ROWS], d_key[LEVEL_ROWS:]) * SCORE_SCALE
            ).astype(BF16)
            dqkv[rows, 1024 + pair * 128 : 1024 + (pair + 1) * 128] = jnp.where(
                lane < 64, d_value[:LEVEL_ROWS], d_value[LEVEL_ROWS:]
            ).astype(BF16)


def input_gradient(dqkv, w_qkv, gain, normed, inv_std):
    d_normed = dot(dqkv[...], w_qkv[...]) * gain[...]
    mean_plain = jnp.mean(d_normed, axis=-1, keepdims=True)
    mean_normed = jnp.mean(d_normed * normed, axis=-1, keepdims=True)
    return inv_std * (d_normed - mean_plain - normed * mean_normed)


def normalised(x):
    center = jnp.mean(x, axis=-1, keepdims=True)
    moved = x - center
    spread = jnp.mean(jnp.square(moved), axis=-1, keepdims=True)
    inv_std = lax.rsqrt(spread + EPSILON)
    return moved * inv_std, inv_std


def first_kernel(
    own, lon, lat, cor, w_qkv_ref, w_proj, gain, bias,
    skip, inputs, fields, projected_out, att_out,
    dqkv, w_qkv, sem,
):
    fetch = pltpu.make_async_copy(w_qkv_ref, w_qkv, sem)
    fetch.start()
    tiles_x, tiles_g = [], []
    labels = []
    row = row_index((8, FEATURES), 0)
    for level in range(2):
        for i in range(6):
            left, right = (own, lon) if i < 3 else (lat, cor)
            left, right = left[level, i % 3].astype(F32), right[level, i % 3].astype(F32)
            if level == 0:
                labels.append(left[6:7, :128])
            for tile in (left, right):
                tiles_x.append(jnp.where(row < 6, tile[:8], 0.0))
                tiles_g.append(tile[8:])
    x = jnp.concatenate(tiles_x, axis=0)
    c = jnp.concatenate(tiles_g, axis=0)
    normed, inv_std = normalised(x)
    scaled = normed * gain[...]
    packed = pack_rows(scaled).astype(BF16)
    for p in range(inputs.shape[0]):
        inputs[p] = packed
    fetch.wait()
    projected = dot(scaled.astype(BF16), w_qkv[...], ((1,), (1,)))
    c_low = c.astype(BF16)
    d_first_value = dot(c_low, w_proj[...])
    fields[0] = x.astype(BF16)
    fields[1] = c_low
    projected_out[...] = projected.astype(BF16)

    lane_row = row_index((1, 128), 1) >> 4
    along = labels[0]
    for b in range(1, 6):
        along = jnp.where(lane_row == b, labels[b], along)
    allowed = jnp.concatenate(
        [
            jnp.broadcast_to(jnp.where(labels[b] == along, 0.0, MASKED), (16, 128))
            for b in range(6)
        ],
        axis=0,
    )

    def probabilities(level, pair):
        rows = slice(level * LEVEL_ROWS, (level + 1) * LEVEL_ROWS)
        cols = slice(pair * 128, (pair + 1) * 128)
        added = bias[pair * 192 : (pair + 1) * 192, :].reshape(2, LEVEL_ROWS, 128) + allowed[None]
        keys = per_head(projected_out[rows, 512 + pair * 128 : 512 + (pair + 1) * 128])
        scores = dot(keys, projected_out[rows, cols], ((1,), (1,))).reshape(2, LEVEL_ROWS, LEVEL_ROWS)
        scores = scores * SCORE_SCALE + added[:, :, :LEVEL_ROWS]
        weights = jnp.exp(scores - jnp.max(scores, axis=1, keepdims=True))
        probs = weights * (1.0 / jnp.sum(weights, axis=1, keepdims=True))
        att_out[level, pair] = probs.astype(BF16)
        return probs

    attention_backward(probabilities, d_first_value.astype(BF16), projected_out, dqkv)
    skip[...] = (c + input_gradient(dqkv, w_qkv, gain, normed, inv_std)).astype(BF16)


def second_kernel(
    arrived, fields, projected, att, w_proj, w_qkv_ref, gain,
    blocks, near, far, dqkv, w_qkv, sem,
):
    fetch = pltpu.make_async_copy(w_qkv_ref, w_qkv, sem)
    fetch.start()
    d_low = (dot(fields[1], w_proj[...]) + dot(arrived[...], w_proj[...])).astype(BF16)
    attention_backward(lambda level, pair: att[level, pair].astype(F32), d_low, projected, dqkv)
    lane = row_index((80, 128), 1)
    for t in range(4):
        whole = [
            pack_rows(dqkv[:, 384 * t + 128 * j : 384 * t + 128 * (j + 1)].astype(F32))
            for j in range(3)
        ]
        blocks[2 * t, :144, :] = whole[0].astype(BF16)
        blocks[2 * t + 1, :144, :] = whole[2].astype(BF16)
        top = whole[1][:80]
        bottom = jnp.concatenate([whole[1][80:], jnp.zeros((16, 128), F32)], axis=0)
        blocks[2 * t, 144:, :] = jnp.where(lane < 64, top, pltpu.roll(bottom, 64, 1)).astype(BF16)
        blocks[2 * t + 1, 144:, :] = jnp.where(lane < 64, pltpu.roll(top, 64, 1), bottom).astype(
            BF16
        )
    normed, inv_std = normalised(fields[0].astype(F32))
    fetch.wait()
    shifted = input_gradient(dqkv, w_qkv, gain, normed, inv_std)
    total = fields[1].astype(F32) + (arrived[...].astype(F32) + shifted)
    for i in range(6):
        for half, target in ((0, near), (1, far)):
            start = 16 * i + 8 * half
            both = jnp.concatenate(
                [total[start : start + 8], total[96 + start : 96 + start + 8]], axis=0
            )
            target[i] = both.astype(BF16)


def product_kernel(core, blocks, inputs, other_inputs, near, left, out, upward):
    whole = jnp.zeros((128, FEATURES), F32)
    upper = jnp.zeros((128, FEATURES), F32)
    lower = jnp.zeros((128, FEATURES), F32)
    for x in range(inputs.shape[0]):
        for cells, place in ((inputs, 2 * x + core[0]), (other_inputs, 2 * x + 1 - core[0])):
            whole += dot(blocks[place, :144, :], cells[x], ((0,), (0,)))
            folded = blocks[place, 144:, :]
            upper += dot(folded, cells[x, :80, :], ((0,), (0,)))
            lower += dot(folded[:64], cells[x, 80:, :], ((0,), (0,)))
    half = upper[:64] + lower[64:]
    whole_t = whole.T
    half_t = jnp.concatenate([half, jnp.zeros((64, FEATURES), F32)], axis=0).T
    bands = out.shape[0]
    width = FEATURES // bands
    lane = row_index((width // 2, 128), 1)
    for band in range(bands):
        out[band, :width, :] = whole_t[band * width : (band + 1) * width].astype(BF16)
        part = half_t[band * width : (band + 1) * width]
        out[band, width:, :] = jnp.where(
            lane < 64, part[: width // 2], pltpu.roll(part[width // 2 :], 64, 1)
        ).astype(BF16)
    for i in range(3):
        upward[0, i] = left[3 + i]
        upward[1, i] = near[3 + i]


def sum_kernel(odd, parts, out):
    bands, rows, _ = parts.shape
    width = rows * 2 // 3
    total = parts[0].astype(F32)
    for band in range(1, bands):
        total = total + parts[band].astype(F32)
    whole = total[:width]
    folded = total[width:]
    half = jnp.concatenate([folded, pltpu.roll(folded, 64, 1)], axis=0)
    half = half[:, :64]

    @pl.when(odd[0] == 0)
    def _():
        out[0, :, :128] = whole
        out[0, :, 128:] = half

    @pl.when(odd[0] == 1)
    def _():
        out[0, :, :64] = half
        out[0, :, 64:] = whole


def join_kernel(near, left, arrived, out):
    row = row_index((8, FEATURES), 0)
    for level in range(2):
        part = slice(level * 8, level * 8 + 8)
        for i in range(6):
            low, high = (arrived[0, i], arrived[1, i]) if i < 3 else (left[i - 3], near[i - 3])
            low = low.astype(F32)[part]
            high = pltpu.roll(high.astype(F32)[part], 6, 0)
            out[0, level, i, 0:8, :] = jnp.where(row < 6, low, high).astype(BF16)
            out[0, level, i, 8:12, :] = high[:4].astype(BF16)


def passed(array, lat_by, lon_by):
    lats, lons = lax.axis_size("lat"), lax.axis_size("lon")
    pairs = [
        (a * lons + o, ((a + lat_by) % lats) * lons + (o + lon_by) % lons)
        for a in range(lats)
        for o in range(lons)
    ]
    return lax.ppermute(array, ("lat", "lon"), pairs)


def other_core(array):
    return lax.ppermute(array, "lat", [(a, a ^ 1) for a in range(lax.axis_size("lat"))])


def per_device(x_in, out_grad, w_qkv, w_proj, norm_gain, bias_table, lat_labels):
    lats, lons = lax.axis_size("lat"), lax.axis_size("lon")
    w_qkv, w_proj = w_qkv[0], w_proj[0]
    piece = struct((2, 3, 16, FEATURES), BF16)
    own, lon, lat, cor = call(
        cut_kernel,
        (piece,) * 4,
        [
            pltpu.SMEM(lat_labels.shape, jnp.int32),
            pltpu.VMEM((6, 12, 2, FEATURES), BF16),
            pltpu.VMEM((6, 12, 2, FEATURES), BF16),
            pltpu.SemaphoreType.DMA,
            pltpu.SemaphoreType.DMA((2, 6)),
        ],
        places={0: pl.ANY, 1: pl.ANY, 2: pl.ANY},
        limit=58 * MIB,
    )(lat_labels, x_in[0].transpose(1, 2, 0, 3), out_grad[0].transpose(1, 2, 0, 3))
    lon = passed(lon, 0, -1)
    lat = passed(lat, -1, 0)
    cor = passed(cor, -1, -1)
    table = jnp.pad(bias_table[0, :, 253:506], ((0, 0), (0, 3)))
    bias = call(
        bias_kernel,
        struct((HEADS * LEVEL_ROWS, 128), F32),
        cost=pl.CostEstimate(flops=4_000_000_000, bytes_accessed=20_000_000, transcendentals=0),
    )(table)

    scratch = [
        pltpu.VMEM((ROWS, 3 * FEATURES), BF16),
        pltpu.VMEM(w_qkv.shape, BF16),
        pltpu.SemaphoreType.DMA,
    ]
    skip, inputs, fields, projected, att = call(
        first_kernel,
        (
            struct((ROWS, FEATURES), BF16),
            struct((lats // 2, PACKED_ROWS, FEATURES), BF16),
            struct((2, ROWS, FEATURES), BF16),
            struct((ROWS, 3 * FEATURES), BF16),
            struct((2, 4, 2, LEVEL_ROWS, LEVEL_ROWS), BF16),
        ),
        scratch,
        places={4: pl.ANY},
    )(own, lon, lat, cor, w_qkv, w_proj, norm_gain, bias)

    core = (lax.axis_index("lat") % 2).astype(jnp.int32).reshape(1)
    same_core = [[2 * x + c for x in range(lats // 2)] for c in range(2)]
    arrived = lax.ppermute(skip, "phase", [(1, 0)])
    inputs = lax.all_to_all(inputs, "lat", 0, 0, tiled=True, axis_index_groups=same_core)
    back = struct((6, 16, FEATURES), BF16)
    blocks, near, far = call(
        second_kernel,
        (struct((lats, 224, 128), BF16), back, back),
        scratch,
        places={5: pl.ANY},
        cost=pl.CostEstimate(flops=4_000_000_000, bytes_accessed=20_000_000, transcendentals=0),
    )(arrived, fields, projected, att, w_proj, w_qkv, norm_gain)
    blocks = lax.all_to_all(blocks, "lat", 0, 0, tiled=True)
    inputs, near = lax.optimization_barrier((inputs, near))
    other_inputs = other_core(inputs)
    left = passed(far, 0, 1)
    rows = FEATURES * 3 // 2 // lons
    slices, upward = call(
        product_kernel,
        (struct((lons, rows, 128), BF16), struct((2, 3, 16, FEATURES), BF16)),
        places={0: pltpu.SMEM},
    )(core, blocks, inputs, other_inputs, near, left)
    above = passed(upward, 1, 0)
    grad_input = call(join_kernel, struct((1, 2, 6, 12, FEATURES), BF16))(near, left, above)
    slices = lax.all_to_all(slices, "lon", 0, 0, tiled=True)
    grad_qkv = call(
        sum_kernel, struct((1, FEATURES // lons, 192), F32), places={0: pltpu.SMEM}
    )(core, slices)
    return grad_input, grad_qkv.transpose(0, 2, 1)


def solution(mesh):
    in_specs = (
        P("phase", None, "lat", "lon", None),
        P("phase", None, "lat", "lon", None),
        P("phase", None, None),
        P("phase", None, None),
        P("phase", None),
        P("phase", None, None),
        P("lat"),
    )
    out_specs = (P("phase", None, "lat", "lon", None), P("phase", "lat", "lon"))
    return jax.shard_map(
        per_device, mesh=mesh, in_specs=in_specs, out_specs=out_specs, check_vma=False
    )
```

```python
import functools

import jax
import jax.numpy as jnp
from jax import lax
from jax.experimental import pallas as pl
from jax.experimental.pallas import tpu as pltpu
from jax.sharding import PartitionSpec as P

F32 = jnp.float32
BF16 = jnp.bfloat16
HEADS = 8
FEATURES = 512
EPSILON = 1e-05
MASKED = -1e30
SCORE_SCALE = 0.125
MIB = 1024 * 1024

LEVEL_ROWS = 96
ROWS = 192
PACKED_ROWS = 144


def call(kernel, out_shape, scratch=(), places=(), out_places=(), cost=None, limit=50 * MIB):
    def run(*args):
        places_of = dict(places)
        specs = [
            pl.BlockSpec(memory_space=places_of.get(i, pltpu.VMEM)) for i in range(len(args))
        ]
        outs_of = dict(out_places)
        outs = [
            pl.BlockSpec(memory_space=outs_of.get(i, pltpu.VMEM))
            for i in range(len(jax.tree.leaves(out_shape)))
        ]
        outs = tuple(outs) if isinstance(out_shape, tuple) else outs[0]
        return pl.pallas_call(
            kernel,
            out_shape=out_shape,
            in_specs=specs,
            out_specs=outs,
            scratch_shapes=list(scratch),
            cost_estimate=cost,
            compiler_params=pltpu.CompilerParams(vmem_limit_bytes=limit),
        )(*args)

    return run


def struct(shape, dtype):
    return jax.ShapeDtypeStruct(shape, dtype)


def dot(left, right, dims=((1,), (0,))):
    return lax.dot_general(left, right, (dims, ((), ())), preferred_element_type=F32)


def row_index(shape, dim):
    return lax.broadcasted_iota(jnp.int32, shape, dim)


def cut_kernel(labels_ref, x_ref, g_ref, own, lon, lat, cor, labels, x_rows, g_rows, sem, sems):
    fetch = pltpu.make_async_copy(labels_ref, labels, sem)
    fetch.start()
    fetches = []
    for i in range(6):
        fetches.append(pltpu.make_async_copy(x_ref.at[i], x_rows.at[i], sems.at[0, i]))
        fetches.append(pltpu.make_async_copy(g_ref.at[i], g_rows.at[i], sems.at[1, i]))
    for copy in fetches:
        copy.start()
    row = row_index((8, FEATURES), 0)

    def halves(field, level, fill):
        low, high = field[0:8, level, :], field[4:12, level, :]
        return (
            jnp.where(row < 6, low, fill),
            jnp.where(row < 6, pltpu.roll(high, 6, 0), fill),
        )

    fetch.wait()
    for i in range(6):
        label = labels[i].astype(F32)
        fetches[2 * i].wait()
        fetches[2 * i + 1].wait()
        x, g = x_rows[i].astype(F32), g_rows[i].astype(F32)
        for level in range(2):
            x_low, x_high = halves(x, level, label)
            g_low, g_high = halves(g, level, 0.0)
            low = jnp.concatenate([x_low, g_low], axis=0).astype(BF16)
            high = jnp.concatenate([x_high, g_high], axis=0).astype(BF16)
            if i < 3:
                cor[level, i] = low
                lat[level, i] = high
            else:
                lon[level, i - 3] = low
                own[level, i - 3] = high


def bias_kernel(table, out):
    parts = []
    for h in range(HEADS):
        line = jnp.broadcast_to(table[h : h + 1, :], (8, 256))
        parts.append(pltpu.roll(line, 0, 1, stride=1, stride_axis=0))
        parts.append(pltpu.roll(line, 6, 1, stride=1, stride_axis=0))
    shifted = jnp.concatenate(parts, axis=0)
    source = row_index((256, 256), 0)
    lane = row_index((256, 256), 1)
    column = lane & 7
    target = (lane >> 4) * 23 + ((lane >> 3) & 1) * 6 + column + 11
    picked = jnp.where((source == target) & (column < 6), 1.0, 0.0).astype(BF16)
    first = shifted.astype(BF16)
    rest = shifted - first.astype(F32)
    second = rest.astype(BF16)
    third = (rest - second.astype(F32)).astype(BF16)
    spread = dot(first, picked) + dot(second, picked) + dot(third, picked)
    empty = (row_index((128, 128), 0) & 7) >= 6
    for b in range(6):
        shift = (256 - (5 - b) * 16) % 256
        moved = spread if shift == 0 else pltpu.roll(spread, shift, 1)
        moved = jnp.where(empty, MASKED, moved[:, :128])
        for h in range(HEADS):
            out[h * 96 + b * 16 : h * 96 + b * 16 + 16, :] = moved[h * 16 : h * 16 + 16, :]


def pack_rows(array):
    columns = array.shape[1]
    groups = array.reshape(6, 4, 8, columns)
    row = row_index((8, columns), 0)
    out = []
    for q in range(6):
        last = groups[q, 3]
        for g in range(3):
            out.append(jnp.where(row < 6, groups[q, g], pltpu.roll(last, 6 - 2 * g, 0)))
    return jnp.concatenate(out, axis=0)


def per_head(pair):
    even = row_index(pair.shape, 1) < 64
    wide = pair.astype(F32)
    return jnp.concatenate(
        [jnp.where(even, wide, 0.0).astype(BF16), jnp.where(even, 0.0, wide).astype(BF16)], axis=0
    )


def attention_backward(att, d_low, projected, dqkv):
    lane = row_index((LEVEL_ROWS, 128), 1)
    for level in range(2):
        rows = slice(level * LEVEL_ROWS, (level + 1) * LEVEL_ROWS)
        for pair in range(4):
            cols = slice(pair * 128, (pair + 1) * 128)
            probs = att(level, pair)
            probs_low = probs.astype(BF16).reshape(2 * LEVEL_ROWS, LEVEL_ROWS)
            d_out = d_low[rows, cols]
            query = projected[rows, cols]
            keys = per_head(projected[rows, 512 + pair * 128 : 512 + (pair + 1) * 128])
            values = per_head(projected[rows, 1024 + pair * 128 : 1024 + (pair + 1) * 128])
            d_probs = dot(values, d_out, ((1,), (1,))).reshape(2, LEVEL_ROWS, LEVEL_ROWS)
            inner = jnp.sum(probs * d_probs, axis=1, keepdims=True)
            d_scores = (probs * (d_probs - inner)).astype(BF16).reshape(2 * LEVEL_ROWS, LEVEL_ROWS)
            d_value = dot(probs_low, d_out)
            d_key = dot(d_scores, query)
            d_query = dot(d_scores, keys, ((0,), (0,)))
            dqkv[rows, pair * 128 : (pair + 1) * 128] = (d_query * SCORE_SCALE).astype(BF16)
            dqkv[rows, 512 + pair * 128 : 512 + (pair + 1) * 128] = (
                jnp.where(lane < 64, d_key[:LEVEL_ROWS], d_key[LEVEL_ROWS:]) * SCORE_SCALE
            ).astype(BF16)
            dqkv[rows, 1024 + pair * 128 : 1024 + (pair + 1) * 128] = jnp.where(
                lane < 64, d_value[:LEVEL_ROWS], d_value[LEVEL_ROWS:]
            ).astype(BF16)


def input_gradient(dqkv, w_qkv, gain, normed, inv_std):
    d_normed = dot(dqkv[...], w_qkv[...]) * gain[...]
    mean_plain = jnp.mean(d_normed, axis=-1, keepdims=True)
    mean_normed = jnp.mean(d_normed * normed, axis=-1, keepdims=True)
    return inv_std * (d_normed - mean_plain - normed * mean_normed)


def normalised(x):
    center = jnp.mean(x, axis=-1, keepdims=True)
    moved = x - center
    spread = jnp.mean(jnp.square(moved), axis=-1, keepdims=True)
    inv_std = lax.rsqrt(spread + EPSILON)
    return moved * inv_std, inv_std


def first_kernel(
    own, lon, lat, cor, w_qkv_ref, w_proj, gain, bias,
    skip, inputs, fields, projected_out, att_out,
    dqkv, w_qkv, sem,
):
    fetch = pltpu.make_async_copy(w_qkv_ref, w_qkv, sem)
    fetch.start()
    tiles_x, tiles_g = [], []
    labels = []
    row = row_index((8, FEATURES), 0)
    for level in range(2):
        for i in range(6):
            left, right = (own, lon) if i < 3 else (lat, cor)
            left, right = left[level, i % 3].astype(F32), right[level, i % 3].astype(F32)
            if level == 0:
                labels.append(left[6:7, :128])
            for tile in (left, right):
                tiles_x.append(jnp.where(row < 6, tile[:8], 0.0))
                tiles_g.append(tile[8:])
    x = jnp.concatenate(tiles_x, axis=0)
    c = jnp.concatenate(tiles_g, axis=0)
    normed, inv_std = normalised(x)
    scaled = normed * gain[...]
    packed = pack_rows(scaled).astype(BF16)
    inputs[...] = packed
    fetch.wait()
    projected = dot(scaled.astype(BF16), w_qkv[...], ((1,), (1,)))
    c_low = c.astype(BF16)
    d_first_value = dot(c_low, w_proj[...])
    fields[0] = x.astype(BF16)
    fields[1] = c_low
    projected_out[...] = projected.astype(BF16)

    lane_row = row_index((1, 128), 1) >> 4
    along = labels[0]
    for b in range(1, 6):
        along = jnp.where(lane_row == b, labels[b], along)
    allowed = jnp.concatenate(
        [
            jnp.broadcast_to(jnp.where(labels[b] == along, 0.0, MASKED), (16, 128))
            for b in range(6)
        ],
        axis=0,
    )

    def probabilities(level, pair):
        rows = slice(level * LEVEL_ROWS, (level + 1) * LEVEL_ROWS)
        cols = slice(pair * 128, (pair + 1) * 128)
        added = bias[pair * 192 : (pair + 1) * 192, :].reshape(2, LEVEL_ROWS, 128) + allowed[None]
        keys = per_head(projected_out[rows, 512 + pair * 128 : 512 + (pair + 1) * 128])
        scores = dot(keys, projected_out[rows, cols], ((1,), (1,))).reshape(2, LEVEL_ROWS, LEVEL_ROWS)
        scores = scores * SCORE_SCALE + added[:, :, :LEVEL_ROWS]
        weights = jnp.exp(scores - jnp.max(scores, axis=1, keepdims=True))
        probs = weights * (1.0 / jnp.sum(weights, axis=1, keepdims=True))
        att_out[level, pair] = probs.astype(BF16)
        return probs

    attention_backward(probabilities, d_first_value.astype(BF16), projected_out, dqkv)
    skip[...] = (c + input_gradient(dqkv, w_qkv, gain, normed, inv_std)).astype(BF16)


def second_kernel(
    arrived, fields, projected, att, w_proj, w_qkv_ref, gain,
    blocks, kept, up, dqkv, w_qkv, sem,
):
    fetch = pltpu.make_async_copy(w_qkv_ref, w_qkv, sem)
    fetch.start()
    d_low = (dot(fields[1], w_proj[...]) + dot(arrived[...], w_proj[...])).astype(BF16)
    attention_backward(lambda level, pair: att[level, pair].astype(F32), d_low, projected, dqkv)
    lane = row_index((80, 128), 1)
    for t in range(4):
        whole = [
            pack_rows(dqkv[:, 384 * t + 128 * j : 384 * t + 128 * (j + 1)].astype(F32))
            for j in range(3)
        ]
        blocks[2 * t, :144, :] = whole[0].astype(BF16)
        blocks[2 * t + 1, :144, :] = whole[2].astype(BF16)
        top = whole[1][:80]
        bottom = jnp.concatenate([whole[1][80:], jnp.zeros((16, 128), F32)], axis=0)
        blocks[2 * t, 144:, :] = jnp.where(lane < 64, top, pltpu.roll(bottom, 64, 1)).astype(BF16)
        blocks[2 * t + 1, 144:, :] = jnp.where(lane < 64, pltpu.roll(top, 64, 1), bottom).astype(
            BF16
        )
    normed, inv_std = normalised(fields[0].astype(F32))
    fetch.wait()
    shifted = input_gradient(dqkv, w_qkv, gain, normed, inv_std)
    total = fields[1].astype(F32) + (arrived[...].astype(F32) + shifted)
    for i in range(6):
        for half in range(2):
            start = 16 * i + 8 * half
            both = jnp.concatenate(
                [total[start : start + 8], total[96 + start : 96 + start + 8]], axis=0
            )
            (kept, up)[i // 3][half, i % 3] = both.astype(BF16)


def stack_kernel(a, b, c, d, kept, low, high):
    low[0], low[1], high[0], high[1] = a[...], b[...], c[...], d[...]


def product_kernel(
    lat_index, blocks, low, high, other_low, other_high, kept, above, out, sideways
):
    whole = jnp.zeros((128, FEATURES), F32)
    upper = jnp.zeros((128, FEATURES), F32)
    lower = jnp.zeros((128, FEATURES), F32)
    lats = blocks.shape[0]
    for x in range(lats // 2):
        inputs, other_inputs = (low, other_low) if x < 2 else (high, other_high)
        first = lat_index[0] + 2 * x
        first = jnp.where(first >= lats, first - lats, first)
        second = first + 1 - 2 * lax.rem(lat_index[0], 2)
        for cells, place in ((inputs, first), (other_inputs, second)):
            whole += dot(blocks[place, :144, :], cells[x % 2], ((0,), (0,)))
            folded = blocks[place, 144:, :]
            upper += dot(folded, cells[x % 2, :80, :], ((0,), (0,)))
            lower += dot(folded[:64], cells[x % 2, 80:, :], ((0,), (0,)))
    half = upper[:64] + lower[64:]
    whole_t = whole.T
    half_t = jnp.concatenate([half, jnp.zeros((64, FEATURES), F32)], axis=0).T
    bands = out.shape[0]
    width = FEATURES // bands
    lane = row_index((width // 2, 128), 1)
    for band in range(bands):
        out[band, :width, :] = whole_t[band * width : (band + 1) * width].astype(BF16)
        part = half_t[band * width : (band + 1) * width]
        out[band, width:, :] = jnp.where(
            lane < 64, part[: width // 2], pltpu.roll(part[width // 2 :], 64, 1)
        ).astype(BF16)
    for i in range(3):
        sideways[i] = above[1, i]
        sideways[3 + i] = kept[1, i]


def sum_kernel(lat_index, parts, out):
    bands, rows, _ = parts.shape
    width = rows * 2 // 3
    total = parts[0].astype(F32)
    for band in range(1, bands):
        total = total + parts[band].astype(F32)
    whole = total[:width]
    folded = total[width:]
    half = jnp.concatenate([folded, pltpu.roll(folded, 64, 1)], axis=0)
    half = half[:, :64]

    @pl.when(lax.rem(lat_index[0], 2) == 0)
    def _():
        out[0, :, :128] = whole
        out[0, :, 128:] = half

    @pl.when(lax.rem(lat_index[0], 2) == 1)
    def _():
        out[0, :, :64] = half
        out[0, :, 64:] = whole


def join_kernel(kept, above, left, out):
    row = row_index((8, FEATURES), 0)
    for level in range(2):
        part = slice(level * 8, level * 8 + 8)
        for i in range(6):
            low, high = left[i], above[0, i] if i < 3 else kept[0, i - 3]
            low = low.astype(F32)[part]
            high = pltpu.roll(high.astype(F32)[part], 6, 0)
            out[0, level, i, 0:8, :] = jnp.where(row < 6, low, high).astype(BF16)
            out[0, level, i, 8:12, :] = high[:4].astype(BF16)


def passed(array, lat_by, lon_by):
    lats, lons = lax.axis_size("lat"), lax.axis_size("lon")
    pairs = [
        (a * lons + o, ((a + lat_by) % lats) * lons + (o + lon_by) % lons)
        for a in range(lats)
        for o in range(lons)
    ]
    return lax.ppermute(array, ("lat", "lon"), pairs)


def other_core(array):
    return lax.ppermute(array, "lat", [(a, a ^ 1) for a in range(lax.axis_size("lat"))])


def per_device(x_in, out_grad, w_qkv, w_proj, norm_gain, bias_table, lat_labels):
    lats, lons = lax.axis_size("lat"), lax.axis_size("lon")
    w_qkv, w_proj = w_qkv[0], w_proj[0]
    piece = struct((2, 3, 16, FEATURES), BF16)
    own, lon, lat, cor = call(
        cut_kernel,
        (piece,) * 4,
        [
            pltpu.SMEM(lat_labels.shape, jnp.int32),
            pltpu.VMEM((6, 12, 2, FEATURES), BF16),
            pltpu.VMEM((6, 12, 2, FEATURES), BF16),
            pltpu.SemaphoreType.DMA,
            pltpu.SemaphoreType.DMA((2, 6)),
        ],
        places={0: pl.ANY, 1: pl.ANY, 2: pl.ANY},
        limit=58 * MIB,
    )(lat_labels, x_in[0].transpose(1, 2, 0, 3), out_grad[0].transpose(1, 2, 0, 3))
    lon = passed(lon, 0, -1)
    lat = passed(lat, -1, 0)
    cor = passed(cor, -1, -1)
    table = jnp.pad(bias_table[0, :, 253:506], ((0, 0), (0, 3)))
    bias = call(
        bias_kernel,
        struct((HEADS * LEVEL_ROWS, 128), F32),
        cost=pl.CostEstimate(flops=4_000_000_000, bytes_accessed=20_000_000, transcendentals=0),
    )(table)

    scratch = [
        pltpu.VMEM((ROWS, 3 * FEATURES), BF16),
        pltpu.VMEM(w_qkv.shape, BF16),
        pltpu.SemaphoreType.DMA,
    ]
    skip, inputs, fields, projected, att = call(
        first_kernel,
        (
            struct((ROWS, FEATURES), BF16),
            struct((PACKED_ROWS, FEATURES), BF16),
            struct((2, ROWS, FEATURES), BF16),
            struct((ROWS, 3 * FEATURES), BF16),
            struct((2, 4, 2, LEVEL_ROWS, LEVEL_ROWS), BF16),
        ),
        scratch,
        places={4: pl.ANY},
    )(own, lon, lat, cor, w_qkv, w_proj, norm_gain, bias)

    lat_index = lax.axis_index("lat").astype(jnp.int32).reshape(1)
    arrived = lax.ppermute(skip, "phase", [(1, 0)])
    along = [inputs] + [passed(inputs, -2 * x, 0) for x in range(1, lats // 2)]
    back = struct((2, 3, 16, FEATURES), BF16)
    blocks, kept, up = call(
        second_kernel,
        (struct((lats, 224, 128), BF16), back, back),
        scratch,
        places={5: pl.ANY},
        cost=pl.CostEstimate(flops=4_000_000_000, bytes_accessed=20_000_000, transcendentals=0),
    )(arrived, fields, projected, att, w_proj, w_qkv, norm_gain)
    blocks = lax.all_to_all(blocks, "lat", 0, 0, tiled=True)
    two = struct((2, PACKED_ROWS, FEATURES), BF16)
    low, high = call(stack_kernel, (two, two), places={4: pl.ANY})(*along, kept)
    other_low, other_high = other_core(low), other_core(high)
    above = passed(up, 1, 0)
    rows = FEATURES * 3 // 2 // lons
    slices, sideways = call(
        product_kernel,
        (struct((lons, rows, 128), BF16), struct((6, 16, FEATURES), BF16)),
        places={0: pltpu.SMEM},
    )(lat_index, blocks, low, high, other_low, other_high, kept, above)
    left = passed(sideways, 0, 1)
    grad_input = call(join_kernel, struct((1, 2, 6, 12, FEATURES), BF16))(kept, above, left)
    slices = lax.all_to_all(slices, "lon", 0, 0, tiled=True)
    grad_qkv = call(
        sum_kernel, struct((1, FEATURES // lons, 192), F32), places={0: pltpu.SMEM}
    )(lat_index, slices)
    return grad_input, grad_qkv.transpose(0, 2, 1)


def solution(mesh):
    in_specs = (
        P("phase", None, "lat", "lon", None),
        P("phase", None, "lat", "lon", None),
        P("phase", None, None),
        P("phase", None, None),
        P("phase", None),
        P("phase", None, None),
        P("lat"),
    )
    out_specs = (P("phase", None, "lat", "lon", None), P("phase", "lat", "lon"))
    return jax.shard_map(
        per_device, mesh=mesh, in_specs=in_specs, out_specs=out_specs, check_vma=False
    )
```

```python
import functools

import jax
import jax.numpy as jnp
from jax import lax
from jax.experimental import pallas as pl
from jax.experimental.pallas import tpu as pltpu
from jax.sharding import PartitionSpec as P

F32 = jnp.float32
BF16 = jnp.bfloat16
HEADS = 8
FEATURES = 512
EPSILON = 1e-05
MASKED = -1e30
SCORE_SCALE = 0.125
MIB = 1024 * 1024

LEVEL_ROWS = 96
ROWS = 192
PACKED_ROWS = 144


def call(kernel, out_shape, scratch=(), places=(), out_places=(), cost=None, limit=50 * MIB):
    def run(*args):
        places_of = dict(places)
        specs = [
            pl.BlockSpec(memory_space=places_of.get(i, pltpu.VMEM)) for i in range(len(args))
        ]
        outs_of = dict(out_places)
        outs = [
            pl.BlockSpec(memory_space=outs_of.get(i, pltpu.VMEM))
            for i in range(len(jax.tree.leaves(out_shape)))
        ]
        outs = tuple(outs) if isinstance(out_shape, tuple) else outs[0]
        return pl.pallas_call(
            kernel,
            out_shape=out_shape,
            in_specs=specs,
            out_specs=outs,
            scratch_shapes=list(scratch),
            cost_estimate=cost,
            compiler_params=pltpu.CompilerParams(vmem_limit_bytes=limit),
        )(*args)

    return run


def struct(shape, dtype):
    return jax.ShapeDtypeStruct(shape, dtype)


def dot(left, right, dims=((1,), (0,))):
    return lax.dot_general(left, right, (dims, ((), ())), preferred_element_type=F32)


def row_index(shape, dim):
    return lax.broadcasted_iota(jnp.int32, shape, dim)


def pack(tiles):
    row = row_index(tiles[3].shape, 0)
    return [jnp.where(row < 6, tiles[g], pltpu.roll(tiles[3], 6 - 2 * g, 0)) for g in range(3)]


def unpack(rows):
    tiles = [rows[8 * g : 8 * g + 8] for g in range(3)]
    row = row_index(tiles[0].shape, 0)
    last = jnp.where(row < 2, pltpu.roll(tiles[0], 2, 0), 0.0)
    last = jnp.where((row >= 2) & (row < 4), pltpu.roll(tiles[1], 4, 0), last)
    last = jnp.where((row >= 4) & (row < 6), pltpu.roll(tiles[2], 6, 0), last)
    return [jnp.where(row < 6, tile, 0.0) for tile in tiles] + [last]


def cut_kernel(labels_ref, x_ref, g_ref, own, lon, lat, cor, labels, x_rows, g_rows, sem, sems):
    fetch = pltpu.make_async_copy(labels_ref, labels, sem)
    fetch.start()
    fetches = []
    for i in range(6):
        fetches.append(pltpu.make_async_copy(x_ref.at[i], x_rows.at[i], sems.at[0, i]))
        fetches.append(pltpu.make_async_copy(g_ref.at[i], g_rows.at[i], sems.at[1, i]))
    for copy in fetches:
        copy.start()
    row = row_index((8, FEATURES), 0)

    fetch.wait()
    parts = {}
    marks = [jnp.zeros((8, FEATURES), F32)] * 2
    for i in range(6):
        fetches[2 * i].wait()
        fetches[2 * i + 1].wait()
        fields = x_rows[i].astype(F32), g_rows[i].astype(F32)
        low = [field[0:8, level, :] for field in fields for level in range(2)]
        high = [pltpu.roll(field[4:12, level, :], 6, 0) for field in fields for level in range(2)]
        parts.setdefault((i // 3, 0), []).extend(pack(low))
        parts.setdefault((i // 3, 1), []).extend(pack(high))
        marks[i // 3] = jnp.where(row == i % 3, labels[i].astype(F32), marks[i // 3])
    cor[...] = jnp.concatenate(parts[0, 0] + [marks[0]], axis=0).astype(BF16)
    lat[...] = jnp.concatenate(parts[0, 1], axis=0).astype(BF16)
    lon[...] = jnp.concatenate(parts[1, 0], axis=0).astype(BF16)
    own[...] = jnp.concatenate(parts[1, 1] + [marks[1]], axis=0).astype(BF16)


def bias_kernel(table, out):
    parts = []
    for h in range(HEADS):
        line = jnp.broadcast_to(table[h : h + 1, :], (8, 256))
        parts.append(pltpu.roll(line, 0, 1, stride=1, stride_axis=0))
        parts.append(pltpu.roll(line, 6, 1, stride=1, stride_axis=0))
    shifted = jnp.concatenate(parts, axis=0)
    source = row_index((256, 256), 0)
    lane = row_index((256, 256), 1)
    column = lane & 7
    target = (lane >> 4) * 23 + ((lane >> 3) & 1) * 6 + column + 11
    picked = jnp.where((source == target) & (column < 6), 1.0, 0.0).astype(BF16)
    first = shifted.astype(BF16)
    rest = shifted - first.astype(F32)
    second = rest.astype(BF16)
    third = (rest - second.astype(F32)).astype(BF16)
    spread = dot(first, picked) + dot(second, picked) + dot(third, picked)
    empty = (row_index((128, 128), 0) & 7) >= 6
    for b in range(6):
        shift = (256 - (5 - b) * 16) % 256
        moved = spread if shift == 0 else pltpu.roll(spread, shift, 1)
        moved = jnp.where(empty, MASKED, moved[:, :128])
        for h in range(HEADS):
            out[h * 96 + b * 16 : h * 96 + b * 16 + 16, :] = moved[h * 16 : h * 16 + 16, :]


def pack_rows(array):
    columns = array.shape[1]
    groups = array.reshape(6, 4, 8, columns)
    row = row_index((8, columns), 0)
    out = []
    for q in range(6):
        last = groups[q, 3]
        for g in range(3):
            out.append(jnp.where(row < 6, groups[q, g], pltpu.roll(last, 6 - 2 * g, 0)))
    return jnp.concatenate(out, axis=0)


def per_head(pair):
    even = row_index(pair.shape, 1) < 64
    wide = pair.astype(F32)
    return jnp.concatenate(
        [jnp.where(even, wide, 0.0).astype(BF16), jnp.where(even, 0.0, wide).astype(BF16)], axis=0
    )


def attention_backward(att, d_low, projected, dqkv):
    lane = row_index((LEVEL_ROWS, 128), 1)
    for level in range(2):
        rows = slice(level * LEVEL_ROWS, (level + 1) * LEVEL_ROWS)
        for pair in range(4):
            cols = slice(pair * 128, (pair + 1) * 128)
            probs = att(level, pair)
            probs_low = probs.astype(BF16).reshape(2 * LEVEL_ROWS, LEVEL_ROWS)
            d_out = d_low[rows, cols]
            query = projected[rows, cols]
            keys = per_head(projected[rows, 512 + pair * 128 : 512 + (pair + 1) * 128])
            values = per_head(projected[rows, 1024 + pair * 128 : 1024 + (pair + 1) * 128])
            d_probs = dot(values, d_out, ((1,), (1,))).reshape(2, LEVEL_ROWS, LEVEL_ROWS)
            inner = jnp.sum(probs * d_probs, axis=1, keepdims=True)
            d_scores = (probs * (d_probs - inner)).astype(BF16).reshape(2 * LEVEL_ROWS, LEVEL_ROWS)
            d_value = dot(probs_low, d_out)
            d_key = dot(d_scores, query)
            d_query = dot(d_scores, keys, ((0,), (0,)))
            dqkv[rows, pair * 128 : (pair + 1) * 128] = (d_query * SCORE_SCALE).astype(BF16)
            dqkv[rows, 512 + pair * 128 : 512 + (pair + 1) * 128] = (
                jnp.where(lane < 64, d_key[:LEVEL_ROWS], d_key[LEVEL_ROWS:]) * SCORE_SCALE
            ).astype(BF16)
            dqkv[rows, 1024 + pair * 128 : 1024 + (pair + 1) * 128] = jnp.where(
                lane < 64, d_value[:LEVEL_ROWS], d_value[LEVEL_ROWS:]
            ).astype(BF16)


def input_gradient(dqkv, w_qkv, gain, normed, inv_std):
    d_normed = dot(dqkv[...], w_qkv[...]) * gain[...]
    mean_plain = jnp.mean(d_normed, axis=-1, keepdims=True)
    mean_normed = jnp.mean(d_normed * normed, axis=-1, keepdims=True)
    return inv_std * (d_normed - mean_plain - normed * mean_normed)


def normalised(x):
    center = jnp.mean(x, axis=-1, keepdims=True)
    moved = x - center
    spread = jnp.mean(jnp.square(moved), axis=-1, keepdims=True)
    inv_std = lax.rsqrt(spread + EPSILON)
    return moved * inv_std, inv_std


def first_kernel(
    own, lon, lat, cor, w_qkv_ref, w_proj, gain, bias,
    skip, inputs, fields, projected_out, att_out,
    dqkv, w_qkv, sems,
):
    thirds = [slice(FEATURES * j, FEATURES * (j + 1)) for j in range(3)]
    fetches = [
        pltpu.make_async_copy(w_qkv_ref.at[third], w_qkv.at[third], sems.at[j])
        for j, third in enumerate(thirds)
    ]
    for copy in fetches:
        copy.start()
    labels = []
    tiles = {}
    for upper, (left, right) in enumerate(((own, lon), (lat, cor))):
        left, right = left[...].astype(F32), right[...].astype(F32)
        marked = right if upper else left
        labels.extend(marked[72 + i : 73 + i, :128] for i in range(3))
        for i in range(3):
            for half, piece in ((0, left), (1, right)):
                found = unpack(piece[24 * i : 24 * i + 24])
                for k in range(4):
                    tiles[k // 2, k % 2, 3 * upper + i, half] = found[k]
    order = [(level, i, half) for level in range(2) for i in range(6) for half in range(2)]
    tiles_x, tiles_g = ([tiles[(field,) + place] for place in order] for field in range(2))
    x = jnp.concatenate(tiles_x, axis=0)
    c = jnp.concatenate(tiles_g, axis=0)
    normed, inv_std = normalised(x)
    scaled = normed * gain[...]
    inputs[...] = pack_rows(scaled).astype(BF16)
    c_low = c.astype(BF16)
    d_low = dot(c_low, w_proj[...]).astype(BF16)
    fields[0] = x.astype(BF16)
    fields[1] = c_low
    scaled_low = scaled.astype(BF16)
    for copy, third in zip(fetches, thirds):
        copy.wait()
        projected_out[:, third] = dot(scaled_low, w_qkv[third, :], ((1,), (1,))).astype(BF16)

    lane_row = row_index((1, 128), 1) >> 4
    along = labels[0]
    for b in range(1, 6):
        along = jnp.where(lane_row == b, labels[b], along)
    allowed = jnp.concatenate(
        [
            jnp.broadcast_to(jnp.where(labels[b] == along, 0.0, MASKED), (16, 128))
            for b in range(6)
        ],
        axis=0,
    )

    def probabilities(level, pair):
        rows = slice(level * LEVEL_ROWS, (level + 1) * LEVEL_ROWS)
        cols = slice(pair * 128, (pair + 1) * 128)
        added = bias[pair * 192 : (pair + 1) * 192, :].reshape(2, LEVEL_ROWS, 128) + allowed[None]
        keys = per_head(projected_out[rows, 512 + pair * 128 : 512 + (pair + 1) * 128])
        scores = dot(keys, projected_out[rows, cols], ((1,), (1,))).reshape(2, LEVEL_ROWS, LEVEL_ROWS)
        scores = scores * SCORE_SCALE + added[:, :, :LEVEL_ROWS]
        weights = jnp.exp(scores - jnp.max(scores, axis=1, keepdims=True))
        probs = weights * (1.0 / jnp.sum(weights, axis=1, keepdims=True))
        att_out[level, pair] = probs.astype(BF16)
        return probs

    attention_backward(probabilities, d_low, projected_out, dqkv)
    skip[...] = (c + input_gradient(dqkv, w_qkv, gain, normed, inv_std)).astype(BF16)


def second_kernel(
    arrived, fields, projected, att, w_proj, w_qkv_ref, gain,
    blocks, kept, up, dqkv, w_qkv, sem,
):
    fetch = pltpu.make_async_copy(w_qkv_ref, w_qkv, sem)
    fetch.start()
    d_low = (dot(fields[1], w_proj[...]) + dot(arrived[...], w_proj[...])).astype(BF16)
    attention_backward(lambda level, pair: att[level, pair].astype(F32), d_low, projected, dqkv)
    lane = row_index((80, 128), 1)
    for t in range(4):
        whole = [
            pack_rows(dqkv[:, 384 * t + 128 * j : 384 * t + 128 * (j + 1)].astype(F32))
            for j in range(3)
        ]
        blocks[2 * t, :144, :] = whole[0].astype(BF16)
        blocks[2 * t + 1, :144, :] = whole[2].astype(BF16)
        top = whole[1][:80]
        bottom = jnp.concatenate([whole[1][80:], jnp.zeros((16, 128), F32)], axis=0)
        blocks[2 * t, 144:, :] = jnp.where(lane < 64, top, pltpu.roll(bottom, 64, 1)).astype(BF16)
        blocks[2 * t + 1, 144:, :] = jnp.where(lane < 64, pltpu.roll(top, 64, 1), bottom).astype(
            BF16
        )
    normed, inv_std = normalised(fields[0].astype(F32))
    fetch.wait()
    shifted = input_gradient(dqkv, w_qkv, gain, normed, inv_std)
    total = fields[1].astype(F32) + (arrived[...].astype(F32) + shifted)
    for target, first in ((kept, 0), (up, 3)):
        parts = []
        for i in range(first, first + 3):
            starts = [96 * level + 16 * i + 8 * half for half in range(2) for level in range(2)]
            parts.extend(pack([total[start : start + 8] for start in starts]))
        target[...] = jnp.concatenate(parts, axis=0).astype(BF16)


def stack_kernel(a, b, c, d, kept, low, high):
    low[0], low[1], high[0], high[1] = a[...], b[...], c[...], d[...]


def product_kernel(
    lat_index, blocks, low, high, other_low, other_high, kept, above, out, sideways
):
    whole = jnp.zeros((128, FEATURES), F32)
    upper = jnp.zeros((128, FEATURES), F32)
    lower = jnp.zeros((128, FEATURES), F32)
    lats = blocks.shape[0]
    for x in range(lats // 2):
        inputs, other_inputs = (low, other_low) if x < 2 else (high, other_high)
        first = lat_index[0] + 2 * x
        first = jnp.where(first >= lats, first - lats, first)
        second = first + 1 - 2 * lax.rem(lat_index[0], 2)
        for cells, place in ((inputs, first), (other_inputs, second)):
            whole += dot(blocks[place, :144, :], cells[x % 2], ((0,), (0,)))
            folded = blocks[place, 144:, :]
            upper += dot(folded, cells[x % 2, :80, :], ((0,), (0,)))
            lower += dot(folded[:64], cells[x % 2, 80:, :], ((0,), (0,)))
    half = upper[:64] + lower[64:]
    whole_t = whole.T
    half_t = jnp.concatenate([half, jnp.zeros((64, FEATURES), F32)], axis=0).T
    bands = out.shape[0]
    width = FEATURES // bands
    lane = row_index((width // 2, 128), 1)
    for band in range(bands):
        out[band, :width, :] = whole_t[band * width : (band + 1) * width].astype(BF16)
        part = half_t[band * width : (band + 1) * width]
        out[band, width:, :] = jnp.where(
            lane < 64, part[: width // 2], pltpu.roll(part[width // 2 :], 64, 1)
        ).astype(BF16)
    tiles = []
    for part in (above, kept):
        part = part[...].astype(F32)
        for i in range(3):
            tiles.extend(unpack(part[24 * i : 24 * i + 24])[2:])
    packed = pack(tiles[:4]) + pack(tiles[4:8]) + pack(tiles[8:])
    sideways[...] = jnp.concatenate(packed, axis=0).astype(BF16)


def sum_kernel(lat_index, parts, out):
    bands, rows, _ = parts.shape
    width = rows * 2 // 3
    total = parts[0].astype(F32)
    for band in range(1, bands):
        total = total + parts[band].astype(F32)
    whole = total[:width]
    folded = total[width:]
    half = jnp.concatenate([folded, pltpu.roll(folded, 64, 1)], axis=0)
    half = half[:, :64]

    @pl.when(lax.rem(lat_index[0], 2) == 0)
    def _():
        out[0, :, :128] = whole
        out[0, :, 128:] = half

    @pl.when(lax.rem(lat_index[0], 2) == 1)
    def _():
        out[0, :, :64] = half
        out[0, :, 64:] = whole


def join_kernel(kept, above, left, out):
    row = row_index((8, FEATURES), 0)
    low, high = [], []
    side = left[...].astype(F32)
    for g in range(3):
        low.extend(unpack(side[24 * g : 24 * g + 24]))
    for part in (above, kept):
        part = part[...].astype(F32)
        for i in range(3):
            high.extend(unpack(part[24 * i : 24 * i + 24])[:2])
    for i in range(6):
        for level in range(2):
            moved = pltpu.roll(high[2 * i + level], 6, 0)
            out[0, level, i, 0:8, :] = jnp.where(row < 6, low[2 * i + level], moved).astype(BF16)
            out[0, level, i, 8:12, :] = moved[:4].astype(BF16)


def passed(array, lat_by, lon_by):
    lats, lons = lax.axis_size("lat"), lax.axis_size("lon")
    pairs = [
        (a * lons + o, ((a + lat_by) % lats) * lons + (o + lon_by) % lons)
        for a in range(lats)
        for o in range(lons)
    ]
    return lax.ppermute(array, ("lat", "lon"), pairs)


def other_core(array):
    return lax.ppermute(array, "lat", [(a, a ^ 1) for a in range(lax.axis_size("lat"))])


def per_device(x_in, out_grad, w_qkv, w_proj, norm_gain, bias_table, lat_labels):
    lats, lons = lax.axis_size("lat"), lax.axis_size("lon")
    w_qkv, w_proj = w_qkv[0], w_proj[0]
    part = struct((72, FEATURES), BF16)
    marked = struct((80, FEATURES), BF16)
    own, lon, lat, cor = call(
        cut_kernel,
        (marked, part, part, marked),
        [
            pltpu.SMEM(lat_labels.shape, jnp.int32),
            pltpu.VMEM((6, 12, 2, FEATURES), BF16),
            pltpu.VMEM((6, 12, 2, FEATURES), BF16),
            pltpu.SemaphoreType.DMA,
            pltpu.SemaphoreType.DMA((2, 6)),
        ],
        places={0: pl.ANY, 1: pl.ANY, 2: pl.ANY},
        limit=58 * MIB,
    )(lat_labels, x_in[0].transpose(1, 2, 0, 3), out_grad[0].transpose(1, 2, 0, 3))
    lon = passed(lon, 0, -1)
    lat = passed(lat, -1, 0)
    cor = passed(cor, -1, -1)
    table = jnp.pad(bias_table[0, :, 253:506], ((0, 0), (0, 3)))
    bias = call(
        bias_kernel,
        struct((HEADS * LEVEL_ROWS, 128), F32),
        cost=pl.CostEstimate(flops=4_000_000_000, bytes_accessed=20_000_000, transcendentals=0),
    )(table)

    scratch = [
        pltpu.VMEM((ROWS, 3 * FEATURES), BF16),
        pltpu.VMEM(w_qkv.shape, BF16),
        pltpu.SemaphoreType.DMA,
    ]
    skip, inputs, fields, projected, att = call(
        first_kernel,
        (
            struct((ROWS, FEATURES), BF16),
            struct((PACKED_ROWS, FEATURES), BF16),
            struct((2, ROWS, FEATURES), BF16),
            struct((ROWS, 3 * FEATURES), BF16),
            struct((2, 4, 2, LEVEL_ROWS, LEVEL_ROWS), BF16),
        ),
        scratch[:2] + [pltpu.SemaphoreType.DMA((3,))],
        places={4: pl.ANY},
    )(own, lon, lat, cor, w_qkv, w_proj, norm_gain, bias)

    lat_index = lax.axis_index("lat").astype(jnp.int32).reshape(1)
    arrived = lax.ppermute(skip, "phase", [(1, 0)])
    along = [inputs] + [passed(inputs, -2 * x, 0) for x in range(1, lats // 2)]
    blocks, kept, up = call(
        second_kernel,
        (struct((lats, 224, 128), BF16), part, part),
        scratch,
        places={5: pl.ANY},
        cost=pl.CostEstimate(flops=4_000_000_000, bytes_accessed=20_000_000, transcendentals=0),
    )(arrived, fields, projected, att, w_proj, w_qkv, norm_gain)
    blocks = lax.all_to_all(blocks, "lat", 0, 0, tiled=True)
    two = struct((2, PACKED_ROWS, FEATURES), BF16)
    low, high = call(stack_kernel, (two, two), places={4: pl.ANY})(*along, kept)
    other_low, other_high = other_core(low), other_core(high)
    above = passed(up, 1, 0)
    rows = FEATURES * 3 // 2 // lons
    slices, sideways = call(
        product_kernel,
        (struct((lons, rows, 128), BF16), part),
        places={0: pltpu.SMEM},
    )(lat_index, blocks, low, high, other_low, other_high, kept, above)
    left = passed(sideways, 0, 1)
    grad_input = call(join_kernel, struct((1, 2, 6, 12, FEATURES), BF16))(kept, above, left)
    slices = lax.all_to_all(slices, "lon", 0, 0, tiled=True)
    grad_qkv = call(
        sum_kernel, struct((1, FEATURES // lons, 192), F32), places={0: pltpu.SMEM}
    )(lat_index, slices)
    return grad_input, grad_qkv.transpose(0, 2, 1)


def solution(mesh):
    in_specs = (
        P("phase", None, "lat", "lon", None),
        P("phase", None, "lat", "lon", None),
        P("phase", None, None),
        P("phase", None, None),
        P("phase", None),
        P("phase", None, None),
        P("lat"),
    )
    out_specs = (P("phase", None, "lat", "lon", None), P("phase", "lat", "lon"))
    return jax.shard_map(
        per_device, mesh=mesh, in_specs=in_specs, out_specs=out_specs, check_vma=False
    )
```

```python
import functools

import jax
import jax.numpy as jnp
from jax import lax
from jax.experimental import pallas as pl
from jax.experimental.pallas import tpu as pltpu
from jax.sharding import PartitionSpec as P

F32 = jnp.float32
BF16 = jnp.bfloat16
HEADS = 8
FEATURES = 512
EPSILON = 1e-05
MASKED = -1e30
SCORE_SCALE = 0.125
MIB = 1024 * 1024

LEVEL_ROWS = 96
ROWS = 192
PACKED_ROWS = 144
GROUP = 8


def call(kernel, out_shape, scratch=(), places=(), out_places=(), cost=None, limit=50 * MIB):
    def run(*args):
        places_of = dict(places)
        specs = [
            pl.BlockSpec(memory_space=places_of.get(i, pltpu.VMEM)) for i in range(len(args))
        ]
        outs_of = dict(out_places)
        outs = [
            pl.BlockSpec(memory_space=outs_of.get(i, pltpu.VMEM))
            for i in range(len(jax.tree.leaves(out_shape)))
        ]
        outs = tuple(outs) if isinstance(out_shape, tuple) else outs[0]
        return pl.pallas_call(
            kernel,
            out_shape=out_shape,
            in_specs=specs,
            out_specs=outs,
            scratch_shapes=list(scratch),
            cost_estimate=cost,
            compiler_params=pltpu.CompilerParams(vmem_limit_bytes=limit),
        )(*args)

    return run


def struct(shape, dtype):
    return jax.ShapeDtypeStruct(shape, dtype)


def dot(left, right, dims=((1,), (0,))):
    return lax.dot_general(left, right, (dims, ((), ())), preferred_element_type=F32)


def row_index(shape, dim):
    return lax.broadcasted_iota(jnp.int32, shape, dim)


def pack(tiles):
    row = row_index(tiles[3].shape, 0)
    return [jnp.where(row < 6, tiles[g], pltpu.roll(tiles[3], 6 - 2 * g, 0)) for g in range(3)]


def unpack(rows):
    tiles = [rows[8 * g : 8 * g + 8] for g in range(3)]
    row = row_index(tiles[0].shape, 0)
    last = jnp.where(row < 2, pltpu.roll(tiles[0], 2, 0), 0.0)
    last = jnp.where((row >= 2) & (row < 4), pltpu.roll(tiles[1], 4, 0), last)
    last = jnp.where((row >= 4) & (row < 6), pltpu.roll(tiles[2], 6, 0), last)
    return [jnp.where(row < 6, tile, 0.0) for tile in tiles] + [last]


def cut_kernel(labels_ref, x_ref, g_ref, own, lon, lat, cor, labels, x_rows, g_rows, sem, sems):
    fetch = pltpu.make_async_copy(labels_ref, labels, sem)
    fetch.start()
    fetches = []
    for i in range(6):
        fetches.append(pltpu.make_async_copy(x_ref.at[i], x_rows.at[i], sems.at[0, i]))
        fetches.append(pltpu.make_async_copy(g_ref.at[i], g_rows.at[i], sems.at[1, i]))
    for copy in fetches:
        copy.start()
    row = row_index((8, FEATURES), 0)

    fetch.wait()
    parts = {}
    marks = [jnp.zeros((8, FEATURES), F32)] * 2
    for i in range(6):
        fetches[2 * i].wait()
        fetches[2 * i + 1].wait()
        fields = x_rows[i].astype(F32), g_rows[i].astype(F32)
        low = [field[0:8, level, :] for field in fields for level in range(2)]
        high = [pltpu.roll(field[4:12, level, :], 6, 0) for field in fields for level in range(2)]
        parts.setdefault((i // 3, 0), []).extend(pack(low))
        parts.setdefault((i // 3, 1), []).extend(pack(high))
        marks[i // 3] = jnp.where(row == i % 3, labels[i].astype(F32), marks[i // 3])
    cor[...] = jnp.concatenate(parts[0, 0] + [marks[0]], axis=0).astype(BF16)
    lat[...] = jnp.concatenate(parts[0, 1], axis=0).astype(BF16)
    lon[...] = jnp.concatenate(parts[1, 0], axis=0).astype(BF16)
    own[...] = jnp.concatenate(parts[1, 1] + [marks[1]], axis=0).astype(BF16)


def bias_kernel(table, out):
    parts = []
    for h in range(HEADS):
        line = jnp.broadcast_to(table[h : h + 1, :], (8, 256))
        parts.append(pltpu.roll(line, 0, 1, stride=1, stride_axis=0))
        parts.append(pltpu.roll(line, 6, 1, stride=1, stride_axis=0))
    shifted = jnp.concatenate(parts, axis=0)
    source = row_index((256, 256), 0)
    lane = row_index((256, 256), 1)
    column = lane & 7
    target = (lane >> 4) * 23 + ((lane >> 3) & 1) * 6 + column + 11
    picked = jnp.where((source == target) & (column < 6), 1.0, 0.0).astype(BF16)
    first = shifted.astype(BF16)
    rest = shifted - first.astype(F32)
    second = rest.astype(BF16)
    third = (rest - second.astype(F32)).astype(BF16)
    spread = dot(first, picked) + dot(second, picked) + dot(third, picked)
    empty = (row_index((128, 128), 0) & 7) >= 6
    for b in range(6):
        shift = (256 - (5 - b) * 16) % 256
        moved = spread if shift == 0 else pltpu.roll(spread, shift, 1)
        moved = jnp.where(empty, MASKED, moved[:, :128])
        for h in range(HEADS):
            out[h * 96 + b * 16 : h * 96 + b * 16 + 16, :] = moved[h * 16 : h * 16 + 16, :]


def pack_rows(array):
    columns = array.shape[1]
    groups = array.reshape(6, 4, 8, columns)
    row = row_index((8, columns), 0)
    out = []
    for q in range(6):
        last = groups[q, 3]
        for g in range(3):
            out.append(jnp.where(row < 6, groups[q, g], pltpu.roll(last, 6 - 2 * g, 0)))
    return jnp.concatenate(out, axis=0)


def per_head(pair, factor=1.0):
    even = (row_index(pair.shape, 1) < 64).astype(F32)
    return jnp.concatenate(
        [pair * (even * factor).astype(BF16), pair * ((1.0 - even) * factor).astype(BF16)], axis=0
    )


def attention_backward(att, d_low, projected, dqkv):
    lane = row_index((LEVEL_ROWS, 128), 1)
    units = [(level, pair) for level in range(2) for pair in range(4)]
    for first in range(0, len(units), GROUP):
        group = units[first : first + GROUP]
        places = [
            (slice(level * LEVEL_ROWS, (level + 1) * LEVEL_ROWS), slice(pair * 128, (pair + 1) * 128))
            for level, pair in group
        ]
        probs = att(group)
        d_probs = [
            dot(
                per_head(projected[rows, 1024 + cols.start : 1024 + cols.stop]),
                d_low[rows, cols],
                ((1,), (1,)),
            ).reshape(2, LEVEL_ROWS, LEVEL_ROWS)
            for rows, cols in places
        ]
        d_values = [
            dot(p.astype(BF16).reshape(2 * LEVEL_ROWS, LEVEL_ROWS), d_low[rows, cols])
            for p, (rows, cols) in zip(probs, places)
        ]
        inner = [jnp.sum(p * d, axis=1, keepdims=True) for p, d in zip(probs, d_probs)]
        d_scores = [
            (p * (d - i)).astype(BF16).reshape(2 * LEVEL_ROWS, LEVEL_ROWS)
            for p, d, i in zip(probs, d_probs, inner)
        ]
        d_keys = [dot(d, projected[rows, cols]) for d, (rows, cols) in zip(d_scores, places)]
        d_queries = [
            dot(
                d,
                per_head(projected[rows, 512 + cols.start : 512 + cols.stop], SCORE_SCALE),
                ((0,), (0,)),
            )
            for d, (rows, cols) in zip(d_scores, places)
        ]
        for (rows, cols), d_query, d_key, d_value in zip(places, d_queries, d_keys, d_values):
            dqkv[rows, cols] = d_query.astype(BF16)
            dqkv[rows, 512 + cols.start : 512 + cols.stop] = jnp.where(
                lane < 64, d_key[:LEVEL_ROWS], d_key[LEVEL_ROWS:]
            ).astype(BF16)
            dqkv[rows, 1024 + cols.start : 1024 + cols.stop] = jnp.where(
                lane < 64, d_value[:LEVEL_ROWS], d_value[LEVEL_ROWS:]
            ).astype(BF16)


def input_gradient(dqkv, w_qkv, gain, normed, inv_std):
    d_normed = dot(dqkv[...], w_qkv[...]) * gain[...]
    mean_plain = jnp.mean(d_normed, axis=-1, keepdims=True)
    mean_normed = jnp.mean(d_normed * normed, axis=-1, keepdims=True)
    return inv_std * (d_normed - mean_plain - normed * mean_normed)


def normalised(x):
    center = jnp.mean(x, axis=-1, keepdims=True)
    moved = x - center
    spread = jnp.mean(jnp.square(moved), axis=-1, keepdims=True)
    inv_std = lax.rsqrt(spread + EPSILON)
    return moved * inv_std, inv_std


def first_kernel(
    own, lon, lat, cor, w_qkv_ref, w_proj, gain, bias,
    skip, inputs, fields, projected_out, att_out,
    dqkv, w_qkv, sems,
):
    thirds = [slice(FEATURES * j, FEATURES * (j + 1)) for j in range(3)]
    fetches = [
        pltpu.make_async_copy(w_qkv_ref.at[third], w_qkv.at[third], sems.at[j])
        for j, third in enumerate(thirds)
    ]
    for copy in fetches:
        copy.start()
    labels = []
    tiles = {}
    for upper, (left, right) in enumerate(((own, lon), (lat, cor))):
        left, right = left[...].astype(F32), right[...].astype(F32)
        marked = right if upper else left
        labels.extend(marked[72 + i : 73 + i, :128] for i in range(3))
        for i in range(3):
            for half, piece in ((0, left), (1, right)):
                found = unpack(piece[24 * i : 24 * i + 24])
                for k in range(4):
                    tiles[k // 2, k % 2, 3 * upper + i, half] = found[k]
    order = [(level, i, half) for level in range(2) for i in range(6) for half in range(2)]
    tiles_x, tiles_g = ([tiles[(field,) + place] for place in order] for field in range(2))
    x = jnp.concatenate(tiles_x, axis=0)
    c = jnp.concatenate(tiles_g, axis=0)
    normed, inv_std = normalised(x)
    scaled = normed * gain[...]
    inputs[...] = pack_rows(scaled).astype(BF16)
    c_low = c.astype(BF16)
    d_low = dot(c_low, w_proj[...]).astype(BF16)
    fields[0] = x.astype(BF16)
    fields[1] = c_low
    scaled_low = scaled.astype(BF16)
    for copy, third in zip(fetches, thirds):
        copy.wait()
        projected = dot(scaled_low, w_qkv[third, :], ((1,), (1,)))
        projected_out[:, third] = (projected * (SCORE_SCALE if third.start == 0 else 1.0)).astype(BF16)

    lane_row = row_index((1, 128), 1) >> 4
    along = labels[0]
    for b in range(1, 6):
        along = jnp.where(lane_row == b, labels[b], along)
    allowed = jnp.concatenate(
        [
            jnp.broadcast_to(jnp.where(labels[b] == along, 0.0, MASKED), (16, 128))
            for b in range(6)
        ],
        axis=0,
    )

    def probabilities(group):
        scores = []
        for level, pair in group:
            rows = slice(level * LEVEL_ROWS, (level + 1) * LEVEL_ROWS)
            cols = slice(pair * 128, (pair + 1) * 128)
            keys = per_head(projected_out[rows, 512 + cols.start : 512 + cols.stop])
            score = dot(keys, projected_out[rows, cols], ((1,), (1,)))
            scores.append(score.reshape(2, LEVEL_ROWS, LEVEL_ROWS))
        probs = []
        for (level, pair), score in zip(group, scores):
            added = bias[pair * 192 : (pair + 1) * 192, :].reshape(2, LEVEL_ROWS, 128) + allowed[None]
            score = score + added[:, :, :LEVEL_ROWS]
            weights = jnp.exp(score - jnp.max(score, axis=1, keepdims=True))
            probs.append(weights * (1.0 / jnp.sum(weights, axis=1, keepdims=True)))
        for (level, pair), prob in zip(group, probs):
            att_out[level, pair] = prob.astype(BF16)
        return probs

    attention_backward(probabilities, d_low, projected_out, dqkv)
    skip[...] = (c + input_gradient(dqkv, w_qkv, gain, normed, inv_std)).astype(BF16)


def second_kernel(
    arrived, fields, projected, att, w_proj, w_qkv_ref, gain,
    blocks, kept, up, dqkv, w_qkv, sem,
):
    fetch = pltpu.make_async_copy(w_qkv_ref, w_qkv, sem)
    fetch.start()
    d_low = (dot(fields[1], w_proj[...]) + dot(arrived[...], w_proj[...])).astype(BF16)
    attention_backward(
        lambda group: [att[level, pair].astype(F32) for level, pair in group], d_low, projected, dqkv
    )
    lane = row_index((80, 128), 1)
    for t in range(4):
        whole = [
            pack_rows(dqkv[:, 384 * t + 128 * j : 384 * t + 128 * (j + 1)].astype(F32))
            for j in range(3)
        ]
        blocks[2 * t, :144, :] = whole[0].astype(BF16)
        blocks[2 * t + 1, :144, :] = whole[2].astype(BF16)
        top = whole[1][:80]
        bottom = jnp.concatenate([whole[1][80:], jnp.zeros((16, 128), F32)], axis=0)
        blocks[2 * t, 144:, :] = jnp.where(lane < 64, top, pltpu.roll(bottom, 64, 1)).astype(BF16)
        blocks[2 * t + 1, 144:, :] = jnp.where(lane < 64, pltpu.roll(top, 64, 1), bottom).astype(
            BF16
        )
    normed, inv_std = normalised(fields[0].astype(F32))
    fetch.wait()
    shifted = input_gradient(dqkv, w_qkv, gain, normed, inv_std)
    total = fields[1].astype(F32) + (arrived[...].astype(F32) + shifted)
    for target, first in ((kept, 0), (up, 3)):
        parts = []
        for i in range(first, first + 3):
            starts = [96 * level + 16 * i + 8 * half for half in range(2) for level in range(2)]
            parts.extend(pack([total[start : start + 8] for start in starts]))
        target[...] = jnp.concatenate(parts, axis=0).astype(BF16)


def stack_kernel(a, b, c, d, kept, low, high):
    low[0], low[1], high[0], high[1] = a[...], b[...], c[...], d[...]


def product_kernel(
    lat_index, blocks, low, high, other_low, other_high, kept, above, out, sideways
):
    lats = blocks.shape[0]

    def columns(place):
        folded = blocks[place, 144:, :]
        bottom = pltpu.roll(folded[:64].astype(F32), 64, 1).astype(BF16)
        return jnp.concatenate(
            [blocks[place, :144, :], jnp.concatenate([folded, bottom], axis=0)], axis=1
        )

    gradients, cells = [], []
    for x in range(0, lats // 2, 2):
        places = []
        for step in (x, x + 1):
            first = lat_index[0] + 2 * step
            first = jnp.where(first >= lats, first - lats, first)
            places.append((first, first + 1 - 2 * lax.rem(lat_index[0], 2)))
        for same, source in enumerate((low, other_low) if x == 0 else (high, other_high)):
            gradients.extend(columns(place[same]) for place in places)
            cells.append(source[...].reshape(2 * PACKED_ROWS, FEATURES))
    product = dot(
        jnp.concatenate(cells, axis=0), jnp.concatenate(gradients, axis=0), ((0,), (0,))
    )
    bands = out.shape[0]
    width = FEATURES // bands
    whole = product[:, :128].reshape(bands, width, 128)
    half = product[:, 128:].reshape(bands, width, 128)
    lane = row_index((bands, width // 2, 128), 2)
    out[:, :width, :] = whole.astype(BF16)
    folded = jnp.where(lane < 64, half[:, : width // 2], pltpu.roll(half[:, width // 2 :], 64, 2))
    out[:, width:, :] = folded.astype(BF16)
    tiles = []
    for part in (above, kept):
        part = part[...].astype(F32)
        for i in range(3):
            tiles.extend(unpack(part[24 * i : 24 * i + 24])[2:])
    packed = pack(tiles[:4]) + pack(tiles[4:8]) + pack(tiles[8:])
    sideways[...] = jnp.concatenate(packed, axis=0).astype(BF16)


def sum_kernel(lat_index, parts, out):
    bands, rows, _ = parts.shape
    width = rows * 2 // 3
    total = parts[0].astype(F32)
    for band in range(1, bands):
        total = total + parts[band].astype(F32)
    whole = total[:width]
    folded = total[width:]
    half = jnp.concatenate([folded, pltpu.roll(folded, 64, 1)], axis=0)
    half = half[:, :64]

    @pl.when(lax.rem(lat_index[0], 2) == 0)
    def _():
        out[0, :, :128] = whole
        out[0, :, 128:] = half

    @pl.when(lax.rem(lat_index[0], 2) == 1)
    def _():
        out[0, :, :64] = half
        out[0, :, 64:] = whole


def join_kernel(kept, above, left, out):
    row = row_index((8, FEATURES), 0)
    low, high = [], []
    side = left[...].astype(F32)
    for g in range(3):
        low.extend(unpack(side[24 * g : 24 * g + 24]))
    for part in (above, kept):
        part = part[...].astype(F32)
        for i in range(3):
            high.extend(unpack(part[24 * i : 24 * i + 24])[:2])
    for i in range(6):
        for level in range(2):
            moved = pltpu.roll(high[2 * i + level], 6, 0)
            out[0, level, i, 0:8, :] = jnp.where(row < 6, low[2 * i + level], moved).astype(BF16)
            out[0, level, i, 8:12, :] = moved[:4].astype(BF16)


def passed(array, lat_by, lon_by):
    lats, lons = lax.axis_size("lat"), lax.axis_size("lon")
    pairs = [
        (a * lons + o, ((a + lat_by) % lats) * lons + (o + lon_by) % lons)
        for a in range(lats)
        for o in range(lons)
    ]
    return lax.ppermute(array, ("lat", "lon"), pairs)


def other_core(array):
    return lax.ppermute(array, "lat", [(a, a ^ 1) for a in range(lax.axis_size("lat"))])


def per_device(x_in, out_grad, w_qkv, w_proj, norm_gain, bias_table, lat_labels):
    lats, lons = lax.axis_size("lat"), lax.axis_size("lon")
    w_qkv, w_proj = w_qkv[0], w_proj[0]
    part = struct((72, FEATURES), BF16)
    marked = struct((80, FEATURES), BF16)
    own, lon, lat, cor = call(
        cut_kernel,
        (marked, part, part, marked),
        [
            pltpu.SMEM(lat_labels.shape, jnp.int32),
            pltpu.VMEM((6, 12, 2, FEATURES), BF16),
            pltpu.VMEM((6, 12, 2, FEATURES), BF16),
            pltpu.SemaphoreType.DMA,
            pltpu.SemaphoreType.DMA((2, 6)),
        ],
        places={0: pl.ANY, 1: pl.ANY, 2: pl.ANY},
        limit=58 * MIB,
    )(lat_labels, x_in[0].transpose(1, 2, 0, 3), out_grad[0].transpose(1, 2, 0, 3))
    lon = passed(lon, 0, -1)
    lat = passed(lat, -1, 0)
    cor = passed(cor, -1, -1)
    table = jnp.pad(bias_table[0, :, 253:506], ((0, 0), (0, 3)))
    bias = call(
        bias_kernel,
        struct((HEADS * LEVEL_ROWS, 128), F32),
        cost=pl.CostEstimate(flops=4_000_000_000, bytes_accessed=20_000_000, transcendentals=0),
    )(table)

    scratch = [
        pltpu.VMEM((ROWS, 3 * FEATURES), BF16),
        pltpu.VMEM(w_qkv.shape, BF16),
        pltpu.SemaphoreType.DMA,
    ]
    skip, inputs, fields, projected, att = call(
        first_kernel,
        (
            struct((ROWS, FEATURES), BF16),
            struct((PACKED_ROWS, FEATURES), BF16),
            struct((2, ROWS, FEATURES), BF16),
            struct((ROWS, 3 * FEATURES), BF16),
            struct((2, 4, 2, LEVEL_ROWS, LEVEL_ROWS), BF16),
        ),
        scratch[:2] + [pltpu.SemaphoreType.DMA((3,))],
        places={4: pl.ANY},
    )(own, lon, lat, cor, w_qkv, w_proj, norm_gain, bias)

    lat_index = lax.axis_index("lat").astype(jnp.int32).reshape(1)
    arrived = lax.ppermute(skip, "phase", [(1, 0)])
    along = [inputs] + [passed(inputs, -2 * x, 0) for x in range(1, lats // 2)]
    blocks, kept, up = call(
        second_kernel,
        (struct((lats, 224, 128), BF16), part, part),
        scratch,
        places={5: pl.ANY},
        cost=pl.CostEstimate(flops=4_000_000_000, bytes_accessed=20_000_000, transcendentals=0),
    )(arrived, fields, projected, att, w_proj, w_qkv, norm_gain)
    blocks = lax.all_to_all(blocks, "lat", 0, 0, tiled=True)
    two = struct((2, PACKED_ROWS, FEATURES), BF16)
    low, high = call(stack_kernel, (two, two), places={4: pl.ANY})(*along, kept)
    other_low, other_high = other_core(low), other_core(high)
    above = passed(up, 1, 0)
    rows = FEATURES * 3 // 2 // lons
    slices, sideways = call(
        product_kernel,
        (struct((lons, rows, 128), BF16), part),
        places={0: pltpu.SMEM},
    )(lat_index, blocks, low, high, other_low, other_high, kept, above)
    left = passed(sideways, 0, 1)
    grad_input = call(join_kernel, struct((1, 2, 6, 12, FEATURES), BF16))(kept, above, left)
    slices = lax.all_to_all(slices, "lon", 0, 0, tiled=True)
    grad_qkv = call(
        sum_kernel, struct((1, FEATURES // lons, 192), F32), places={0: pltpu.SMEM}
    )(lat_index, slices)
    return grad_input, grad_qkv.transpose(0, 2, 1)


def solution(mesh):
    in_specs = (
        P("phase", None, "lat", "lon", None),
        P("phase", None, "lat", "lon", None),
        P("phase", None, None),
        P("phase", None, None),
        P("phase", None),
        P("phase", None, None),
        P("lat"),
    )
    out_specs = (P("phase", None, "lat", "lon", None), P("phase", "lat", "lon"))
    return jax.shard_map(
        per_device, mesh=mesh, in_specs=in_specs, out_specs=out_specs, check_vma=False
    )
```

```python
import functools

import jax
import jax.numpy as jnp
from jax import lax
from jax.experimental import pallas as pl
from jax.experimental.pallas import tpu as pltpu
from jax.sharding import PartitionSpec as P

F32 = jnp.float32
BF16 = jnp.bfloat16
HEADS = 8
FEATURES = 512
EPSILON = 1e-05
MASKED = -1e30
SCORE_SCALE = 0.125
MIB = 1024 * 1024
HIDING = pl.CostEstimate(flops=4_000_000_000, bytes_accessed=20_000_000, transcendentals=0)

LEVEL_ROWS = 96
ROWS = 192
PACKED_ROWS = 144
GROUP = 8


def call(kernel, out_shape, scratch=(), places=(), out_places=(), cost=None, limit=50 * MIB):
    def run(*args):
        places_of = dict(places)
        specs = [
            pl.BlockSpec(memory_space=places_of.get(i, pltpu.VMEM)) for i in range(len(args))
        ]
        outs_of = dict(out_places)
        outs = [
            pl.BlockSpec(memory_space=outs_of.get(i, pltpu.VMEM))
            for i in range(len(jax.tree.leaves(out_shape)))
        ]
        outs = tuple(outs) if isinstance(out_shape, tuple) else outs[0]
        return pl.pallas_call(
            kernel,
            out_shape=out_shape,
            in_specs=specs,
            out_specs=outs,
            scratch_shapes=list(scratch),
            cost_estimate=cost,
            compiler_params=pltpu.CompilerParams(vmem_limit_bytes=limit),
        )(*args)

    return run


def struct(shape, dtype):
    return jax.ShapeDtypeStruct(shape, dtype)


def dot(left, right, dims=((1,), (0,))):
    return lax.dot_general(left, right, (dims, ((), ())), preferred_element_type=F32)


def row_index(shape, dim):
    return lax.broadcasted_iota(jnp.int32, shape, dim)


def pack(tiles):
    row = row_index(tiles[3].shape, 0)
    return [jnp.where(row < 6, tiles[g], pltpu.roll(tiles[3], 6 - 2 * g, 0)) for g in range(3)]


def unpack(rows):
    tiles = [rows[8 * g : 8 * g + 8] for g in range(3)]
    row = row_index(tiles[0].shape, 0)
    last = jnp.where(row < 2, pltpu.roll(tiles[0], 2, 0), 0.0)
    last = jnp.where((row >= 2) & (row < 4), pltpu.roll(tiles[1], 4, 0), last)
    last = jnp.where((row >= 4) & (row < 6), pltpu.roll(tiles[2], 6, 0), last)
    return [jnp.where(row < 6, tile, 0.0) for tile in tiles] + [last]


def cut_kernel(labels_ref, x_ref, g_ref, own, lon, lat, cor, labels, x_rows, g_rows, sem, sems):
    fetch = pltpu.make_async_copy(labels_ref, labels, sem)
    fetch.start()
    fetches = []
    for i in range(6):
        fetches.append(pltpu.make_async_copy(x_ref.at[i], x_rows.at[i], sems.at[0, i]))
        fetches.append(pltpu.make_async_copy(g_ref.at[i], g_rows.at[i], sems.at[1, i]))
    for copy in fetches:
        copy.start()
    row = row_index((8, FEATURES), 0)

    fetch.wait()
    parts = {}
    marks = [jnp.zeros((8, FEATURES), F32)] * 2
    for i in range(6):
        fetches[2 * i].wait()
        fetches[2 * i + 1].wait()
        fields = x_rows[i].astype(F32), g_rows[i].astype(F32)
        low = [field[0:8, level, :] for field in fields for level in range(2)]
        high = [pltpu.roll(field[4:12, level, :], 6, 0) for field in fields for level in range(2)]
        parts.setdefault((i // 3, 0), []).extend(pack(low))
        parts.setdefault((i // 3, 1), []).extend(pack(high))
        marks[i // 3] = jnp.where(row == i % 3, labels[i].astype(F32), marks[i // 3])
    cor[...] = jnp.concatenate(parts[0, 0] + [marks[0]], axis=0).astype(BF16)
    lat[...] = jnp.concatenate(parts[0, 1], axis=0).astype(BF16)
    lon[...] = jnp.concatenate(parts[1, 0], axis=0).astype(BF16)
    own[...] = jnp.concatenate(parts[1, 1] + [marks[1]], axis=0).astype(BF16)


def bias_kernel(table, out):
    parts = []
    for h in range(HEADS):
        line = jnp.broadcast_to(table[h : h + 1, :], (8, 256))
        parts.append(pltpu.roll(line, 0, 1, stride=1, stride_axis=0))
        parts.append(pltpu.roll(line, 6, 1, stride=1, stride_axis=0))
    shifted = jnp.concatenate(parts, axis=0)
    source = row_index((256, 256), 0)
    lane = row_index((256, 256), 1)
    column = lane & 7
    target = (lane >> 4) * 23 + ((lane >> 3) & 1) * 6 + column + 11
    picked = jnp.where((source == target) & (column < 6), 1.0, 0.0).astype(BF16)
    first = shifted.astype(BF16)
    rest = shifted - first.astype(F32)
    second = rest.astype(BF16)
    third = (rest - second.astype(F32)).astype(BF16)
    spread = dot(first, picked) + dot(second, picked) + dot(third, picked)
    empty = (row_index((128, 128), 0) & 7) >= 6
    for b in range(6):
        shift = (256 - (5 - b) * 16) % 256
        moved = spread if shift == 0 else pltpu.roll(spread, shift, 1)
        moved = jnp.where(empty, MASKED, moved[:, :128])
        for h in range(HEADS):
            out[h * 96 + b * 16 : h * 96 + b * 16 + 16, :] = moved[h * 16 : h * 16 + 16, :]


def pack_rows(array):
    columns = array.shape[1]
    groups = array.reshape(6, 4, 8, columns)
    row = row_index((8, columns), 0)
    out = []
    for q in range(6):
        last = groups[q, 3]
        for g in range(3):
            out.append(jnp.where(row < 6, groups[q, g], pltpu.roll(last, 6 - 2 * g, 0)))
    return jnp.concatenate(out, axis=0)


def per_head(pair, factor=1.0):
    even = (row_index(pair.shape, 1) < 64).astype(F32)
    return jnp.concatenate(
        [pair * (even * factor).astype(BF16), pair * ((1.0 - even) * factor).astype(BF16)], axis=0
    )


def attention_backward(att, d_low, projected, dqkv):
    lane = row_index((LEVEL_ROWS, 128), 1)
    units = [(level, pair) for level in range(2) for pair in range(4)]
    for first in range(0, len(units), GROUP):
        group = units[first : first + GROUP]
        places = [
            (slice(level * LEVEL_ROWS, (level + 1) * LEVEL_ROWS), slice(pair * 128, (pair + 1) * 128))
            for level, pair in group
        ]
        probs = att(group)
        d_probs = [
            dot(
                per_head(projected[rows, 1024 + cols.start : 1024 + cols.stop]),
                d_low[rows, cols],
                ((1,), (1,)),
            ).reshape(2, LEVEL_ROWS, LEVEL_ROWS)
            for rows, cols in places
        ]
        d_values = [
            dot(p.astype(BF16).reshape(2 * LEVEL_ROWS, LEVEL_ROWS), d_low[rows, cols])
            for p, (rows, cols) in zip(probs, places)
        ]
        inner = [jnp.sum(p * d, axis=1, keepdims=True) for p, d in zip(probs, d_probs)]
        d_scores = [
            (p * (d - i)).astype(BF16).reshape(2 * LEVEL_ROWS, LEVEL_ROWS)
            for p, d, i in zip(probs, d_probs, inner)
        ]
        d_keys = [dot(d, projected[rows, cols]) for d, (rows, cols) in zip(d_scores, places)]
        d_queries = [
            dot(
                d,
                per_head(projected[rows, 512 + cols.start : 512 + cols.stop], SCORE_SCALE),
                ((0,), (0,)),
            )
            for d, (rows, cols) in zip(d_scores, places)
        ]
        for (rows, cols), d_query, d_key, d_value in zip(places, d_queries, d_keys, d_values):
            dqkv[rows, cols] = d_query.astype(BF16)
            dqkv[rows, 512 + cols.start : 512 + cols.stop] = jnp.where(
                lane < 64, d_key[:LEVEL_ROWS], d_key[LEVEL_ROWS:]
            ).astype(BF16)
            dqkv[rows, 1024 + cols.start : 1024 + cols.stop] = jnp.where(
                lane < 64, d_value[:LEVEL_ROWS], d_value[LEVEL_ROWS:]
            ).astype(BF16)


def input_gradient(dqkv, w_qkv, gain, normed, inv_std):
    d_normed = dot(dqkv[...], w_qkv[...]) * gain[...]
    mean_plain = jnp.mean(d_normed, axis=-1, keepdims=True)
    mean_normed = jnp.mean(d_normed * normed, axis=-1, keepdims=True)
    return inv_std * (d_normed - mean_plain - normed * mean_normed)


def normalised(x):
    center = jnp.mean(x, axis=-1, keepdims=True)
    moved = x - center
    spread = jnp.mean(jnp.square(moved), axis=-1, keepdims=True)
    inv_std = lax.rsqrt(spread + EPSILON)
    return moved * inv_std, inv_std


def first_kernel(
    own, lon, lat, cor, w_qkv_ref, w_proj, gain, bias,
    skip, inputs, fields, projected_out, att_out,
    dqkv, w_qkv, sems,
):
    thirds = [slice(FEATURES * j, FEATURES * (j + 1)) for j in range(3)]
    fetches = [
        pltpu.make_async_copy(w_qkv_ref.at[third], w_qkv.at[third], sems.at[j])
        for j, third in enumerate(thirds)
    ]
    for copy in fetches:
        copy.start()
    labels = []
    tiles = {}
    for upper, (left, right) in enumerate(((own, lon), (lat, cor))):
        left, right = left[...].astype(F32), right[...].astype(F32)
        marked = right if upper else left
        labels.extend(marked[72 + i : 73 + i, :128] for i in range(3))
        for i in range(3):
            for half, piece in ((0, left), (1, right)):
                found = unpack(piece[24 * i : 24 * i + 24])
                for k in range(4):
                    tiles[k // 2, k % 2, 3 * upper + i, half] = found[k]
    order = [(level, i, half) for level in range(2) for i in range(6) for half in range(2)]
    tiles_x, tiles_g = ([tiles[(field,) + place] for place in order] for field in range(2))
    x = jnp.concatenate(tiles_x, axis=0)
    c = jnp.concatenate(tiles_g, axis=0)
    normed, inv_std = normalised(x)
    scaled = normed * gain[...]
    inputs[...] = pack_rows(scaled).astype(BF16)
    c_low = c.astype(BF16)
    d_low = dot(c_low, w_proj[...]).astype(BF16)
    fields[0] = x.astype(BF16)
    fields[1] = c_low
    scaled_low = scaled.astype(BF16)
    for copy, third in zip(fetches, thirds):
        copy.wait()
        projected = dot(scaled_low, w_qkv[third, :], ((1,), (1,)))
        projected_out[:, third] = (projected * (SCORE_SCALE if third.start == 0 else 1.0)).astype(BF16)

    lane_row = row_index((1, 128), 1) >> 4
    along = labels[0]
    for b in range(1, 6):
        along = jnp.where(lane_row == b, labels[b], along)
    allowed = jnp.concatenate(
        [
            jnp.broadcast_to(jnp.where(labels[b] == along, 0.0, MASKED), (16, 128))
            for b in range(6)
        ],
        axis=0,
    )

    def probabilities(group):
        scores = []
        for level, pair in group:
            rows = slice(level * LEVEL_ROWS, (level + 1) * LEVEL_ROWS)
            cols = slice(pair * 128, (pair + 1) * 128)
            keys = per_head(projected_out[rows, 512 + cols.start : 512 + cols.stop])
            score = dot(keys, projected_out[rows, cols], ((1,), (1,)))
            scores.append(score.reshape(2, LEVEL_ROWS, LEVEL_ROWS))
        probs = []
        for (level, pair), score in zip(group, scores):
            added = bias[pair * 192 : (pair + 1) * 192, :].reshape(2, LEVEL_ROWS, 128) + allowed[None]
            score = score + added[:, :, :LEVEL_ROWS]
            weights = jnp.exp(score - jnp.max(score, axis=1, keepdims=True))
            probs.append(weights * (1.0 / jnp.sum(weights, axis=1, keepdims=True)))
        for (level, pair), prob in zip(group, probs):
            att_out[level, pair] = prob.astype(BF16)
        return probs

    attention_backward(probabilities, d_low, projected_out, dqkv)
    skip[...] = (c + input_gradient(dqkv, w_qkv, gain, normed, inv_std)).astype(BF16)


def second_kernel(
    arrived, fields, projected, att, w_proj, w_qkv_ref, gain,
    blocks, kept, up, dqkv, w_qkv, sem,
):
    fetch = pltpu.make_async_copy(w_qkv_ref, w_qkv, sem)
    fetch.start()
    d_low = (dot(fields[1], w_proj[...]) + dot(arrived[...], w_proj[...])).astype(BF16)
    attention_backward(
        lambda group: [att[level, pair].astype(F32) for level, pair in group], d_low, projected, dqkv
    )
    lane = row_index((80, 128), 1)
    for t in range(4):
        whole = [
            pack_rows(dqkv[:, 384 * t + 128 * j : 384 * t + 128 * (j + 1)].astype(F32))
            for j in range(3)
        ]
        blocks[2 * t, :144, :] = whole[0].astype(BF16)
        blocks[2 * t + 1, :144, :] = whole[2].astype(BF16)
        top = whole[1][:80]
        bottom = jnp.concatenate([whole[1][80:], jnp.zeros((16, 128), F32)], axis=0)
        blocks[2 * t, 144:, :] = jnp.where(lane < 64, top, pltpu.roll(bottom, 64, 1)).astype(BF16)
        blocks[2 * t + 1, 144:, :] = jnp.where(lane < 64, pltpu.roll(top, 64, 1), bottom).astype(
            BF16
        )
    normed, inv_std = normalised(fields[0].astype(F32))
    fetch.wait()
    shifted = input_gradient(dqkv, w_qkv, gain, normed, inv_std)
    total = fields[1].astype(F32) + (arrived[...].astype(F32) + shifted)
    for target, first in ((kept, 0), (up, 3)):
        parts = []
        for i in range(first, first + 3):
            starts = [96 * level + 16 * i + 8 * half for half in range(2) for level in range(2)]
            parts.extend(pack([total[start : start + 8] for start in starts]))
        target[...] = jnp.concatenate(parts, axis=0).astype(BF16)


def stack_kernel(a, b, c, d, kept, low, high):
    low[0], low[1], high[0], high[1] = a[...], b[...], c[...], d[...]


def product_kernel(
    lat_index, blocks, low, high, other_low, other_high, out
):
    lats = blocks.shape[0]

    def columns(place):
        folded = blocks[place, 144:, :]
        bottom = pltpu.roll(folded[:64].astype(F32), 64, 1).astype(BF16)
        return jnp.concatenate(
            [blocks[place, :144, :], jnp.concatenate([folded, bottom], axis=0)], axis=1
        )

    gradients, cells = [], []
    for x in range(0, lats // 2, 2):
        places = []
        for step in (x, x + 1):
            first = lat_index[0] + 2 * step
            first = jnp.where(first >= lats, first - lats, first)
            places.append((first, first + 1 - 2 * lax.rem(lat_index[0], 2)))
        for same, source in enumerate((low, other_low) if x == 0 else (high, other_high)):
            gradients.extend(columns(place[same]) for place in places)
            cells.append(source[...].reshape(2 * PACKED_ROWS, FEATURES))
    product = dot(
        jnp.concatenate(cells, axis=0), jnp.concatenate(gradients, axis=0), ((0,), (0,))
    )
    bands = out.shape[0]
    width = FEATURES // bands
    whole = product[:, :128].reshape(bands, width, 128)
    half = product[:, 128:].reshape(bands, width, 128)
    lane = row_index((bands, width // 2, 128), 2)
    out[:, :width, :] = whole.astype(BF16)
    folded = jnp.where(lane < 64, half[:, : width // 2], pltpu.roll(half[:, width // 2 :], 64, 2))
    out[:, width:, :] = folded.astype(BF16)


def sideways_kernel(kept, above, sideways):
    tiles = []
    for part in (above, kept):
        part = part[...].astype(F32)
        for i in range(3):
            tiles.extend(unpack(part[24 * i : 24 * i + 24])[2:])
    packed = pack(tiles[:4]) + pack(tiles[4:8]) + pack(tiles[8:])
    sideways[...] = jnp.concatenate(packed, axis=0).astype(BF16)


def sum_kernel(lat_index, parts, out):
    bands, rows, _ = parts.shape
    width = rows * 2 // 3
    total = parts[0].astype(F32)
    for band in range(1, bands):
        total = total + parts[band].astype(F32)
    whole = total[:width]
    folded = total[width:]
    half = jnp.concatenate([folded, pltpu.roll(folded, 64, 1)], axis=0)
    half = half[:, :64]

    @pl.when(lax.rem(lat_index[0], 2) == 0)
    def _():
        out[0, :, :128] = whole
        out[0, :, 128:] = half

    @pl.when(lax.rem(lat_index[0], 2) == 1)
    def _():
        out[0, :, :64] = half
        out[0, :, 64:] = whole


def join_kernel(kept, above, left, out):
    row = row_index((8, FEATURES), 0)
    low, high = [], []
    side = left[...].astype(F32)
    for g in range(3):
        low.extend(unpack(side[24 * g : 24 * g + 24]))
    for part in (above, kept):
        part = part[...].astype(F32)
        for i in range(3):
            high.extend(unpack(part[24 * i : 24 * i + 24])[:2])
    for i in range(6):
        for level in range(2):
            moved = pltpu.roll(high[2 * i + level], 6, 0)
            out[0, level, i, 0:8, :] = jnp.where(row < 6, low[2 * i + level], moved).astype(BF16)
            out[0, level, i, 8:12, :] = moved[:4].astype(BF16)


def passed(array, lat_by, lon_by):
    lats, lons = lax.axis_size("lat"), lax.axis_size("lon")
    pairs = [
        (a * lons + o, ((a + lat_by) % lats) * lons + (o + lon_by) % lons)
        for a in range(lats)
        for o in range(lons)
    ]
    return lax.ppermute(array, ("lat", "lon"), pairs)


def other_core(array):
    return lax.ppermute(array, "lat", [(a, a ^ 1) for a in range(lax.axis_size("lat"))])


def per_device(x_in, out_grad, w_qkv, w_proj, norm_gain, bias_table, lat_labels):
    lats, lons = lax.axis_size("lat"), lax.axis_size("lon")
    w_qkv, w_proj = w_qkv[0], w_proj[0]
    part = struct((72, FEATURES), BF16)
    marked = struct((80, FEATURES), BF16)
    own, lon, lat, cor = call(
        cut_kernel,
        (marked, part, part, marked),
        [
            pltpu.SMEM(lat_labels.shape, jnp.int32),
            pltpu.VMEM((6, 12, 2, FEATURES), BF16),
            pltpu.VMEM((6, 12, 2, FEATURES), BF16),
            pltpu.SemaphoreType.DMA,
            pltpu.SemaphoreType.DMA((2, 6)),
        ],
        places={0: pl.ANY, 1: pl.ANY, 2: pl.ANY},
        limit=58 * MIB,
    )(lat_labels, x_in[0].transpose(1, 2, 0, 3), out_grad[0].transpose(1, 2, 0, 3))
    lon = passed(lon, 0, -1)
    lat = passed(lat, -1, 0)
    cor = passed(cor, -1, -1)
    table = jnp.pad(bias_table[0, :, 253:506], ((0, 0), (0, 3)))
    bias = call(
        bias_kernel,
        struct((HEADS * LEVEL_ROWS, 128), F32),
        cost=HIDING,
    )(table)

    scratch = [
        pltpu.VMEM((ROWS, 3 * FEATURES), BF16),
        pltpu.VMEM(w_qkv.shape, BF16),
        pltpu.SemaphoreType.DMA,
    ]
    skip, inputs, fields, projected, att = call(
        first_kernel,
        (
            struct((ROWS, FEATURES), BF16),
            struct((PACKED_ROWS, FEATURES), BF16),
            struct((2, ROWS, FEATURES), BF16),
            struct((ROWS, 3 * FEATURES), BF16),
            struct((2, 4, 2, LEVEL_ROWS, LEVEL_ROWS), BF16),
        ),
        scratch[:2] + [pltpu.SemaphoreType.DMA((3,))],
        places={4: pl.ANY},
    )(own, lon, lat, cor, w_qkv, w_proj, norm_gain, bias)

    lat_index = lax.axis_index("lat").astype(jnp.int32).reshape(1)
    arrived = lax.ppermute(skip, "phase", [(1, 0)])
    along = [inputs] + [passed(inputs, -2 * x, 0) for x in range(1, lats // 2)]
    blocks, kept, up = call(
        second_kernel,
        (struct((lats, 224, 128), BF16), part, part),
        scratch,
        places={5: pl.ANY},
        cost=HIDING,
    )(arrived, fields, projected, att, w_proj, w_qkv, norm_gain)
    blocks = lax.all_to_all(blocks, "lat", 0, 0, tiled=True)
    two = struct((2, PACKED_ROWS, FEATURES), BF16)
    low, high = call(stack_kernel, (two, two), places={4: pl.ANY})(*along, kept)
    other_low, other_high = other_core(low), other_core(high)
    above = passed(up, 1, 0)
    rows = FEATURES * 3 // 2 // lons
    slices = call(product_kernel, struct((lons, rows, 128), BF16), places={0: pltpu.SMEM})(
        lat_index, blocks, low, high, other_low, other_high
    )
    sideways = call(sideways_kernel, part, cost=HIDING)(kept, above)
    left = passed(sideways, 0, 1)
    grad_input = call(join_kernel, struct((1, 2, 6, 12, FEATURES), BF16))(kept, above, left)
    slices = lax.all_to_all(slices, "lon", 0, 0, tiled=True)
    grad_qkv = call(
        sum_kernel, struct((1, FEATURES // lons, 192), F32), places={0: pltpu.SMEM}
    )(lat_index, slices)
    return grad_input, grad_qkv.transpose(0, 2, 1)


def solution(mesh):
    in_specs = (
        P("phase", None, "lat", "lon", None),
        P("phase", None, "lat", "lon", None),
        P("phase", None, None),
        P("phase", None, None),
        P("phase", None),
        P("phase", None, None),
        P("lat"),
    )
    out_specs = (P("phase", None, "lat", "lon", None), P("phase", "lat", "lon"))
    return jax.shard_map(
        per_device, mesh=mesh, in_specs=in_specs, out_specs=out_specs, check_vma=False
    )
```

```python
import functools

import jax
import jax.numpy as jnp
from jax import lax
from jax.experimental import pallas as pl
from jax.experimental.pallas import tpu as pltpu
from jax.sharding import PartitionSpec as P

F32 = jnp.float32
BF16 = jnp.bfloat16
HEADS = 8
FEATURES = 512
EPSILON = 1e-05
MASKED = -1e30
SCORE_SCALE = 0.125
MIB = 1024 * 1024
HIDING = pl.CostEstimate(flops=4_000_000_000, bytes_accessed=20_000_000, transcendentals=0)

LEVEL_ROWS = 96
ROWS = 192
PACKED_ROWS = 144
GROUP = 8


def call(kernel, out_shape, scratch=(), places=(), out_places=(), cost=None, limit=50 * MIB):
    def run(*args):
        places_of = dict(places)
        specs = [
            pl.BlockSpec(memory_space=places_of.get(i, pltpu.VMEM)) for i in range(len(args))
        ]
        outs_of = dict(out_places)
        outs = [
            pl.BlockSpec(memory_space=outs_of.get(i, pltpu.VMEM))
            for i in range(len(jax.tree.leaves(out_shape)))
        ]
        outs = tuple(outs) if isinstance(out_shape, tuple) else outs[0]
        return pl.pallas_call(
            kernel,
            out_shape=out_shape,
            in_specs=specs,
            out_specs=outs,
            scratch_shapes=list(scratch),
            cost_estimate=cost,
            compiler_params=pltpu.CompilerParams(vmem_limit_bytes=limit),
        )(*args)

    return run


def struct(shape, dtype):
    return jax.ShapeDtypeStruct(shape, dtype)


def dot(left, right, dims=((1,), (0,))):
    return lax.dot_general(left, right, (dims, ((), ())), preferred_element_type=F32)


def row_index(shape, dim):
    return lax.broadcasted_iota(jnp.int32, shape, dim)


def pack(tiles):
    row = row_index(tiles[3].shape, 0)
    return [jnp.where(row < 6, tiles[g], pltpu.roll(tiles[3], 6 - 2 * g, 0)) for g in range(3)]


def unpack(rows):
    tiles = [rows[8 * g : 8 * g + 8] for g in range(3)]
    row = row_index(tiles[0].shape, 0)
    last = jnp.where(row < 2, pltpu.roll(tiles[0], 2, 0), 0.0)
    last = jnp.where((row >= 2) & (row < 4), pltpu.roll(tiles[1], 4, 0), last)
    last = jnp.where((row >= 4) & (row < 6), pltpu.roll(tiles[2], 6, 0), last)
    return [jnp.where(row < 6, tile, 0.0) for tile in tiles] + [last]


def cut_kernel(labels_ref, x_ref, g_ref, own, lon, lat, cor, labels, x_rows, g_rows, sem, sems):
    fetch = pltpu.make_async_copy(labels_ref, labels, sem)
    fetch.start()
    fetches = []
    for i in range(6):
        fetches.append(pltpu.make_async_copy(x_ref.at[i], x_rows.at[i], sems.at[0, i]))
        fetches.append(pltpu.make_async_copy(g_ref.at[i], g_rows.at[i], sems.at[1, i]))
    for copy in fetches:
        copy.start()
    row = row_index((8, FEATURES), 0)

    fetch.wait()
    parts = {}
    marks = [jnp.zeros((8, FEATURES), F32)] * 2
    for i in range(6):
        fetches[2 * i].wait()
        fetches[2 * i + 1].wait()
        fields = x_rows[i].astype(F32), g_rows[i].astype(F32)
        low = [field[0:8, level, :] for field in fields for level in range(2)]
        high = [pltpu.roll(field[4:12, level, :], 6, 0) for field in fields for level in range(2)]
        parts.setdefault((i // 3, 0), []).extend(pack(low))
        parts.setdefault((i // 3, 1), []).extend(pack(high))
        marks[i // 3] = jnp.where(row == i % 3, labels[i].astype(F32), marks[i // 3])
    cor[...] = jnp.concatenate(parts[0, 0] + [marks[0]], axis=0).astype(BF16)
    lat[...] = jnp.concatenate(parts[0, 1], axis=0).astype(BF16)
    lon[...] = jnp.concatenate(parts[1, 0], axis=0).astype(BF16)
    own[...] = jnp.concatenate(parts[1, 1] + [marks[1]], axis=0).astype(BF16)


def bias_kernel(table, out):
    parts = []
    for h in range(HEADS):
        line = jnp.broadcast_to(table[h : h + 1, :], (8, 256))
        parts.append(pltpu.roll(line, 0, 1, stride=1, stride_axis=0))
        parts.append(pltpu.roll(line, 6, 1, stride=1, stride_axis=0))
    shifted = jnp.concatenate(parts, axis=0)
    source = row_index((256, 256), 0)
    lane = row_index((256, 256), 1)
    column = lane & 7
    target = (lane >> 4) * 23 + ((lane >> 3) & 1) * 6 + column + 11
    picked = jnp.where((source == target) & (column < 6), 1.0, 0.0).astype(BF16)
    first = shifted.astype(BF16)
    rest = shifted - first.astype(F32)
    second = rest.astype(BF16)
    third = (rest - second.astype(F32)).astype(BF16)
    spread = dot(first, picked) + dot(second, picked) + dot(third, picked)
    empty = (row_index((128, 128), 0) & 7) >= 6
    for b in range(6):
        shift = (256 - (5 - b) * 16) % 256
        moved = spread if shift == 0 else pltpu.roll(spread, shift, 1)
        moved = jnp.where(empty, MASKED, moved[:, :128])
        for h in range(HEADS):
            out[h * 96 + b * 16 : h * 96 + b * 16 + 16, :] = moved[h * 16 : h * 16 + 16, :]


def pack_rows(array):
    columns = array.shape[1]
    groups = array.reshape(6, 4, 8, columns)
    row = row_index((8, columns), 0)
    out = []
    for q in range(6):
        last = groups[q, 3]
        for g in range(3):
            out.append(jnp.where(row < 6, groups[q, g], pltpu.roll(last, 6 - 2 * g, 0)))
    return jnp.concatenate(out, axis=0)


def per_head(pair, factor=1.0):
    even = (row_index(pair.shape, 1) < 64).astype(F32)
    return jnp.concatenate(
        [pair * (even * factor).astype(BF16), pair * ((1.0 - even) * factor).astype(BF16)], axis=0
    )


def attention_backward(att, d_low, projected, dqkv):
    lane = row_index((LEVEL_ROWS, 128), 1)
    units = [(level, pair) for level in range(2) for pair in range(4)]
    for first in range(0, len(units), GROUP):
        group = units[first : first + GROUP]
        places = [
            (slice(level * LEVEL_ROWS, (level + 1) * LEVEL_ROWS), slice(pair * 128, (pair + 1) * 128))
            for level, pair in group
        ]
        probs = att(group)
        d_probs = [
            dot(
                per_head(projected[rows, 1024 + cols.start : 1024 + cols.stop]),
                d_low[rows, cols],
                ((1,), (1,)),
            ).reshape(2, LEVEL_ROWS, LEVEL_ROWS)
            for rows, cols in places
        ]
        d_values = [
            dot(p.astype(BF16).reshape(2 * LEVEL_ROWS, LEVEL_ROWS), d_low[rows, cols])
            for p, (rows, cols) in zip(probs, places)
        ]
        inner = [jnp.sum(p * d, axis=1, keepdims=True) for p, d in zip(probs, d_probs)]
        d_scores = [
            (p * (d - i)).astype(BF16).reshape(2 * LEVEL_ROWS, LEVEL_ROWS)
            for p, d, i in zip(probs, d_probs, inner)
        ]
        d_keys = [dot(d, projected[rows, cols]) for d, (rows, cols) in zip(d_scores, places)]
        d_queries = [
            dot(
                d,
                per_head(projected[rows, 512 + cols.start : 512 + cols.stop], SCORE_SCALE),
                ((0,), (0,)),
            )
            for d, (rows, cols) in zip(d_scores, places)
        ]
        for (rows, cols), d_query, d_key, d_value in zip(places, d_queries, d_keys, d_values):
            dqkv[rows, cols] = d_query.astype(BF16)
            dqkv[rows, 512 + cols.start : 512 + cols.stop] = jnp.where(
                lane < 64, d_key[:LEVEL_ROWS], d_key[LEVEL_ROWS:]
            ).astype(BF16)
            dqkv[rows, 1024 + cols.start : 1024 + cols.stop] = jnp.where(
                lane < 64, d_value[:LEVEL_ROWS], d_value[LEVEL_ROWS:]
            ).astype(BF16)


def input_gradient(dqkv, w_qkv, gain, normed, inv_std):
    d_normed = dot(dqkv[...], w_qkv[...]) * gain[...]
    mean_plain = jnp.mean(d_normed, axis=-1, keepdims=True)
    mean_normed = jnp.mean(d_normed * normed, axis=-1, keepdims=True)
    return inv_std * (d_normed - mean_plain - normed * mean_normed)


def normalised(x):
    center = jnp.mean(x, axis=-1, keepdims=True)
    moved = x - center
    spread = jnp.mean(jnp.square(moved), axis=-1, keepdims=True)
    inv_std = lax.rsqrt(spread + EPSILON)
    return moved * inv_std, inv_std


def first_kernel(
    own, lon, lat, cor, w_qkv_ref, w_proj, gain, bias,
    skip, inputs, fields, projected_out, att_out,
    dqkv, w_qkv, sems,
):
    thirds = [slice(FEATURES * j, FEATURES * (j + 1)) for j in range(3)]
    fetches = [
        pltpu.make_async_copy(w_qkv_ref.at[third], w_qkv.at[third], sems.at[j])
        for j, third in enumerate(thirds)
    ]
    for copy in fetches:
        copy.start()
    labels = []
    tiles = {}
    for upper, (left, right) in enumerate(((own, lon), (lat, cor))):
        left, right = left[...].astype(F32), right[...].astype(F32)
        marked = right if upper else left
        labels.extend(marked[72 + i : 73 + i, :128] for i in range(3))
        for i in range(3):
            for half, piece in ((0, left), (1, right)):
                found = unpack(piece[24 * i : 24 * i + 24])
                for k in range(4):
                    tiles[k // 2, k % 2, 3 * upper + i, half] = found[k]
    order = [(level, i, half) for level in range(2) for i in range(6) for half in range(2)]
    tiles_x, tiles_g = ([tiles[(field,) + place] for place in order] for field in range(2))
    x = jnp.concatenate(tiles_x, axis=0)
    c = jnp.concatenate(tiles_g, axis=0)
    normed, inv_std = normalised(x)
    scaled = normed * gain[...]
    inputs[...] = pack_rows(scaled).astype(BF16)
    c_low = c.astype(BF16)
    d_low = dot(c_low, w_proj[...]).astype(BF16)
    fields[0] = x.astype(BF16)
    fields[1] = c_low
    scaled_low = scaled.astype(BF16)
    for copy, third in zip(fetches, thirds):
        copy.wait()
        projected = dot(scaled_low, w_qkv[third, :], ((1,), (1,)))
        projected_out[:, third] = (projected * (SCORE_SCALE if third.start == 0 else 1.0)).astype(BF16)

    lane_row = row_index((1, 128), 1) >> 4
    along = labels[0]
    for b in range(1, 6):
        along = jnp.where(lane_row == b, labels[b], along)
    allowed = jnp.concatenate(
        [
            jnp.broadcast_to(jnp.where(labels[b] == along, 0.0, MASKED), (16, 128))
            for b in range(6)
        ],
        axis=0,
    )

    def probabilities(group):
        scores = []
        for level, pair in group:
            rows = slice(level * LEVEL_ROWS, (level + 1) * LEVEL_ROWS)
            cols = slice(pair * 128, (pair + 1) * 128)
            keys = per_head(projected_out[rows, 512 + cols.start : 512 + cols.stop])
            score = dot(keys, projected_out[rows, cols], ((1,), (1,)))
            scores.append(score.reshape(2, LEVEL_ROWS, LEVEL_ROWS))
        probs = []
        for (level, pair), score in zip(group, scores):
            added = bias[pair * 192 : (pair + 1) * 192, :].reshape(2, LEVEL_ROWS, 128) + allowed[None]
            score = score + added[:, :, :LEVEL_ROWS]
            weights = jnp.exp(score - jnp.max(score, axis=1, keepdims=True))
            probs.append(weights * (1.0 / jnp.sum(weights, axis=1, keepdims=True)))
        for (level, pair), prob in zip(group, probs):
            att_out[level, pair] = prob.astype(BF16)
        return probs

    attention_backward(probabilities, d_low, projected_out, dqkv)
    skip[...] = (c + input_gradient(dqkv, w_qkv, gain, normed, inv_std)).astype(BF16)


def second_kernel(
    arrived, fields, projected, att, w_proj, w_qkv_ref, gain,
    blocks, kept, up, dqkv, w_qkv, sem,
):
    fetch = pltpu.make_async_copy(w_qkv_ref, w_qkv, sem)
    fetch.start()
    d_low = (dot(fields[1], w_proj[...]) + dot(arrived[...], w_proj[...])).astype(BF16)
    attention_backward(
        lambda group: [att[level, pair].astype(F32) for level, pair in group], d_low, projected, dqkv
    )
    lane = row_index((80, 128), 1)
    for t in range(4):
        whole = [
            pack_rows(dqkv[:, 384 * t + 128 * j : 384 * t + 128 * (j + 1)].astype(F32))
            for j in range(3)
        ]
        blocks[2 * t, :144, :] = whole[0].astype(BF16)
        blocks[2 * t + 1, :144, :] = whole[2].astype(BF16)
        top = whole[1][:80]
        bottom = jnp.concatenate([whole[1][80:], jnp.zeros((16, 128), F32)], axis=0)
        blocks[2 * t, 144:, :] = jnp.where(lane < 64, top, pltpu.roll(bottom, 64, 1)).astype(BF16)
        blocks[2 * t + 1, 144:, :] = jnp.where(lane < 64, pltpu.roll(top, 64, 1), bottom).astype(
            BF16
        )
    normed, inv_std = normalised(fields[0].astype(F32))
    fetch.wait()
    shifted = input_gradient(dqkv, w_qkv, gain, normed, inv_std)
    total = fields[1].astype(F32) + (arrived[...].astype(F32) + shifted)
    for target, first in ((kept, 0), (up, 3)):
        parts = []
        for i in range(first, first + 3):
            starts = [96 * level + 16 * i + 8 * half for half in range(2) for level in range(2)]
            parts.extend(pack([total[start : start + 8] for start in starts]))
        target[...] = jnp.concatenate(parts, axis=0).astype(BF16)


def stack_kernel(a, b, kept, out):
    out[0], out[1] = a[...], b[...]


def product_kernel(
    lat_index, blocks, stack, other_stack, far, other_far, last, other_last, out
):
    lats = blocks.shape[0]

    def columns(place):
        folded = blocks[place, 144:, :]
        bottom = pltpu.roll(folded[:64].astype(F32), 64, 1).astype(BF16)
        return jnp.concatenate(
            [blocks[place, :144, :], jnp.concatenate([folded, bottom], axis=0)], axis=1
        )

    def place(step, same):
        first = lat_index[0] + 2 * step
        first = jnp.where(first >= lats, first - lats, first)
        return first if same else first + 1 - 2 * lax.rem(lat_index[0], 2)

    steps = stack.shape[0]
    gradients = [columns(place(step, same)) for same in (True, False) for step in range(steps)]
    gradients += [columns(place(step, same)) for step in (2, 3) for same in (True, False)]
    cells = [part[...].reshape(steps * PACKED_ROWS, FEATURES) for part in (stack, other_stack)]
    cells += [far[...], other_far[...], last[...], other_last[...]]
    product = dot(
        jnp.concatenate(cells, axis=0), jnp.concatenate(gradients, axis=0), ((0,), (0,))
    )
    bands = out.shape[0]
    width = FEATURES // bands
    whole = product[:, :128].reshape(bands, width, 128)
    half = product[:, 128:].reshape(bands, width, 128)
    lane = row_index((bands, width // 2, 128), 2)
    out[:, :width, :] = whole.astype(BF16)
    folded = jnp.where(lane < 64, half[:, : width // 2], pltpu.roll(half[:, width // 2 :], 64, 2))
    out[:, width:, :] = folded.astype(BF16)


def sideways_kernel(kept, above, sideways):
    tiles = []
    for part in (above, kept):
        part = part[...].astype(F32)
        for i in range(3):
            tiles.extend(unpack(part[24 * i : 24 * i + 24])[2:])
    packed = pack(tiles[:4]) + pack(tiles[4:8]) + pack(tiles[8:])
    sideways[...] = jnp.concatenate(packed, axis=0).astype(BF16)


def sum_kernel(lat_index, parts, out):
    bands, rows, _ = parts.shape
    width = rows * 2 // 3
    total = parts[0].astype(F32)
    for band in range(1, bands):
        total = total + parts[band].astype(F32)
    whole = total[:width]
    folded = total[width:]
    half = jnp.concatenate([folded, pltpu.roll(folded, 64, 1)], axis=0)
    half = half[:, :64]

    @pl.when(lax.rem(lat_index[0], 2) == 0)
    def _():
        out[0, :, :128] = whole
        out[0, :, 128:] = half

    @pl.when(lax.rem(lat_index[0], 2) == 1)
    def _():
        out[0, :, :64] = half
        out[0, :, 64:] = whole


def join_kernel(kept, above, left, out):
    row = row_index((8, FEATURES), 0)
    low, high = [], []
    side = left[...].astype(F32)
    for g in range(3):
        low.extend(unpack(side[24 * g : 24 * g + 24]))
    for part in (above, kept):
        part = part[...].astype(F32)
        for i in range(3):
            high.extend(unpack(part[24 * i : 24 * i + 24])[:2])
    for i in range(6):
        for level in range(2):
            moved = pltpu.roll(high[2 * i + level], 6, 0)
            out[0, level, i, 0:8, :] = jnp.where(row < 6, low[2 * i + level], moved).astype(BF16)
            out[0, level, i, 8:12, :] = moved[:4].astype(BF16)


def passed(array, lat_by, lon_by):
    lats, lons = lax.axis_size("lat"), lax.axis_size("lon")
    pairs = [
        (a * lons + o, ((a + lat_by) % lats) * lons + (o + lon_by) % lons)
        for a in range(lats)
        for o in range(lons)
    ]
    return lax.ppermute(array, ("lat", "lon"), pairs)


def other_core(array):
    return lax.ppermute(array, "lat", [(a, a ^ 1) for a in range(lax.axis_size("lat"))])


def per_device(x_in, out_grad, w_qkv, w_proj, norm_gain, bias_table, lat_labels):
    lats, lons = lax.axis_size("lat"), lax.axis_size("lon")
    w_qkv, w_proj = w_qkv[0], w_proj[0]
    part = struct((72, FEATURES), BF16)
    marked = struct((80, FEATURES), BF16)
    own, lon, lat, cor = call(
        cut_kernel,
        (marked, part, part, marked),
        [
            pltpu.SMEM(lat_labels.shape, jnp.int32),
            pltpu.VMEM((6, 12, 2, FEATURES), BF16),
            pltpu.VMEM((6, 12, 2, FEATURES), BF16),
            pltpu.SemaphoreType.DMA,
            pltpu.SemaphoreType.DMA((2, 6)),
        ],
        places={0: pl.ANY, 1: pl.ANY, 2: pl.ANY},
        limit=58 * MIB,
    )(lat_labels, x_in[0].transpose(1, 2, 0, 3), out_grad[0].transpose(1, 2, 0, 3))
    lon = passed(lon, 0, -1)
    lat = passed(lat, -1, 0)
    cor = passed(cor, -1, -1)
    table = jnp.pad(bias_table[0, :, 253:506], ((0, 0), (0, 3)))
    bias = call(
        bias_kernel,
        struct((HEADS * LEVEL_ROWS, 128), F32),
        cost=HIDING,
    )(table)

    scratch = [
        pltpu.VMEM((ROWS, 3 * FEATURES), BF16),
        pltpu.VMEM(w_qkv.shape, BF16),
        pltpu.SemaphoreType.DMA,
    ]
    skip, inputs, fields, projected, att = call(
        first_kernel,
        (
            struct((ROWS, FEATURES), BF16),
            struct((PACKED_ROWS, FEATURES), BF16),
            struct((2, ROWS, FEATURES), BF16),
            struct((ROWS, 3 * FEATURES), BF16),
            struct((2, 4, 2, LEVEL_ROWS, LEVEL_ROWS), BF16),
        ),
        scratch[:2] + [pltpu.SemaphoreType.DMA((3,))],
        places={4: pl.ANY},
    )(own, lon, lat, cor, w_qkv, w_proj, norm_gain, bias)

    lat_index = lax.axis_index("lat").astype(jnp.int32).reshape(1)
    arrived = lax.ppermute(skip, "phase", [(1, 0)])
    next_inputs, far = passed(inputs, -2, 0), passed(inputs, -4, 0)
    blocks, kept, up = call(
        second_kernel,
        (struct((lats, 224, 128), BF16), part, part),
        scratch,
        places={5: pl.ANY},
        cost=HIDING,
    )(arrived, fields, projected, att, w_proj, w_qkv, norm_gain)
    blocks = lax.all_to_all(blocks, "lat", 0, 0, tiled=True)
    inputs, far, kept = lax.optimization_barrier((inputs, far, kept))
    last = passed(inputs, 2, 0)
    stack = call(
        stack_kernel, struct((2, PACKED_ROWS, FEATURES), BF16), places={2: pl.ANY}
    )(inputs, next_inputs, kept)
    other_stack, other_far, other_last = other_core(stack), other_core(far), other_core(last)
    above = passed(up, 1, 0)
    rows = FEATURES * 3 // 2 // lons
    slices = call(product_kernel, struct((lons, rows, 128), BF16), places={0: pltpu.SMEM})(
        lat_index, blocks, stack, other_stack, far, other_far, last, other_last
    )
    sideways = call(sideways_kernel, part, cost=HIDING)(kept, above)
    left = passed(sideways, 0, 1)
    grad_input = call(join_kernel, struct((1, 2, 6, 12, FEATURES), BF16))(kept, above, left)
    slices = lax.all_to_all(slices, "lon", 0, 0, tiled=True)
    grad_qkv = call(
        sum_kernel, struct((1, FEATURES // lons, 192), F32), places={0: pltpu.SMEM}
    )(lat_index, slices)
    return grad_input, grad_qkv.transpose(0, 2, 1)


def solution(mesh):
    in_specs = (
        P("phase", None, "lat", "lon", None),
        P("phase", None, "lat", "lon", None),
        P("phase", None, None),
        P("phase", None, None),
        P("phase", None),
        P("phase", None, None),
        P("lat"),
    )
    out_specs = (P("phase", None, "lat", "lon", None), P("phase", "lat", "lon"))
    return jax.shard_map(
        per_device, mesh=mesh, in_specs=in_specs, out_specs=out_specs, check_vma=False
    )
```

```python
import functools

import jax
import jax.numpy as jnp
from jax import lax
from jax.experimental import pallas as pl
from jax.experimental.pallas import tpu as pltpu
from jax.sharding import PartitionSpec as P

F32 = jnp.float32
BF16 = jnp.bfloat16
HEADS = 8
FEATURES = 512
EPSILON = 1e-05
MASKED = -1e30
SCORE_SCALE = 0.125
MIB = 1024 * 1024
HIDING = pl.CostEstimate(flops=4_000_000_000, bytes_accessed=20_000_000, transcendentals=0)

LEVEL_ROWS = 96
ROWS = 192
PACKED_ROWS = 144
GROUP = 8


def call(kernel, out_shape, scratch=(), places=(), out_places=(), cost=None, limit=50 * MIB):
    def run(*args):
        places_of = dict(places)
        specs = [
            pl.BlockSpec(memory_space=places_of.get(i, pltpu.VMEM)) for i in range(len(args))
        ]
        outs_of = dict(out_places)
        outs = [
            pl.BlockSpec(memory_space=outs_of.get(i, pltpu.VMEM))
            for i in range(len(jax.tree.leaves(out_shape)))
        ]
        outs = tuple(outs) if isinstance(out_shape, tuple) else outs[0]
        return pl.pallas_call(
            kernel,
            out_shape=out_shape,
            in_specs=specs,
            out_specs=outs,
            scratch_shapes=list(scratch),
            cost_estimate=cost,
            compiler_params=pltpu.CompilerParams(vmem_limit_bytes=limit),
        )(*args)

    return run


def struct(shape, dtype):
    return jax.ShapeDtypeStruct(shape, dtype)


def dot(left, right, dims=((1,), (0,))):
    return lax.dot_general(left, right, (dims, ((), ())), preferred_element_type=F32)


def row_index(shape, dim):
    return lax.broadcasted_iota(jnp.int32, shape, dim)


def pack(tiles):
    row = row_index(tiles[3].shape, 0)
    return [jnp.where(row < 6, tiles[g], pltpu.roll(tiles[3], 6 - 2 * g, 0)) for g in range(3)]


def unpack(rows):
    tiles = [rows[8 * g : 8 * g + 8] for g in range(3)]
    row = row_index(tiles[0].shape, 0)
    last = jnp.where(row < 2, pltpu.roll(tiles[0], 2, 0), 0.0)
    last = jnp.where((row >= 2) & (row < 4), pltpu.roll(tiles[1], 4, 0), last)
    last = jnp.where((row >= 4) & (row < 6), pltpu.roll(tiles[2], 6, 0), last)
    return [jnp.where(row < 6, tile, 0.0) for tile in tiles] + [last]


def cut_kernel(labels_ref, x_ref, g_ref, own, lon, lat, cor, labels, x_rows, g_rows, sem, sems):
    fetch = pltpu.make_async_copy(labels_ref, labels, sem)
    fetch.start()
    fetches = []
    for i in range(6):
        fetches.append(pltpu.make_async_copy(x_ref.at[i], x_rows.at[i], sems.at[0, i]))
        fetches.append(pltpu.make_async_copy(g_ref.at[i], g_rows.at[i], sems.at[1, i]))
    for copy in fetches:
        copy.start()
    row = row_index((8, FEATURES), 0)

    fetch.wait()
    parts = {}
    marks = [jnp.zeros((8, FEATURES), F32)] * 2
    for i in range(6):
        fetches[2 * i].wait()
        fetches[2 * i + 1].wait()
        fields = x_rows[i].astype(F32), g_rows[i].astype(F32)
        low = [field[0:8, level, :] for field in fields for level in range(2)]
        high = [pltpu.roll(field[4:12, level, :], 6, 0) for field in fields for level in range(2)]
        parts.setdefault((i // 3, 0), []).extend(pack(low))
        parts.setdefault((i // 3, 1), []).extend(pack(high))
        marks[i // 3] = jnp.where(row == i % 3, labels[i].astype(F32), marks[i // 3])
    cor[...] = jnp.concatenate(parts[0, 0] + [marks[0]], axis=0).astype(BF16)
    lat[...] = jnp.concatenate(parts[0, 1], axis=0).astype(BF16)
    lon[...] = jnp.concatenate(parts[1, 0], axis=0).astype(BF16)
    own[...] = jnp.concatenate(parts[1, 1] + [marks[1]], axis=0).astype(BF16)


def bias_kernel(table, out):
    parts = []
    for h in range(HEADS):
        line = jnp.broadcast_to(table[h : h + 1, :], (8, 256))
        parts.append(pltpu.roll(line, 0, 1, stride=1, stride_axis=0))
        parts.append(pltpu.roll(line, 6, 1, stride=1, stride_axis=0))
    shifted = jnp.concatenate(parts, axis=0)
    source = row_index((256, 256), 0)
    lane = row_index((256, 256), 1)
    column = lane & 7
    target = (lane >> 4) * 23 + ((lane >> 3) & 1) * 6 + column + 11
    picked = jnp.where((source == target) & (column < 6), 1.0, 0.0).astype(BF16)
    first = shifted.astype(BF16)
    rest = shifted - first.astype(F32)
    second = rest.astype(BF16)
    third = (rest - second.astype(F32)).astype(BF16)
    spread = dot(first, picked) + dot(second, picked) + dot(third, picked)
    empty = (row_index((128, 128), 0) & 7) >= 6
    for b in range(6):
        shift = (256 - (5 - b) * 16) % 256
        moved = spread if shift == 0 else pltpu.roll(spread, shift, 1)
        moved = jnp.where(empty, MASKED, moved[:, :128])
        for h in range(HEADS):
            out[h * 96 + b * 16 : h * 96 + b * 16 + 16, :] = moved[h * 16 : h * 16 + 16, :]


def pack_rows(array):
    columns = array.shape[1]
    groups = array.reshape(6, 4, 8, columns)
    row = row_index((8, columns), 0)
    out = []
    for q in range(6):
        last = groups[q, 3]
        for g in range(3):
            out.append(jnp.where(row < 6, groups[q, g], pltpu.roll(last, 6 - 2 * g, 0)))
    return jnp.concatenate(out, axis=0)


def per_head(pair, factor=1.0):
    even = (row_index(pair.shape, 1) < 64).astype(F32)
    return jnp.concatenate(
        [pair * (even * factor).astype(BF16), pair * ((1.0 - even) * factor).astype(BF16)], axis=0
    )


def attention_backward(att, d_low, projected, dqkv):
    lane = row_index((LEVEL_ROWS, 128), 1)
    units = [(level, pair) for level in range(2) for pair in range(4)]
    for first in range(0, len(units), GROUP):
        group = units[first : first + GROUP]
        places = [
            (slice(level * LEVEL_ROWS, (level + 1) * LEVEL_ROWS), slice(pair * 128, (pair + 1) * 128))
            for level, pair in group
        ]
        probs = att(group)
        d_probs = [
            dot(
                per_head(projected[rows, 1024 + cols.start : 1024 + cols.stop]),
                d_low[rows, cols],
                ((1,), (1,)),
            ).reshape(2, LEVEL_ROWS, LEVEL_ROWS)
            for rows, cols in places
        ]
        d_values = [
            dot(p.astype(BF16).reshape(2 * LEVEL_ROWS, LEVEL_ROWS), d_low[rows, cols])
            for p, (rows, cols) in zip(probs, places)
        ]
        inner = [jnp.sum(p * d, axis=1, keepdims=True) for p, d in zip(probs, d_probs)]
        d_scores = [
            (p * (d - i)).astype(BF16).reshape(2 * LEVEL_ROWS, LEVEL_ROWS)
            for p, d, i in zip(probs, d_probs, inner)
        ]
        d_keys = [dot(d, projected[rows, cols]) for d, (rows, cols) in zip(d_scores, places)]
        d_queries = [
            dot(
                d,
                per_head(projected[rows, 512 + cols.start : 512 + cols.stop], SCORE_SCALE),
                ((0,), (0,)),
            )
            for d, (rows, cols) in zip(d_scores, places)
        ]
        for (rows, cols), d_query, d_key, d_value in zip(places, d_queries, d_keys, d_values):
            dqkv[rows, cols] = d_query.astype(BF16)
            dqkv[rows, 512 + cols.start : 512 + cols.stop] = jnp.where(
                lane < 64, d_key[:LEVEL_ROWS], d_key[LEVEL_ROWS:]
            ).astype(BF16)
            dqkv[rows, 1024 + cols.start : 1024 + cols.stop] = jnp.where(
                lane < 64, d_value[:LEVEL_ROWS], d_value[LEVEL_ROWS:]
            ).astype(BF16)


def input_gradient(dqkv, w_qkv, gain, normed, inv_std):
    d_normed = dot(dqkv[...], w_qkv[...]) * gain[...]
    mean_plain = jnp.mean(d_normed, axis=-1, keepdims=True)
    mean_normed = jnp.mean(d_normed * normed, axis=-1, keepdims=True)
    return inv_std * (d_normed - mean_plain - normed * mean_normed)


def normalised(x):
    center = jnp.mean(x, axis=-1, keepdims=True)
    moved = x - center
    spread = jnp.mean(jnp.square(moved), axis=-1, keepdims=True)
    inv_std = lax.rsqrt(spread + EPSILON)
    return moved * inv_std, inv_std


def first_kernel(
    own, lon, lat, cor, w_qkv_ref, w_proj, gain, bias,
    skip, inputs, fields, projected_out, att_out,
    dqkv, w_qkv, sems,
):
    thirds = [slice(FEATURES * j, FEATURES * (j + 1)) for j in range(3)]
    fetches = [
        pltpu.make_async_copy(w_qkv_ref.at[third], w_qkv.at[third], sems.at[j])
        for j, third in enumerate(thirds)
    ]
    for copy in fetches:
        copy.start()
    labels = []
    tiles = {}
    for upper, (left, right) in enumerate(((own, lon), (lat, cor))):
        left, right = left[...].astype(F32), right[...].astype(F32)
        marked = right if upper else left
        labels.extend(marked[72 + i : 73 + i, :128] for i in range(3))
        for i in range(3):
            for half, piece in ((0, left), (1, right)):
                found = unpack(piece[24 * i : 24 * i + 24])
                for k in range(4):
                    tiles[k // 2, k % 2, 3 * upper + i, half] = found[k]
    order = [(level, i, half) for level in range(2) for i in range(6) for half in range(2)]
    tiles_x, tiles_g = ([tiles[(field,) + place] for place in order] for field in range(2))
    x = jnp.concatenate(tiles_x, axis=0)
    c = jnp.concatenate(tiles_g, axis=0)
    normed, inv_std = normalised(x)
    scaled = normed * gain[...]
    inputs[...] = pack_rows(scaled).astype(BF16)
    c_low = c.astype(BF16)
    d_low = dot(c_low, w_proj[...]).astype(BF16)
    fields[0] = x.astype(BF16)
    fields[1] = c_low
    scaled_low = scaled.astype(BF16)
    for copy, third in zip(fetches, thirds):
        copy.wait()
        projected = dot(scaled_low, w_qkv[third, :], ((1,), (1,)))
        projected_out[:, third] = (projected * (SCORE_SCALE if third.start == 0 else 1.0)).astype(BF16)

    lane_row = row_index((1, 128), 1) >> 4
    along = labels[0]
    for b in range(1, 6):
        along = jnp.where(lane_row == b, labels[b], along)
    allowed = jnp.concatenate(
        [
            jnp.broadcast_to(jnp.where(labels[b] == along, 0.0, MASKED), (16, 128))
            for b in range(6)
        ],
        axis=0,
    )

    def probabilities(group):
        scores = []
        for level, pair in group:
            rows = slice(level * LEVEL_ROWS, (level + 1) * LEVEL_ROWS)
            cols = slice(pair * 128, (pair + 1) * 128)
            keys = per_head(projected_out[rows, 512 + cols.start : 512 + cols.stop])
            score = dot(keys, projected_out[rows, cols], ((1,), (1,)))
            scores.append(score.reshape(2, LEVEL_ROWS, LEVEL_ROWS))
        probs = []
        for (level, pair), score in zip(group, scores):
            added = bias[pair * 192 : (pair + 1) * 192, :].reshape(2, LEVEL_ROWS, 128) + allowed[None]
            score = score + added[:, :, :LEVEL_ROWS]
            weights = jnp.exp(score - jnp.max(score, axis=1, keepdims=True))
            probs.append(weights * (1.0 / jnp.sum(weights, axis=1, keepdims=True)))
        for (level, pair), prob in zip(group, probs):
            att_out[level, pair] = prob.astype(BF16)
        return probs

    attention_backward(probabilities, d_low, projected_out, dqkv)
    skip[...] = (c + input_gradient(dqkv, w_qkv, gain, normed, inv_std)).astype(BF16)


def second_kernel(
    arrived, fields, projected, att, w_proj, w_qkv_ref, gain,
    blocks, kept, up, dqkv, w_qkv, sem,
):
    fetch = pltpu.make_async_copy(w_qkv_ref, w_qkv, sem)
    fetch.start()
    d_low = (dot(fields[1], w_proj[...]) + dot(arrived[...], w_proj[...])).astype(BF16)
    attention_backward(
        lambda group: [att[level, pair].astype(F32) for level, pair in group], d_low, projected, dqkv
    )
    lane = row_index((80, 128), 1)
    for t in range(4):
        whole = [
            pack_rows(dqkv[:, 384 * t + 128 * j : 384 * t + 128 * (j + 1)].astype(F32))
            for j in range(3)
        ]
        blocks[2 * t, :144, :] = whole[0].astype(BF16)
        blocks[2 * t + 1, :144, :] = whole[2].astype(BF16)
        top = whole[1][:80]
        bottom = jnp.concatenate([whole[1][80:], jnp.zeros((16, 128), F32)], axis=0)
        blocks[2 * t, 144:, :] = jnp.where(lane < 64, top, pltpu.roll(bottom, 64, 1)).astype(BF16)
        blocks[2 * t + 1, 144:, :] = jnp.where(lane < 64, pltpu.roll(top, 64, 1), bottom).astype(
            BF16
        )
    normed, inv_std = normalised(fields[0].astype(F32))
    fetch.wait()
    shifted = input_gradient(dqkv, w_qkv, gain, normed, inv_std)
    total = fields[1].astype(F32) + (arrived[...].astype(F32) + shifted)
    for target, first in ((kept, 0), (up, 3)):
        parts = []
        for i in range(first, first + 3):
            starts = [96 * level + 16 * i + 8 * half for half in range(2) for level in range(2)]
            parts.extend(pack([total[start : start + 8] for start in starts]))
        target[...] = jnp.concatenate(parts, axis=0).astype(BF16)


def stack_kernel(a, b, c, d, kept, low, high):
    low[0], low[1], high[0], high[1] = a[...], b[...], c[...], d[...]


def product_kernel(
    lat_index, blocks, low, high, other_low, other_high, out
):
    lats = blocks.shape[0]

    def columns(place):
        folded = blocks[place, 144:, :]
        bottom = pltpu.roll(folded[:64].astype(F32), 64, 1).astype(BF16)
        return jnp.concatenate(
            [blocks[place, :144, :], jnp.concatenate([folded, bottom], axis=0)], axis=1
        )

    gradients, cells = [], []
    for x in range(0, lats // 2, 2):
        places = []
        for step in (x, x + 1):
            first = jnp.bitwise_xor(lat_index[0], 2 * step)
            places.append((first, jnp.bitwise_xor(first, 1)))
        for same, source in enumerate((low, other_low) if x == 0 else (high, other_high)):
            gradients.extend(columns(place[same]) for place in places)
            cells.append(source[...].reshape(2 * PACKED_ROWS, FEATURES))
    product = dot(
        jnp.concatenate(cells, axis=0), jnp.concatenate(gradients, axis=0), ((0,), (0,))
    )
    bands = out.shape[0]
    width = FEATURES // bands
    whole = product[:, :128].reshape(bands, width, 128)
    half = product[:, 128:].reshape(bands, width, 128)
    lane = row_index((bands, width // 2, 128), 2)
    out[:, :width, :] = whole.astype(BF16)
    folded = jnp.where(lane < 64, half[:, : width // 2], pltpu.roll(half[:, width // 2 :], 64, 2))
    out[:, width:, :] = folded.astype(BF16)


def sideways_kernel(kept, above, sideways):
    tiles = []
    for part in (above, kept):
        part = part[...].astype(F32)
        for i in range(3):
            tiles.extend(unpack(part[24 * i : 24 * i + 24])[2:])
    packed = pack(tiles[:4]) + pack(tiles[4:8]) + pack(tiles[8:])
    sideways[...] = jnp.concatenate(packed, axis=0).astype(BF16)


def sum_kernel(lat_index, parts, out):
    bands, rows, _ = parts.shape
    width = rows * 2 // 3
    total = parts[0].astype(F32)
    for band in range(1, bands):
        total = total + parts[band].astype(F32)
    whole = total[:width]
    folded = total[width:]
    half = jnp.concatenate([folded, pltpu.roll(folded, 64, 1)], axis=0)
    half = half[:, :64]

    @pl.when(lax.rem(lat_index[0], 2) == 0)
    def _():
        out[0, :, :128] = whole
        out[0, :, 128:] = half

    @pl.when(lax.rem(lat_index[0], 2) == 1)
    def _():
        out[0, :, :64] = half
        out[0, :, 64:] = whole


def join_kernel(kept, above, left, out):
    row = row_index((8, FEATURES), 0)
    low, high = [], []
    side = left[...].astype(F32)
    for g in range(3):
        low.extend(unpack(side[24 * g : 24 * g + 24]))
    for part in (above, kept):
        part = part[...].astype(F32)
        for i in range(3):
            high.extend(unpack(part[24 * i : 24 * i + 24])[:2])
    for i in range(6):
        for level in range(2):
            moved = pltpu.roll(high[2 * i + level], 6, 0)
            out[0, level, i, 0:8, :] = jnp.where(row < 6, low[2 * i + level], moved).astype(BF16)
            out[0, level, i, 8:12, :] = moved[:4].astype(BF16)


def passed(array, lat_by, lon_by):
    lats, lons = lax.axis_size("lat"), lax.axis_size("lon")
    pairs = [
        (a * lons + o, ((a + lat_by) % lats) * lons + (o + lon_by) % lons)
        for a in range(lats)
        for o in range(lons)
    ]
    return lax.ppermute(array, ("lat", "lon"), pairs)


def swapped(array, bits):
    return lax.ppermute(array, "lat", [(a, a ^ bits) for a in range(lax.axis_size("lat"))])


def per_device(x_in, out_grad, w_qkv, w_proj, norm_gain, bias_table, lat_labels):
    lats, lons = lax.axis_size("lat"), lax.axis_size("lon")
    w_qkv, w_proj = w_qkv[0], w_proj[0]
    part = struct((72, FEATURES), BF16)
    marked = struct((80, FEATURES), BF16)
    own, lon, lat, cor = call(
        cut_kernel,
        (marked, part, part, marked),
        [
            pltpu.SMEM(lat_labels.shape, jnp.int32),
            pltpu.VMEM((6, 12, 2, FEATURES), BF16),
            pltpu.VMEM((6, 12, 2, FEATURES), BF16),
            pltpu.SemaphoreType.DMA,
            pltpu.SemaphoreType.DMA((2, 6)),
        ],
        places={0: pl.ANY, 1: pl.ANY, 2: pl.ANY},
        limit=58 * MIB,
    )(lat_labels, x_in[0].transpose(1, 2, 0, 3), out_grad[0].transpose(1, 2, 0, 3))
    lon = passed(lon, 0, -1)
    lat = passed(lat, -1, 0)
    cor = passed(cor, -1, -1)
    table = jnp.pad(bias_table[0, :, 253:506], ((0, 0), (0, 3)))
    bias = call(
        bias_kernel,
        struct((HEADS * LEVEL_ROWS, 128), F32),
        cost=HIDING,
    )(table)

    scratch = [
        pltpu.VMEM((ROWS, 3 * FEATURES), BF16),
        pltpu.VMEM(w_qkv.shape, BF16),
        pltpu.SemaphoreType.DMA,
    ]
    skip, inputs, fields, projected, att = call(
        first_kernel,
        (
            struct((ROWS, FEATURES), BF16),
            struct((PACKED_ROWS, FEATURES), BF16),
            struct((2, ROWS, FEATURES), BF16),
            struct((ROWS, 3 * FEATURES), BF16),
            struct((2, 4, 2, LEVEL_ROWS, LEVEL_ROWS), BF16),
        ),
        scratch[:2] + [pltpu.SemaphoreType.DMA((3,))],
        places={4: pl.ANY},
    )(own, lon, lat, cor, w_qkv, w_proj, norm_gain, bias)

    lat_index = lax.axis_index("lat").astype(jnp.int32).reshape(1)
    arrived = lax.ppermute(skip, "phase", [(1, 0)])
    along = [inputs] + [swapped(inputs, 2 * x) for x in range(1, lats // 2)]
    blocks, kept, up = call(
        second_kernel,
        (struct((lats, 224, 128), BF16), part, part),
        scratch,
        places={5: pl.ANY},
        cost=HIDING,
    )(arrived, fields, projected, att, w_proj, w_qkv, norm_gain)
    blocks = lax.all_to_all(blocks, "lat", 0, 0, tiled=True)
    two = struct((2, PACKED_ROWS, FEATURES), BF16)
    low, high = call(stack_kernel, (two, two), places={4: pl.ANY})(*along, kept)
    other_low, other_high = swapped(low, 1), swapped(high, 1)
    above = passed(up, 1, 0)
    rows = FEATURES * 3 // 2 // lons
    slices = call(product_kernel, struct((lons, rows, 128), BF16), places={0: pltpu.SMEM})(
        lat_index, blocks, low, high, other_low, other_high
    )
    sideways = call(sideways_kernel, part, cost=HIDING)(kept, above)
    left = passed(sideways, 0, 1)
    grad_input = call(join_kernel, struct((1, 2, 6, 12, FEATURES), BF16))(kept, above, left)
    slices = lax.all_to_all(slices, "lon", 0, 0, tiled=True)
    grad_qkv = call(
        sum_kernel, struct((1, FEATURES // lons, 192), F32), places={0: pltpu.SMEM}
    )(lat_index, slices)
    return grad_input, grad_qkv.transpose(0, 2, 1)


def solution(mesh):
    in_specs = (
        P("phase", None, "lat", "lon", None),
        P("phase", None, "lat", "lon", None),
        P("phase", None, None),
        P("phase", None, None),
        P("phase", None),
        P("phase", None, None),
        P("lat"),
    )
    out_specs = (P("phase", None, "lat", "lon", None), P("phase", "lat", "lon"))
    return jax.shard_map(
        per_device, mesh=mesh, in_specs=in_specs, out_specs=out_specs, check_vma=False
    )
```

```python
import functools

import jax
import jax.numpy as jnp
from jax import lax
from jax.experimental import pallas as pl
from jax.experimental.pallas import tpu as pltpu
from jax.sharding import PartitionSpec as P

F32 = jnp.float32
BF16 = jnp.bfloat16
HEADS = 8
FEATURES = 512
EPSILON = 1e-05
MASKED = -1e30
SCORE_SCALE = 0.125
MIB = 1024 * 1024
HIDING = pl.CostEstimate(flops=4_000_000_000, bytes_accessed=20_000_000, transcendentals=0)

LEVEL_ROWS = 96
ROWS = 192
PACKED_ROWS = 144
GROUP = 8


def call(kernel, out_shape, scratch=(), places=(), out_places=(), cost=None, limit=50 * MIB):
    def run(*args):
        places_of = dict(places)
        specs = [
            pl.BlockSpec(memory_space=places_of.get(i, pltpu.VMEM)) for i in range(len(args))
        ]
        outs_of = dict(out_places)
        outs = [
            pl.BlockSpec(memory_space=outs_of.get(i, pltpu.VMEM))
            for i in range(len(jax.tree.leaves(out_shape)))
        ]
        outs = tuple(outs) if isinstance(out_shape, tuple) else outs[0]
        return pl.pallas_call(
            kernel,
            out_shape=out_shape,
            in_specs=specs,
            out_specs=outs,
            scratch_shapes=list(scratch),
            cost_estimate=cost,
            compiler_params=pltpu.CompilerParams(vmem_limit_bytes=limit),
        )(*args)

    return run


def struct(shape, dtype):
    return jax.ShapeDtypeStruct(shape, dtype)


def dot(left, right, dims=((1,), (0,))):
    return lax.dot_general(left, right, (dims, ((), ())), preferred_element_type=F32)


def row_index(shape, dim):
    return lax.broadcasted_iota(jnp.int32, shape, dim)


def pack(tiles):
    row = row_index(tiles[3].shape, 0)
    return [jnp.where(row < 6, tiles[g], pltpu.roll(tiles[3], 6 - 2 * g, 0)) for g in range(3)]


def unpack(rows):
    tiles = [rows[8 * g : 8 * g + 8] for g in range(3)]
    row = row_index(tiles[0].shape, 0)
    last = jnp.where(row < 2, pltpu.roll(tiles[0], 2, 0), 0.0)
    last = jnp.where((row >= 2) & (row < 4), pltpu.roll(tiles[1], 4, 0), last)
    last = jnp.where((row >= 4) & (row < 6), pltpu.roll(tiles[2], 6, 0), last)
    return [jnp.where(row < 6, tile, 0.0) for tile in tiles] + [last]


def cut_kernel(labels_ref, x_ref, g_ref, own, lon, lat, cor, labels, x_rows, g_rows, sem, sems):
    fetch = pltpu.make_async_copy(labels_ref, labels, sem)
    fetch.start()
    fetches = []
    halves = [pl.ds(3, 3), pl.ds(0, 3)]
    for j, rows in enumerate(halves):
        fetches.append(pltpu.make_async_copy(x_ref.at[rows], x_rows.at[rows], sems.at[0, j]))
        fetches.append(pltpu.make_async_copy(g_ref.at[rows], g_rows.at[rows], sems.at[1, j]))
    for copy in fetches:
        copy.start()
    row = row_index((8, FEATURES), 0)

    fetch.wait()
    parts = {}
    marks = [jnp.zeros((8, FEATURES), F32)] * 2
    for i in (3, 4, 5, 0, 1, 2):
        if i % 3 == 0:
            fetches[2 * (i == 0)].wait()
            fetches[2 * (i == 0) + 1].wait()
        fields = x_rows[i].astype(F32), g_rows[i].astype(F32)
        low = [field[0:8, level, :] for field in fields for level in range(2)]
        high = [pltpu.roll(field[4:12, level, :], 6, 0) for field in fields for level in range(2)]
        parts.setdefault((i // 3, 0), []).extend(pack(low))
        parts.setdefault((i // 3, 1), []).extend(pack(high))
        marks[i // 3] = jnp.where(row == i % 3, labels[i].astype(F32), marks[i // 3])
    cor[...] = jnp.concatenate(parts[0, 0] + [marks[0]], axis=0).astype(BF16)
    lat[...] = jnp.concatenate(parts[0, 1], axis=0).astype(BF16)
    lon[...] = jnp.concatenate(parts[1, 0], axis=0).astype(BF16)
    own[...] = jnp.concatenate(parts[1, 1] + [marks[1]], axis=0).astype(BF16)


def bias_kernel(table, out):
    parts = []
    for h in range(HEADS):
        line = jnp.broadcast_to(table[h : h + 1, :], (8, 256))
        parts.append(pltpu.roll(line, 0, 1, stride=1, stride_axis=0))
        parts.append(pltpu.roll(line, 6, 1, stride=1, stride_axis=0))
    shifted = jnp.concatenate(parts, axis=0)
    source = row_index((256, 256), 0)
    lane = row_index((256, 256), 1)
    column = lane & 7
    target = (lane >> 4) * 23 + ((lane >> 3) & 1) * 6 + column + 11
    picked = jnp.where((source == target) & (column < 6), 1.0, 0.0).astype(BF16)
    first = shifted.astype(BF16)
    rest = shifted - first.astype(F32)
    second = rest.astype(BF16)
    third = (rest - second.astype(F32)).astype(BF16)
    spread = dot(first, picked) + dot(second, picked) + dot(third, picked)
    empty = (row_index((128, 128), 0) & 7) >= 6
    for b in range(6):
        shift = (256 - (5 - b) * 16) % 256
        moved = spread if shift == 0 else pltpu.roll(spread, shift, 1)
        moved = jnp.where(empty, MASKED, moved[:, :128])
        for h in range(HEADS):
            out[h * 96 + b * 16 : h * 96 + b * 16 + 16, :] = moved[h * 16 : h * 16 + 16, :]


def pack_rows(array):
    columns = array.shape[1]
    groups = array.reshape(6, 4, 8, columns)
    row = row_index((8, columns), 0)
    out = []
    for q in range(6):
        last = groups[q, 3]
        for g in range(3):
            out.append(jnp.where(row < 6, groups[q, g], pltpu.roll(last, 6 - 2 * g, 0)))
    return jnp.concatenate(out, axis=0)


def per_head(pair, factor=1.0):
    even = (row_index(pair.shape, 1) < 64).astype(F32)
    return jnp.concatenate(
        [pair * (even * factor).astype(BF16), pair * ((1.0 - even) * factor).astype(BF16)], axis=0
    )


def attention_backward(att, d_low, projected, dqkv):
    lane = row_index((LEVEL_ROWS, 128), 1)
    units = [(level, pair) for level in range(2) for pair in range(4)]
    for first in range(0, len(units), GROUP):
        group = units[first : first + GROUP]
        places = [
            (slice(level * LEVEL_ROWS, (level + 1) * LEVEL_ROWS), slice(pair * 128, (pair + 1) * 128))
            for level, pair in group
        ]
        probs = att(group)
        d_probs = [
            dot(
                per_head(projected[rows, 1024 + cols.start : 1024 + cols.stop]),
                d_low[rows, cols],
                ((1,), (1,)),
            ).reshape(2, LEVEL_ROWS, LEVEL_ROWS)
            for rows, cols in places
        ]
        d_values = [
            dot(p.astype(BF16).reshape(2 * LEVEL_ROWS, LEVEL_ROWS), d_low[rows, cols])
            for p, (rows, cols) in zip(probs, places)
        ]
        inner = [jnp.sum(p * d, axis=1, keepdims=True) for p, d in zip(probs, d_probs)]
        d_scores = [
            (p * (d - i)).astype(BF16).reshape(2 * LEVEL_ROWS, LEVEL_ROWS)
            for p, d, i in zip(probs, d_probs, inner)
        ]
        d_keys = [dot(d, projected[rows, cols]) for d, (rows, cols) in zip(d_scores, places)]
        d_queries = [
            dot(
                d,
                per_head(projected[rows, 512 + cols.start : 512 + cols.stop], SCORE_SCALE),
                ((0,), (0,)),
            )
            for d, (rows, cols) in zip(d_scores, places)
        ]
        for (rows, cols), d_query, d_key, d_value in zip(places, d_queries, d_keys, d_values):
            dqkv[rows, cols] = d_query.astype(BF16)
            dqkv[rows, 512 + cols.start : 512 + cols.stop] = jnp.where(
                lane < 64, d_key[:LEVEL_ROWS], d_key[LEVEL_ROWS:]
            ).astype(BF16)
            dqkv[rows, 1024 + cols.start : 1024 + cols.stop] = jnp.where(
                lane < 64, d_value[:LEVEL_ROWS], d_value[LEVEL_ROWS:]
            ).astype(BF16)


def input_gradient(dqkv, w_qkv, gain, normed, inv_std):
    d_normed = dot(dqkv[...], w_qkv[...]) * gain[...]
    mean_plain = jnp.mean(d_normed, axis=-1, keepdims=True)
    mean_normed = jnp.mean(d_normed * normed, axis=-1, keepdims=True)
    return inv_std * (d_normed - mean_plain - normed * mean_normed)


def normalised(x):
    center = jnp.mean(x, axis=-1, keepdims=True)
    moved = x - center
    spread = jnp.mean(jnp.square(moved), axis=-1, keepdims=True)
    inv_std = lax.rsqrt(spread + EPSILON)
    return moved * inv_std, inv_std


def first_kernel(
    own, lon, lat, cor, w_qkv_ref, w_proj, gain, bias,
    skip, inputs, fields, projected_out, att_out,
    dqkv, w_qkv, sems,
):
    thirds = [slice(FEATURES * j, FEATURES * (j + 1)) for j in range(3)]
    fetches = [
        pltpu.make_async_copy(w_qkv_ref.at[third], w_qkv.at[third], sems.at[j])
        for j, third in enumerate(thirds)
    ]
    for copy in fetches:
        copy.start()
    labels = []
    tiles = {}
    for upper, (left, right) in enumerate(((own, lon), (lat, cor))):
        left, right = left[...].astype(F32), right[...].astype(F32)
        marked = right if upper else left
        labels.extend(marked[72 + i : 73 + i, :128] for i in range(3))
        for i in range(3):
            for half, piece in ((0, left), (1, right)):
                found = unpack(piece[24 * i : 24 * i + 24])
                for k in range(4):
                    tiles[k // 2, k % 2, 3 * upper + i, half] = found[k]
    order = [(level, i, half) for level in range(2) for i in range(6) for half in range(2)]
    tiles_x, tiles_g = ([tiles[(field,) + place] for place in order] for field in range(2))
    x = jnp.concatenate(tiles_x, axis=0)
    c = jnp.concatenate(tiles_g, axis=0)
    normed, inv_std = normalised(x)
    scaled = normed * gain[...]
    inputs[...] = pack_rows(scaled).astype(BF16)
    c_low = c.astype(BF16)
    d_low = dot(c_low, w_proj[...]).astype(BF16)
    fields[0] = x.astype(BF16)
    fields[1] = c_low
    scaled_low = scaled.astype(BF16)
    for copy, third in zip(fetches, thirds):
        copy.wait()
        projected = dot(scaled_low, w_qkv[third, :], ((1,), (1,)))
        projected_out[:, third] = (projected * (SCORE_SCALE if third.start == 0 else 1.0)).astype(BF16)

    lane_row = row_index((1, 128), 1) >> 4
    along = labels[0]
    for b in range(1, 6):
        along = jnp.where(lane_row == b, labels[b], along)
    allowed = jnp.concatenate(
        [
            jnp.broadcast_to(jnp.where(labels[b] == along, 0.0, MASKED), (16, 128))
            for b in range(6)
        ],
        axis=0,
    )

    def probabilities(group):
        scores = []
        for level, pair in group:
            rows = slice(level * LEVEL_ROWS, (level + 1) * LEVEL_ROWS)
            cols = slice(pair * 128, (pair + 1) * 128)
            keys = per_head(projected_out[rows, 512 + cols.start : 512 + cols.stop])
            score = dot(keys, projected_out[rows, cols], ((1,), (1,)))
            scores.append(score.reshape(2, LEVEL_ROWS, LEVEL_ROWS))
        probs = []
        for (level, pair), score in zip(group, scores):
            added = bias[pair * 192 : (pair + 1) * 192, :].reshape(2, LEVEL_ROWS, 128) + allowed[None]
            score = score + added[:, :, :LEVEL_ROWS]
            weights = jnp.exp(score - jnp.max(score, axis=1, keepdims=True))
            probs.append(weights * (1.0 / jnp.sum(weights, axis=1, keepdims=True)))
        for (level, pair), prob in zip(group, probs):
            att_out[level, pair] = prob.astype(BF16)
        return probs

    attention_backward(probabilities, d_low, projected_out, dqkv)
    skip[...] = (c + input_gradient(dqkv, w_qkv, gain, normed, inv_std)).astype(BF16)


def second_kernel(
    arrived, fields, projected, att, w_proj, w_qkv_ref, gain,
    blocks, kept, up, dqkv, w_qkv, sem,
):
    fetch = pltpu.make_async_copy(w_qkv_ref, w_qkv, sem)
    fetch.start()
    d_low = (dot(fields[1], w_proj[...]) + dot(arrived[...], w_proj[...])).astype(BF16)
    attention_backward(
        lambda group: [att[level, pair].astype(F32) for level, pair in group], d_low, projected, dqkv
    )
    lane = row_index((80, 128), 1)
    for t in range(4):
        whole = [
            pack_rows(dqkv[:, 384 * t + 128 * j : 384 * t + 128 * (j + 1)].astype(F32))
            for j in range(3)
        ]
        blocks[2 * t, :144, :] = whole[0].astype(BF16)
        blocks[2 * t + 1, :144, :] = whole[2].astype(BF16)
        top = whole[1][:80]
        bottom = jnp.concatenate([whole[1][80:], jnp.zeros((16, 128), F32)], axis=0)
        blocks[2 * t, 144:, :] = jnp.where(lane < 64, top, pltpu.roll(bottom, 64, 1)).astype(BF16)
        blocks[2 * t + 1, 144:, :] = jnp.where(lane < 64, pltpu.roll(top, 64, 1), bottom).astype(
            BF16
        )
    normed, inv_std = normalised(fields[0].astype(F32))
    fetch.wait()
    shifted = input_gradient(dqkv, w_qkv, gain, normed, inv_std)
    total = fields[1].astype(F32) + (arrived[...].astype(F32) + shifted)
    for target, first in ((kept, 0), (up, 3)):
        parts = []
        for i in range(first, first + 3):
            starts = [96 * level + 16 * i + 8 * half for half in range(2) for level in range(2)]
            parts.extend(pack([total[start : start + 8] for start in starts]))
        target[...] = jnp.concatenate(parts, axis=0).astype(BF16)


def stack_kernel(a, b, c, d, kept, low, high):
    low[0], low[1], high[0], high[1] = a[...], b[...], c[...], d[...]


def product_kernel(
    lat_index, blocks, low, high, other_low, other_high, out
):
    lats = blocks.shape[0]

    def columns(place):
        folded = blocks[place, 144:, :]
        bottom = pltpu.roll(folded[:64].astype(F32), 64, 1).astype(BF16)
        return jnp.concatenate(
            [blocks[place, :144, :], jnp.concatenate([folded, bottom], axis=0)], axis=1
        )

    gradients, cells = [], []
    for x in range(0, lats // 2, 2):
        places = []
        for step in (x, x + 1):
            first = lat_index[0] + 2 * step
            first = jnp.where(first >= lats, first - lats, first)
            places.append((first, first + 1 - 2 * lax.rem(lat_index[0], 2)))
        for same, source in enumerate((low, other_low) if x == 0 else (high, other_high)):
            gradients.extend(columns(place[same]) for place in places)
            cells.append(source[...].reshape(2 * PACKED_ROWS, FEATURES))
    product = dot(
        jnp.concatenate(cells, axis=0), jnp.concatenate(gradients, axis=0), ((0,), (0,))
    )
    bands = out.shape[0]
    width = FEATURES // bands
    whole = product[:, :128].reshape(bands, width, 128)
    half = product[:, 128:].reshape(bands, width, 128)
    lane = row_index((bands, width // 2, 128), 2)
    out[:, :width, :] = whole.astype(BF16)
    folded = jnp.where(lane < 64, half[:, : width // 2], pltpu.roll(half[:, width // 2 :], 64, 2))
    out[:, width:, :] = folded.astype(BF16)


def sideways_kernel(kept, above, sideways):
    tiles = []
    for part in (above, kept):
        part = part[...].astype(F32)
        for i in range(3):
            tiles.extend(unpack(part[24 * i : 24 * i + 24])[2:])
    packed = pack(tiles[:4]) + pack(tiles[4:8]) + pack(tiles[8:])
    sideways[...] = jnp.concatenate(packed, axis=0).astype(BF16)


def sum_kernel(lat_index, parts, out):
    bands, rows, _ = parts.shape
    width = rows * 2 // 3
    total = parts[0].astype(F32)
    for band in range(1, bands):
        total = total + parts[band].astype(F32)
    whole = total[:width]
    folded = total[width:]
    half = jnp.concatenate([folded, pltpu.roll(folded, 64, 1)], axis=0)
    half = half[:, :64]

    @pl.when(lax.rem(lat_index[0], 2) == 0)
    def _():
        out[0, :, :128] = whole
        out[0, :, 128:] = half

    @pl.when(lax.rem(lat_index[0], 2) == 1)
    def _():
        out[0, :, :64] = half
        out[0, :, 64:] = whole


def join_kernel(kept, above, left, out):
    row = row_index((8, FEATURES), 0)
    low, high = [], []
    side = left[...].astype(F32)
    for g in range(3):
        low.extend(unpack(side[24 * g : 24 * g + 24]))
    for part in (above, kept):
        part = part[...].astype(F32)
        for i in range(3):
            high.extend(unpack(part[24 * i : 24 * i + 24])[:2])
    for i in range(6):
        for level in range(2):
            moved = pltpu.roll(high[2 * i + level], 6, 0)
            out[0, level, i, 0:8, :] = jnp.where(row < 6, low[2 * i + level], moved).astype(BF16)
            out[0, level, i, 8:12, :] = moved[:4].astype(BF16)


def passed(array, lat_by, lon_by):
    lats, lons = lax.axis_size("lat"), lax.axis_size("lon")
    pairs = [
        (a * lons + o, ((a + lat_by) % lats) * lons + (o + lon_by) % lons)
        for a in range(lats)
        for o in range(lons)
    ]
    return lax.ppermute(array, ("lat", "lon"), pairs)


def other_core(array):
    return lax.ppermute(array, "lat", [(a, a ^ 1) for a in range(lax.axis_size("lat"))])


def per_device(x_in, out_grad, w_qkv, w_proj, norm_gain, bias_table, lat_labels):
    lats, lons = lax.axis_size("lat"), lax.axis_size("lon")
    w_qkv, w_proj = w_qkv[0], w_proj[0]
    part = struct((72, FEATURES), BF16)
    marked = struct((80, FEATURES), BF16)
    own, lon, lat, cor = call(
        cut_kernel,
        (marked, part, part, marked),
        [
            pltpu.SMEM(lat_labels.shape, jnp.int32),
            pltpu.VMEM((6, 12, 2, FEATURES), BF16),
            pltpu.VMEM((6, 12, 2, FEATURES), BF16),
            pltpu.SemaphoreType.DMA,
            pltpu.SemaphoreType.DMA((2, 2)),
        ],
        places={0: pl.ANY, 1: pl.ANY, 2: pl.ANY},
        limit=58 * MIB,
    )(lat_labels, x_in[0].transpose(1, 2, 0, 3), out_grad[0].transpose(1, 2, 0, 3))
    lon = passed(lon, 0, -1)
    lat = passed(lat, -1, 0)
    cor = passed(cor, -1, -1)
    table = jnp.pad(bias_table[0, :, 253:506], ((0, 0), (0, 3)))
    bias = call(
        bias_kernel,
        struct((HEADS * LEVEL_ROWS, 128), F32),
        cost=HIDING,
    )(table)

    scratch = [
        pltpu.VMEM((ROWS, 3 * FEATURES), BF16),
        pltpu.VMEM(w_qkv.shape, BF16),
        pltpu.SemaphoreType.DMA,
    ]
    skip, inputs, fields, projected, att = call(
        first_kernel,
        (
            struct((ROWS, FEATURES), BF16),
            struct((PACKED_ROWS, FEATURES), BF16),
            struct((2, ROWS, FEATURES), BF16),
            struct((ROWS, 3 * FEATURES), BF16),
            struct((2, 4, 2, LEVEL_ROWS, LEVEL_ROWS), BF16),
        ),
        scratch[:2] + [pltpu.SemaphoreType.DMA((3,))],
        places={4: pl.ANY},
    )(own, lon, lat, cor, w_qkv, w_proj, norm_gain, bias)

    lat_index = lax.axis_index("lat").astype(jnp.int32).reshape(1)
    arrived = lax.ppermute(skip, "phase", [(1, 0)])
    along = [inputs] + [passed(inputs, -2 * x, 0) for x in range(1, lats // 2)]
    blocks, kept, up = call(
        second_kernel,
        (struct((lats, 224, 128), BF16), part, part),
        scratch,
        places={5: pl.ANY},
        cost=HIDING,
    )(arrived, fields, projected, att, w_proj, w_qkv, norm_gain)
    blocks = lax.all_to_all(blocks, "lat", 0, 0, tiled=True)
    two = struct((2, PACKED_ROWS, FEATURES), BF16)
    low, high = call(stack_kernel, (two, two), places={4: pl.ANY})(*along, kept)
    other_low, other_high = other_core(low), other_core(high)
    above = passed(up, 1, 0)
    rows = FEATURES * 3 // 2 // lons
    slices = call(product_kernel, struct((lons, rows, 128), BF16), places={0: pltpu.SMEM})(
        lat_index, blocks, low, high, other_low, other_high
    )
    sideways = call(sideways_kernel, part, cost=HIDING)(kept, above)
    left = passed(sideways, 0, 1)
    grad_input = call(join_kernel, struct((1, 2, 6, 12, FEATURES), BF16))(kept, above, left)
    slices = lax.all_to_all(slices, "lon", 0, 0, tiled=True)
    grad_qkv = call(
        sum_kernel, struct((1, FEATURES // lons, 192), F32), places={0: pltpu.SMEM}
    )(lat_index, slices)
    return grad_input, grad_qkv.transpose(0, 2, 1)


def solution(mesh):
    in_specs = (
        P("phase", None, "lat", "lon", None),
        P("phase", None, "lat", "lon", None),
        P("phase", None, None),
        P("phase", None, None),
        P("phase", None),
        P("phase", None, None),
        P("lat"),
    )
    out_specs = (P("phase", None, "lat", "lon", None), P("phase", "lat", "lon"))
    return jax.shard_map(
        per_device, mesh=mesh, in_specs=in_specs, out_specs=out_specs, check_vma=False
    )
```
